128 devices in a mesh: lat: 16 (over y, z_hi, core), lev: 8 (over x, z_lo).
Axes of the slice: x: 4, y: 4, z: 4 (z_hi: 2, z_lo: 2; z = z_hi * 2 + z_lo), core: 2. Of those that a mesh axis runs over, the one named last changes fastest.
Arguments:
- tracers: float32 [4, 72, 64, 1440], P(None, 'lev', 'lat'), may hold values from -6 to 6
- zonal: float32 [72, 64, 1440], P('lev', 'lat'), may hold values from -0.6 to 0.6
- meridional: float32 [72, 64, 1440], P('lev', 'lat'), may hold values from -0.5 to 0.5
- vertical: float32 [72, 64, 1440], P(None, 'lat', 'lev'), may hold values from -0.5 to 0.5
- route: int32 [64, 1440, 1], P('lat', 'lev'), may hold values from 0 to 127; in each aligned block of 180 rows (0 to 179, 180 to 359, ..., all dimensions but the last counted through in order) at most 3 rows name the same one
- inverse: float32 [16, 8, 288, 288], P('lat', 'lev'), may hold values from -0.5 to 1
Outputs:
- tendency: float32 [4, 72, 64, 1440], P(None, 'lev', 'lat')
The draws below stay inside these ranges and needn't reach their ends.
Inputs may be any that keep to these rules, and one draw needn't show every extreme that they name: `route`: in each latitude row and each group of 180 longitudes with equal b // 180, at most 3 columns name one span.
All inputs are finite; a program needn't handle non-finite values.
Results may differ from the reference program's by a relative error of at most 0.0003.
Values sent between devices are 32-bit elements; how exact they have to be, the bound alone decides.
A program may use at most 64 MiB of HBM per device.

```python
import math
import jax
import jax.numpy as jnp
import numpy as np
from jax import lax

TRAC = 4
LEVELS = 72
NLON = 1440
BANDS = 16
LONGROUPS = 8
SPANS = 128
NLAT = 64
LONDEV = 180
CAP = 3
ORDER = 288
N_LEV = 8


def draw_inverse(key, part):
    first_key, second_key = jax.random.split(jax.random.fold_in(key, 17))
    shape = (BANDS, LONGROUPS, ORDER, ORDER)
    identity = (jnp.arange(ORDER)[:, None] == jnp.arange(ORDER)[None, :]).astype(jnp.float32)
    diagonal = jax.random.uniform(first_key, shape, jnp.float32, 0.6, 1.0)
    spread = 0.25 / math.sqrt(ORDER)
    off_diag = jnp.clip(jax.random.normal(second_key, shape, jnp.float32), -6.0, 6.0) * spread
    return identity * diagonal + (1.0 - identity) * off_diag


def shard_levels(key, shape, cuts, smallest, high):
    def one(dim, parts):
        draws = jax.random.uniform(jax.random.fold_in(jax.random.fold_in(key, 6), dim), (parts,), jnp.float32, smallest / len(cuts), high / len(cuts))
        return jnp.repeat(jnp.exp(draws), shape[dim] // parts).reshape((-1,) + (1,) * (len(shape) - dim - 1))

    level = one(*cuts[0])
    for cut in cuts[1:]:
        level = level * one(*cut)
    return level


def deal_out(stream_key, own, number, rows, count, top, most, slope):
    sequence = jax.random.permutation(stream_key, count)
    heavy_load, usual = shares(count, rows * top, most, slope, True), shares(count, rows * top, most, slope, False)
    places = jnp.arange(count)

    def named(sizes, offset_by):
        used = int((sizes > 0).sum())
        fixed = max(1, used // 4)
        passed = fixed + (places - fixed + offset_by * (used - fixed)) % max(1, count - fixed)
        return jnp.zeros((count,), jnp.int32).at[sequence[jnp.where(places < fixed, places, passed)]].set(jnp.asarray(sizes, jnp.int32))

    sizes = jnp.where(number % 4 == 0, named(heavy_load, number // 4), named(usual, number - number // 4 - 1))
    mixed = jax.random.permutation(jax.random.fold_in(own, 3), count)
    giver, taker = mixed[0:count // 2 * 2:2], mixed[1:count // 2 * 2:2]
    room = jnp.minimum(sizes[giver] - 1, most - sizes[taker]) // 2
    room = jnp.where((giver == sequence[0]) | (taker == sequence[0]) | (sizes[taker] == 0), 0, jnp.maximum(room, 0))
    passed = jax.random.randint(jax.random.fold_in(own, 4), (count // 2,), 0, 1 << 20) % (room + 1)
    sizes = sizes.at[giver].add(-passed).at[taker].add(passed)
    labels = jnp.searchsorted(jnp.cumsum(sizes), jnp.arange(rows * top), side="right").astype(jnp.int32)
    listing = labels.reshape(top, rows).T
    listing = listing[jax.random.permutation(jax.random.fold_in(own, 1), rows)]
    offset_by = jax.random.randint(jax.random.fold_in(own, 2), (rows, 1), 0, top)
    return jnp.take_along_axis(listing, (jnp.arange(top)[None, :] + offset_by) % top, axis=1)


def shares(count, total, reach, lean, full):
    portions = [(1 << 20) // math.isqrt(grade ** lean) + 1 for grade in range(1, count + 1)]
    largest = reach if full else min(reach, max(-(-total // count), total * portions[0] // sum(portions)))
    least = 1 if total - largest >= count - 1 else 0
    holding, rest = [largest] + [least] * (count - 1), total - largest - least * (count - 1)
    while rest > 0:
        candidates = [i for i in range(1, count) if holding[i] < largest] or [i for i in range(1, count) if holding[i] < reach]
        pool, budget = sum([portions[i] for i in candidates]), rest
        for i in candidates:
            addition = min(reach - holding[i], max(1, budget * portions[i] // pool), rest)
            holding[i] = holding[i] + addition
            rest = rest - addition
    return np.array(holding)


def bell_draw(own_key, dims, deviation, bound, pieces=(), kind=jnp.bfloat16):
    gain = shard_levels(own_key, dims, pieces, -0.22, 0.18) if pieces else 1.0
    entries = jax.random.normal(own_key, dims, jnp.float32) * deviation * gain
    return jnp.minimum(jnp.maximum(entries, -bound), bound).astype(kind)


def setup_inputs(seed: int = 0) -> dict:
    seeds = jax.random.split(jax.random.key(seed), 7)
    tracers = bell_draw(seeds[0], (TRAC, LEVELS, NLAT, NLON), 1.0, 6.0, ((1, 8), (2, 16)), jnp.float32)
    zonal = jnp.clip(jax.random.uniform(seeds[1], (LEVELS, NLAT, NLON), jnp.float32, -0.6, 0.6) * shard_levels(seeds[1], (LEVELS, NLAT, NLON), ((0, 8), (1, 16)), -0.4, 0.0), -0.6, 0.6)
    meridional = jnp.clip(jax.random.uniform(seeds[2], (LEVELS, NLAT, NLON), jnp.float32, -0.5, 0.5) * shard_levels(seeds[2], (LEVELS, NLAT, NLON), ((0, 8), (1, 16)), -0.4, 0.0), -0.5, 0.5)
    vertical = jnp.clip(jax.random.uniform(seeds[3], (LEVELS, NLAT, NLON), jnp.float32, -0.5, 0.5) * shard_levels(seeds[3], (LEVELS, NLAT, NLON), ((1, 16), (2, 8)), -0.4, 0.0), -0.5, 0.5)
    route_keys = jax.random.split(jax.random.fold_in(seeds[4], 1), NLAT * NLON // LONDEV)
    route_turns = jax.random.permutation(jax.random.fold_in(seeds[4], 3), NLAT * NLON // LONDEV)
    route = jax.vmap(lambda own, number: deal_out(jax.random.fold_in(seeds[4], 2), own, number, LONDEV, SPANS, 1, CAP, 2))(route_keys, route_turns).reshape((NLAT, NLON, 1))
    inverse = draw_inverse(jax.random.fold_in(seeds[6], 71), 0)
    return dict(tracers=tracers, zonal=zonal, meridional=meridional, vertical=vertical, route=route, inverse=inverse)


def take_range(values, start, finish, axis):
    return lax.slice_in_dim(values, start, finish, axis=axis)


def edge_change(padded, courant, axis, cells):
    faces = (7.0 / 12.0) * (take_range(padded, 1, cells + 4, axis) + take_range(padded, 2, cells + 5, axis))
    faces = faces - (1.0 / 12.0) * (take_range(padded, 0, cells + 3, axis) + take_range(padded, 3, cells + 6, axis))
    left_face = take_range(faces, 0, cells + 2, axis)
    right_face = take_range(faces, 1, cells + 3, axis)
    centre = take_range(padded, 2, cells + 4, axis)
    slope_term = right_face - left_face
    curvature = 6.0 * (centre - 0.5 * (left_face + right_face))
    from_low = courant * (take_range(right_face, 0, cells + 1, axis) - 0.5 * courant * (take_range(slope_term, 0, cells + 1, axis) - (1.0 - 2.0 * courant / 3.0) * take_range(curvature, 0, cells + 1, axis)))
    reverse = -courant
    from_high = courant * (take_range(left_face, 1, cells + 2, axis) + 0.5 * reverse * (take_range(slope_term, 1, cells + 2, axis) + (1.0 - 2.0 * reverse / 3.0) * take_range(curvature, 1, cells + 2, axis)))
    edge_flux = jnp.where(courant >= 0.0, from_low, from_high)
    return take_range(edge_flux, 0, cells, axis) - take_range(edge_flux, 1, cells + 1, axis)


def reference(tracers, zonal, meridional, vertical, route, inverse):
    lon_courant = jnp.concatenate([zonal, zonal[:, :, :1]], axis=2)
    zero_row = jnp.zeros_like(meridional[:, :1, :])
    lat_courant = jnp.concatenate([zero_row, meridional[:, 1:, :], zero_row], axis=1)
    zero_level = jnp.zeros_like(vertical[:1])
    vert_courant = jnp.concatenate([zero_level, vertical[1:], zero_level], axis=0)

    def advect_one(single):
        lon_padded = jnp.concatenate([single[:, :, -3:], single, single[:, :, :3]], axis=2)
        lon_change = edge_change(lon_padded, lon_courant, 2, NLON)
        lat_padded = jnp.pad(single, ((0, 0), (3, 3), (0, 0)))
        lat_change = edge_change(lat_padded, lat_courant, 1, NLAT)
        horizontal = single + lon_change + lat_change
        vert_padded = jnp.pad(horizontal, ((3, 3), (0, 0), (0, 0)))
        return horizontal + edge_change(vert_padded, vert_courant, 0, LEVELS)

    advected = lax.map(advect_one, tracers)
    targets = route[:, :, 0].reshape(NLAT, N_LEV, LONDEV)
    lon_local = jnp.broadcast_to(jnp.arange(LONDEV, dtype=jnp.int32)[None, None, :], (NLAT, N_LEV, LONDEV))
    group_start = (jnp.arange(N_LEV, dtype=jnp.int32) * LONDEV)[None, :, None]
    row_ids = jnp.arange(NLAT, dtype=jnp.int32)[:, None, None]
    group_ids = jnp.arange(N_LEV, dtype=jnp.int32)[None, :, None]
    slot_ids = jnp.arange(CAP, dtype=jnp.int32)[None, None, :]
    order_size = TRAC * LEVELS
    start_out = jnp.zeros((TRAC, LEVELS, NLAT, NLON + 1), advected.dtype)

    def per_span(span_raw, running):
        span = jnp.asarray(span_raw).astype(jnp.int32)
        member = (targets == span).astype(jnp.int32)
        ranking = jnp.cumsum(member, axis=2) - 1
        place = jnp.where(member > 0, ranking, CAP).astype(jnp.int32)
        table = jnp.zeros((NLAT, N_LEV, CAP + 1), jnp.int32).at[row_ids, group_ids, place].set(lon_local)
        counted = jnp.sum(member, axis=2)[:, :, None]
        valid = slot_ids < counted
        lon_index = (table[:, :, :CAP] + group_start).astype(jnp.int32)
        values = advected[:, :, row_ids, lon_index]
        matrix = inverse[span // N_LEV, span % N_LEV]
        mixed = jnp.dot(matrix, values.reshape(order_size, -1), precision=lax.Precision.HIGHEST).reshape(values.shape)
        target_lon = jnp.where(valid, lon_index, NLON).astype(jnp.int32)
        return running.at[:, :, row_ids, target_lon].set(mixed)

    diffused = lax.fori_loop(0, SPANS, per_span, start_out)[:, :, :, :NLON]
    return diffused - tracers
```

```python
import functools
import jax
import jax.numpy as jnp
from jax import lax
from jax.experimental import pallas as pl
from jax.experimental.pallas import tpu as pltpu
from jax.sharding import PartitionSpec as P

MESH = pl.DeviceIdType.MESH
F32 = jnp.float32
BF16 = jnp.bfloat16
VMEM = pl.BlockSpec(memory_space=pltpu.VMEM)
NT = (((1,), (1,)), ((), ()))
NN = (((1,), (0,)), ((), ()))


def dot(a, b, dims=NN):
    return lax.dot_general(a, b, dims, preferred_element_type=F32)


def split(x):
    hi = x.astype(BF16)
    lo = (x - hi.astype(F32)).astype(BF16)
    return hi, lo


def flux(c, e, s_low, s_here, k_low, k_here):
    up = c >= 0.0
    a = jnp.abs(c)
    s = jnp.where(up, -s_low, s_here)
    k = jnp.where(up, k_low, k_here)
    return c * (e + (0.5 * a) * (s + (1.0 - (2.0 / 3.0) * a) * k))


def face(q_m2, q_m1, q_0, q_p1):
    return (7.0 / 12.0) * (q_m1 + q_0) - (1.0 / 12.0) * (q_m2 + q_p1)


def horizontal_kernel(tr_ref, south_ref, north_ref, zon_ref, mer_ref, mern_ref, g_ref):
    lat = lax.axis_index("lat")
    last = lax.axis_size("lat") - 1
    width = tr_ref.shape[3]
    groups = g_ref.shape[0]
    lon = width // groups
    sub = lax.broadcasted_iota(jnp.int32, (8, width), 0) < 4
    ext = -(-width // 128) * 128
    spare = ext - width
    half = spare // 3
    ksouth = (lat > 0).astype(F32)
    knorth = (lat < last).astype(F32)

    def swap(x):
        return pltpu.roll(x, 4, 0)

    def extend(x):
        return jnp.concatenate([x, x[:, :half], x[:, width - (spare - half):]], axis=1)

    def rolled(x, n):
        return pltpu.roll(x, n % ext, 1)

    def level(k, carry):
        row = [tr_ref[r, k] for r in range(4)]
        low = [south_ref[r, k] * ksouth for r in range(3)]
        high = [north_ref[r, k] * knorth for r in range(3)]
        pair = lambda a, b: jnp.concatenate([a, b], axis=0)
        q = [
            pair(low[0], low[0]),
            pair(low[1], low[2]),
            pair(row[0], row[1]),
            pair(row[2], row[3]),
            pair(high[0], high[1]),
            pair(high[2], high[2]),
        ]
        sq = [swap(x) for x in q]
        e = [face(q[p - 1], jnp.where(sub, sq[p - 1], sq[p]), q[p], jnp.where(sub, sq[p], sq[p + 1])) for p in range(1, 5)]
        se = [swap(x) for x in e]
        s, kk = [], []
        for p in range(4):
            right = jnp.where(sub, se[p], se[min(p + 1, 3)])
            s.append(right - e[p])
            kk.append(6.0 * q[p + 1] - 3.0 * (e[p] + right))
        ss = [swap(x) for x in s]
        sk = [swap(x) for x in kk]
        m = mer_ref[k]
        zero = jnp.zeros((8, width), F32)
        m0 = jnp.where(sub, m[0:1] * ksouth, m[1:2])
        m1 = jnp.where(sub, m[2:3], m[3:4])
        m2 = mern_ref[k] * knorth + zero
        f = []
        for i, c in enumerate((m0, m1, m2)):
            p = i + 1
            f.append(
                flux(c, e[p], jnp.where(sub, ss[p - 1], ss[p]), s[p], jnp.where(sub, sk[p - 1], sk[p]), kk[p])
            )
        sf = [swap(x) for x in f]
        z = zon_ref[k]
        out = []
        for p in range(2):
            lat_change = f[p] - jnp.where(sub, sf[p], sf[p + 1])
            x = extend(q[p + 2])
            c = extend(jnp.where(sub, z[2 * p : 2 * p + 1], z[2 * p + 1 : 2 * p + 2]))
            le = face(rolled(x, 2), rolled(x, 1), x, rolled(x, -1))
            right = rolled(le, -1)
            ls = right - le
            lk = 6.0 * x - 3.0 * (le + right)
            lf = flux(c, le, rolled(ls, 1), ls, rolled(lk, 1), lk)
            lon_change = lf - rolled(lf, -1)
            out.append(q[p + 2] + lon_change[:, :width] + lat_change)
        rest = lon - 128
        pad = jnp.zeros((8, 128 - 2 * rest), F32)
        for g in range(groups):
            o = g * lon
            g_ref[g, k] = jnp.concatenate(
                [
                    out[0][:, o : o + 128],
                    out[1][:, o : o + 128],
                    out[0][:, o + 128 : o + lon],
                    out[1][:, o + 128 : o + lon],
                    pad,
                ],
                axis=1,
            )
        return carry

    lax.fori_loop(0, tr_ref.shape[1], level, 0)


def selector(slot_ref, r):
    ids = lax.broadcasted_iota(jnp.int32, (512, 256), 0)
    return (ids == slot_ref[r : r + 1, :]).astype(F32).astype(BF16)


def select_kernel(rest, g_ref, c_ref, slot_ref, p_ref, a_ref):
    levels = g_ref.shape[0]
    sub = lax.broadcasted_iota(jnp.int32, (8, 384), 0) < 4
    half = lax.broadcasted_iota(jnp.int32, (8, 256), 0) < 4
    zero = jnp.zeros((8, 384), F32)
    for r in range(4):
        if r > 0:
            a_ref[r, 0 : 32 * r, :] = jnp.zeros((32 * r, 512), BF16)
        if r < 3:
            a_ref[r, 32 * r + 288 : 384, :] = jnp.zeros((96 - 32 * r, 512), BF16)

    def q(k):
        return g_ref[k] if 0 <= k < levels else zero

    def e_at(k):
        return face(q(k - 2), q(k - 1), q(k), q(k + 1))

    left = e_at(0)
    f_here = zero
    held = []
    right = e_at(1)
    s, kk = right - left, 6.0 * q(0) - 3.0 * (left + right)
    for k in range(levels):
        if k + 1 < levels:
            nxt = e_at(k + 2)
            s1, k1 = nxt - right, 6.0 * q(k + 1) - 3.0 * (right + nxt)
            c = jnp.where(sub, c_ref[k + 1, 0:1, :], c_ref[k + 1, 1:2, :])
            f_next = flux(c, right, s, s1, kk, k1)
            right, s, kk = nxt, s1, k1
        else:
            f_next = zero
        held.append(q(k) + f_here - f_next)
        f_here = f_next
        if k % 4 == 3:
            for rp in range(2):
                x = []
                for h in held:
                    third = h[:, 256:384]
                    if rp == 1:
                        third = pltpu.roll(third, 128 - rest, 1)
                    x.append(jnp.concatenate([h[:, 128 * rp : 128 * rp + 128], third], axis=1))
                t = [pltpu.roll(v, 4, 0) for v in x]
                first = [jnp.where(half, x[0], t[1]), jnp.where(half, x[2], t[3])]
                second = [jnp.where(half, t[0], x[1]), jnp.where(half, t[2], x[3])]
                for r2, rows in enumerate((first, second)):
                    r = 2 * rp + r2
                    hi, lo = split(jnp.concatenate(rows, axis=0))
                    at = 32 * r + 4 * (k - 3)
                    a_ref[r, at : at + 16, 0:256] = hi
                    a_ref[r, at : at + 16, 256:512] = lo
            held = []
    carried = None
    for r in range(4):
        one = selector(slot_ref, r)
        out = dot(jnp.concatenate([one, one], axis=1), a_ref[r], NT)
        for t in range(3):
            part = out[:, 128 * t : 128 * t + 128]
            if t == 0 and r > 0:
                part = part + carried
            if t == 2 and r < 3:
                carried = part
                continue
            p_ref[2 * r + t] = part.reshape(p_ref.shape[1:])


def reorder_kernel(m_ref, o_ref):
    order = m_ref.shape[0]
    levels = order // 4
    x = lax.broadcasted_iota(jnp.int32, (order, order), 0)
    o = lax.broadcasted_iota(jnp.int32, (order, order), 1)
    pick = ((x & 3) * levels + (x >> 2) == o).astype(F32)
    exact = dict(precision=lax.Precision.HIGHEST, preferred_element_type=F32)
    o_ref[...] = lax.dot_general(lax.dot_general(pick, m_ref[...], NN, **exact), pick, NT, **exact)


def route_kernel(lats, levs, p_ref, m_ref, v_ref, r_ref, y_ref, w_ref, ssem, rsem, lsem):
    lat, lev = lax.axis_index("lat"), lax.axis_index("lev")
    order = m_ref.shape[1]
    spans = m_ref.shape[0]
    barrier = pltpu.get_barrier_semaphore()
    for i in range(1, levs):
        pl.semaphore_signal(barrier, inc=1, device_id=(lat, lax.rem(lev + i, levs)), device_id_type=MESH)
    pl.semaphore_wait(barrier, levs - 1)

    def out_copy(i):
        to = lax.rem(lev + i, levs)
        return pltpu.make_async_remote_copy(
            src_ref=p_ref.at[:, to, :, 0:3],
            dst_ref=r_ref.at[:, :, lev, 0:3],
            send_sem=ssem.at[0, i],
            recv_sem=rsem.at[0, i],
            device_id=(lat, to),
            device_id_type=MESH,
        )

    def back_copy(i):
        to = lax.rem(lev + i, levs)
        return pltpu.make_async_remote_copy(
            src_ref=y_ref.at[:, :, to, 0:3],
            dst_ref=v_ref.at[:, lev, :, 0:3],
            send_sem=ssem.at[1, i],
            recv_sem=rsem.at[1, i],
            device_id=(lat, to),
            device_id_type=MESH,
        )

    own_out = pltpu.make_async_copy(p_ref.at[:, lev, :, 0:3], r_ref.at[:, :, lev, 0:3], lsem.at[0])
    own_back = pltpu.make_async_copy(y_ref.at[:, :, lev, 0:3], v_ref.at[:, lev, :, 0:3], lsem.at[1])
    own_out.start()
    for i in range(1, levs):
        out_copy(i).start()

    @pl.loop(0, spans)
    def _(n):
        hi, lo = split(m_ref[n])
        w_ref[0, n] = hi
        w_ref[1, n] = lo

    own_out.wait()
    for i in range(1, levs):
        out_copy(i).wait()

    @pl.loop(0, spans)
    def _(n):
        tiles = [r_ref[j, n].reshape(4 * levs, 128) for j in range(9)]
        rows = []
        for r in range(4):
            x = jnp.concatenate(tiles[2 * r : 2 * r + 3], axis=1)
            if r > 0:
                x = pltpu.roll(x, 384 - 32 * r, 1)
            rows.append(x[:, :order])
        hi, lo = split(jnp.concatenate(rows, axis=0))
        y = dot(hi, w_ref[0, n], NT) + dot(lo, w_ref[0, n], NT) + dot(hi, w_ref[1, n], NT)
        size = 4 * levs
        carried = None
        for r in range(4):
            x = jnp.concatenate([y[r * size : (r + 1) * size], jnp.zeros((size, 384 - order), F32)], axis=1)
            if r > 0:
                x = pltpu.roll(x, 32 * r, 1)
            for t in range(3):
                part = x[:, 128 * t : 128 * t + 128]
                if t == 0 and r > 0:
                    part = part + carried
                if t == 2 and r < 3:
                    carried = part
                    continue
                y_ref[2 * r + t, n] = part.reshape(levs, 4, 128)

    own_back.start()
    for i in range(1, levs):
        back_copy(i).start()
    own_back.wait()
    for i in range(1, levs):
        back_copy(i).wait()


def unselect_kernel(rest, v_ref, slot_ref, d_ref):
    lane = lax.broadcasted_iota(jnp.int32, (128, 512), 1)
    live = (lane & 3) < 3
    turned = [jnp.where(live, v_ref[j].reshape(512, 128).T, 0.0) for j in range(9)]
    turned = jnp.concatenate(turned, axis=0)
    whole = []
    for r in range(4):
        hi, lo = split(turned[288 * r : 288 * r + 288])
        one = selector(slot_ref, r)
        whole.append(dot(jnp.concatenate([hi, lo], axis=1), jnp.concatenate([one, one], axis=0)))
    sub = lax.broadcasted_iota(jnp.int32, (8, 256), 0) < 4
    lane = lax.broadcasted_iota(jnp.int32, (8, 128), 1)
    for n in range(d_ref.shape[0] // 2):
        even, odd = [], []
        for rp in range(2):
            x = whole[2 * rp][8 * n : 8 * n + 8]
            y = whole[2 * rp + 1][8 * n : 8 * n + 8]
            even.append(jnp.where(sub, x, pltpu.roll(y, 4, 0)))
            odd.append(jnp.where(sub, pltpu.roll(x, 4, 0), y))
        for i, (a, b) in enumerate((even, odd)):
            third = jnp.where(lane < rest, a[:, 128:], pltpu.roll(b[:, 128:], rest, 1))
            d_ref[2 * n + i] = jnp.concatenate([a[:, :128], b[:, :128], third], axis=1)


def assemble_kernel(lon, d_ref, o_ref):
    groups = d_ref.shape[0]
    rest = lon - 128

    def level(k, carry):
        for rp in range(2):
            parts = []
            for g in range(groups):
                x = d_ref[g, k]
                parts.append(x[:, 128 * rp : 128 * rp + 128])
                parts.append(x[:, 256 + rest * rp : 256 + rest * rp + rest])
            o_ref[rp, k] = jnp.concatenate(parts, axis=1)
        return carry

    lax.fori_loop(0, d_ref.shape[1], level, 0)


def call(kernel, shape, count, scratch=(), limit=48, **params):
    return pl.pallas_call(
        kernel,
        out_shape=jax.ShapeDtypeStruct(shape, F32),
        in_specs=[VMEM] * count,
        out_specs=VMEM,
        scratch_shapes=list(scratch),
        compiler_params=pltpu.CompilerParams(vmem_limit_bytes=limit << 20, **params),
    )


def body(tracers, zonal, meridional, vertical, route, inverse):
    trac, levs_here, rows, width = tracers.shape
    lats, groups = lax.axis_size("lat"), lax.axis_size("lev")
    levels, _, lon = vertical.shape
    rest = lon - 128
    matrix = call(reorder_kernel, inverse.shape[2:], 1)(inverse[0, 0])
    matrices = lax.all_gather(matrix, "lat")
    turned = jnp.transpose(tracers, (2, 1, 0, 3))
    up = [(i, i + 1) for i in range(lats - 1)]
    down = [(i + 1, i) for i in range(lats - 1)]
    south = lax.ppermute(turned[rows - 3 :], "lat", up)
    north = lax.ppermute(turned[:3], "lat", down)
    mer_north = lax.ppermute(meridional[:, :1], "lat", down)
    targets = route[:, :, 0]
    before = jnp.arange(lon)[:, None] < jnp.arange(lon)[None, :]
    same = jnp.logical_and(targets[:, :, None] == targets[:, None, :], before[None])
    place = (targets % groups) * lats + targets // groups
    slots = place * 4 + jnp.sum(same.astype(jnp.int32), axis=1)
    slots = jnp.pad(slots, ((0, 0), (0, 256 - lon)), constant_values=-1)
    v = vertical.reshape(levels, 2, 2, lon)
    courant = jnp.concatenate(
        [v[:, 0, :, :128], v[:, 1, :, :128], v[:, 0, :, 128:], v[:, 1, :, 128:], jnp.zeros((levels, 2, 128 - 2 * rest), F32)],
        axis=-1,
    )
    sent = call(horizontal_kernel, (groups, levs_here, 8, 384), 6)(turned, south, north, zonal, meridional, mer_north)
    columns = lax.all_to_all(sent, "lev", split_axis=0, concat_axis=0, tiled=True)
    columns = columns.reshape(levels, 8, 384)
    packed = call(
        functools.partial(select_kernel, rest), (9, groups, lats, 4, 128), 3, [pltpu.VMEM((4, 384, 512), BF16)]
    )(columns, courant, slots)
    order = matrix.shape[0]
    back = call(
        functools.partial(route_kernel, lats, groups),
        (9, groups, lats, 4, 128),
        2,
        [
            pltpu.VMEM((9, lats, groups, 4, 128), F32),
            pltpu.VMEM((9, lats, groups, 4, 128), F32),
            pltpu.VMEM((2, lats, order, order), BF16),
            pltpu.SemaphoreType.DMA((2, groups)),
            pltpu.SemaphoreType.DMA((2, groups)),
            pltpu.SemaphoreType.DMA((2,)),
        ],
        collective_id=0,
        has_side_effects=True,
    )(packed, matrices)
    diffused = call(functools.partial(unselect_kernel, rest), (levels, 8, 384), 2)(back, slots)
    owned = lax.all_to_all(diffused.reshape(groups, levs_here, 8, 384), "lev", split_axis=0, concat_axis=0, tiled=True)
    whole = call(functools.partial(assemble_kernel, lon), (2, levs_here, 8, width), 1)(owned)
    whole = whole.reshape(2, levs_here, 2, trac, width)
    return jnp.transpose(whole, (3, 1, 0, 2, 4)).reshape(tracers.shape) - tracers


def solution(mesh):
    in_specs = (
        P(None, "lev", "lat", None),
        P("lev", "lat", None),
        P("lev", "lat", None),
        P(None, "lat", "lev"),
        P("lat", "lev", None),
        P("lat", "lev", None, None),
    )
    out_specs = P(None, "lev", "lat", None)
    return jax.shard_map(body, mesh=mesh, in_specs=in_specs, out_specs=out_specs, check_vma=False)
```

```python
import functools
import jax
import jax.numpy as jnp
from jax import lax
from jax.experimental import pallas as pl
from jax.experimental.pallas import tpu as pltpu
from jax.sharding import PartitionSpec as P

MESH = pl.DeviceIdType.MESH
F32 = jnp.float32
BF16 = jnp.bfloat16
VMEM = pl.BlockSpec(memory_space=pltpu.VMEM)
NT = (((1,), (1,)), ((), ()))
NN = (((1,), (0,)), ((), ()))


def dot(a, b, dims=NN):
    return lax.dot_general(a, b, dims, preferred_element_type=F32)


def split(x):
    hi = x.astype(BF16)
    lo = (x - hi.astype(F32)).astype(BF16)
    return hi, lo


def flux(c, e, s_low, s_here, k_low, k_here):
    up = c >= 0.0
    a = jnp.abs(c)
    s = jnp.where(up, -s_low, s_here)
    k = jnp.where(up, k_low, k_here)
    return c * (e + (0.5 * a) * (s + (1.0 - (2.0 / 3.0) * a) * k))


def face(q_m2, q_m1, q_0, q_p1):
    return (7.0 / 12.0) * (q_m1 + q_0) - (1.0 / 12.0) * (q_m2 + q_p1)


def horizontal(tr_ref, south_ref, north_ref, zon_ref, mer_ref, mern_ref, g_ref, ready):
    lat = lax.axis_index("lat")
    last = lax.axis_size("lat") - 1
    width = tr_ref.shape[3]
    groups = g_ref.shape[0]
    lon = width // groups
    sub = lax.broadcasted_iota(jnp.int32, (8, width), 0) < 4
    ext = -(-width // 128) * 128
    spare = ext - width
    half = spare // 3
    ksouth = (lat > 0).astype(F32)
    knorth = (lat < last).astype(F32)

    def swap(x):
        return pltpu.roll(x, 4, 0)

    def extend(x):
        return jnp.concatenate([x, x[:, :half], x[:, width - (spare - half):]], axis=1)

    def rolled(x, n):
        return pltpu.roll(x, n % ext, 1)

    def level(k, carry):
        row = [tr_ref[r, k] for r in range(4)]
        low = [south_ref[r, k] * ksouth for r in range(3)]
        high = [north_ref[r, k] * knorth for r in range(3)]
        pair = lambda a, b: jnp.concatenate([a, b], axis=0)
        q = [
            pair(low[0], low[0]),
            pair(low[1], low[2]),
            pair(row[0], row[1]),
            pair(row[2], row[3]),
            pair(high[0], high[1]),
            pair(high[2], high[2]),
        ]
        sq = [swap(x) for x in q]
        e = [face(q[p - 1], jnp.where(sub, sq[p - 1], sq[p]), q[p], jnp.where(sub, sq[p], sq[p + 1])) for p in range(1, 5)]
        se = [swap(x) for x in e]
        s, kk = [], []
        for p in range(4):
            right = jnp.where(sub, se[p], se[min(p + 1, 3)])
            s.append(right - e[p])
            kk.append(6.0 * q[p + 1] - 3.0 * (e[p] + right))
        ss = [swap(x) for x in s]
        sk = [swap(x) for x in kk]
        m = mer_ref[k]
        zero = jnp.zeros((8, width), F32)
        m0 = jnp.where(sub, m[0:1] * ksouth, m[1:2])
        m1 = jnp.where(sub, m[2:3], m[3:4])
        m2 = mern_ref[k] * knorth + zero
        f = []
        for i, c in enumerate((m0, m1, m2)):
            p = i + 1
            f.append(
                flux(c, e[p], jnp.where(sub, ss[p - 1], ss[p]), s[p], jnp.where(sub, sk[p - 1], sk[p]), kk[p])
            )
        sf = [swap(x) for x in f]
        z = zon_ref[k]
        out = []
        for p in range(2):
            lat_change = f[p] - jnp.where(sub, sf[p], sf[p + 1])
            x = extend(q[p + 2])
            c = extend(jnp.where(sub, z[2 * p : 2 * p + 1], z[2 * p + 1 : 2 * p + 2]))
            le = face(rolled(x, 2), rolled(x, 1), x, rolled(x, -1))
            right = rolled(le, -1)
            ls = right - le
            lk = 6.0 * x - 3.0 * (le + right)
            lf = flux(c, le, rolled(ls, 1), ls, rolled(lk, 1), lk)
            lon_change = lf - rolled(lf, -1)
            out.append(q[p + 2] + lon_change[:, :width] + lat_change)
        rest = lon - 128
        pad = jnp.zeros((8, 128 - 2 * rest), F32)
        for g in range(groups):
            o = g * lon
            g_ref[g, k] = jnp.concatenate(
                [
                    out[0][:, o : o + 128],
                    out[1][:, o : o + 128],
                    out[0][:, o + 128 : o + lon],
                    out[1][:, o + 128 : o + lon],
                    pad,
                ],
                axis=1,
            )
        ready(k)
        return carry

    lax.fori_loop(0, tr_ref.shape[1], level, 0)


def selector(slot_ref, r):
    ids = lax.broadcasted_iota(jnp.int32, (512, 256), 0)
    return (ids == slot_ref[r : r + 1, :]).astype(F32).astype(BF16)


def select(rest, g_ref, c_ref, slot_ref, p_ref, a_ref, ready):
    block = g_ref.shape[1]
    levels = g_ref.shape[0] * block
    sub = lax.broadcasted_iota(jnp.int32, (8, 384), 0) < 4
    half = lax.broadcasted_iota(jnp.int32, (8, 256), 0) < 4
    zero = jnp.zeros((8, 384), F32)
    for r in range(4):
        if r > 0:
            a_ref[r, 0 : 32 * r, :] = jnp.zeros((32 * r, 512), BF16)
        if r < 3:
            a_ref[r, 32 * r + 288 : 384, :] = jnp.zeros((96 - 32 * r, 512), BF16)

    def q(k):
        return g_ref[k // block, k % block] if 0 <= k < levels else zero

    def e_at(k):
        return face(q(k - 2), q(k - 1), q(k), q(k + 1))

    left = e_at(0)
    f_here = zero
    held = []
    right = e_at(1)
    s, kk = right - left, 6.0 * q(0) - 3.0 * (left + right)
    for k in range(levels):
        if k + 1 < levels:
            nxt = e_at(k + 2)
            s1, k1 = nxt - right, 6.0 * q(k + 1) - 3.0 * (right + nxt)
            c = jnp.where(sub, c_ref[k + 1, 0:1, :], c_ref[k + 1, 1:2, :])
            f_next = flux(c, right, s, s1, kk, k1)
            right, s, kk = nxt, s1, k1
        else:
            f_next = zero
        held.append(q(k) + f_here - f_next)
        f_here = f_next
        if k % 4 == 3:
            for rp in range(2):
                x = []
                for h in held:
                    third = h[:, 256:384]
                    if rp == 1:
                        third = pltpu.roll(third, 128 - rest, 1)
                    x.append(jnp.concatenate([h[:, 128 * rp : 128 * rp + 128], third], axis=1))
                t = [pltpu.roll(v, 4, 0) for v in x]
                first = [jnp.where(half, x[0], t[1]), jnp.where(half, x[2], t[3])]
                second = [jnp.where(half, t[0], x[1]), jnp.where(half, t[2], x[3])]
                for r2, rows in enumerate((first, second)):
                    r = 2 * rp + r2
                    hi, lo = split(jnp.concatenate(rows, axis=0))
                    at = 32 * r + 4 * (k - 3)
                    a_ref[r, at : at + 16, 0:256] = hi
                    a_ref[r, at : at + 16, 256:512] = lo
            held = []
    carried = None
    for r in range(4):
        one = selector(slot_ref, r)
        out = dot(jnp.concatenate([one, one], axis=1), a_ref[r], NT)
        for t in range(3):
            part = out[:, 128 * t : 128 * t + 128]
            if t == 0 and r > 0:
                part = part + carried
            if t == 2 and r < 3:
                carried = part
                continue
            p_ref[2 * r + t] = part.reshape(p_ref.shape[1:])
        ready(r)


def reorder_kernel(m_ref, o_ref):
    order = m_ref.shape[0]
    levels = order // 4
    x = lax.broadcasted_iota(jnp.int32, (order, order), 0)
    o = lax.broadcasted_iota(jnp.int32, (order, order), 1)
    pick = ((x & 3) * levels + (x >> 2) == o).astype(F32)
    exact = dict(precision=lax.Precision.HIGHEST, preferred_element_type=F32)
    out = lax.dot_general(lax.dot_general(pick, m_ref[...], NN, **exact), pick, NT, **exact)
    part = order // 4
    o_ref[0:order] = out[:, 0:128]
    o_ref[order : 2 * order] = out[:, 128:256]
    o_ref[2 * order :] = jnp.concatenate([out[part * i : part * i + part, 256:] for i in range(4)], axis=1)


def unpacked(packed):
    part = packed.shape[0] // 9
    third = packed[8 * part :]
    lanes = third.shape[1] // 4
    third = jnp.concatenate([third[:, lanes * i : lanes * i + lanes] for i in range(4)], axis=0)
    return jnp.concatenate([packed[: 4 * part], packed[4 * part : 8 * part], third], axis=1)


def unselect(rest, v_ref, slot_ref, d_ref):
    lane = lax.broadcasted_iota(jnp.int32, (128, 512), 1)
    live = (lane & 3) < 3
    turned = [jnp.where(live, v_ref[j].reshape(512, 128).T, 0.0) for j in range(9)]
    turned = jnp.concatenate(turned, axis=0)
    whole = []
    for r in range(4):
        hi, lo = split(turned[288 * r : 288 * r + 288])
        one = selector(slot_ref, r)
        whole.append(dot(jnp.concatenate([hi, lo], axis=1), jnp.concatenate([one, one], axis=0)))
    sub = lax.broadcasted_iota(jnp.int32, (8, 256), 0) < 4
    lane = lax.broadcasted_iota(jnp.int32, (8, 128), 1)
    block = d_ref.shape[1]
    for n in range(d_ref.shape[0] * block // 2):
        even, odd = [], []
        for rp in range(2):
            x = whole[2 * rp][8 * n : 8 * n + 8]
            y = whole[2 * rp + 1][8 * n : 8 * n + 8]
            even.append(jnp.where(sub, x, pltpu.roll(y, 4, 0)))
            odd.append(jnp.where(sub, pltpu.roll(x, 4, 0), y))
        for i, (a, b) in enumerate((even, odd)):
            third = jnp.where(lane < rest, a[:, 128:], pltpu.roll(b[:, 128:], rest, 1))
            d_ref[(2 * n + i) // block, (2 * n + i) % block] = jnp.concatenate([a[:, :128], b[:, :128], third], axis=1)


def assemble(lon, d_ref, o_ref):
    groups = d_ref.shape[0]
    rest = lon - 128

    def level(k, carry):
        for rp in range(2):
            parts = []
            for g in range(groups):
                x = d_ref[g, k]
                parts.append(x[:, 128 * rp : 128 * rp + 128])
                parts.append(x[:, 256 + rest * rp : 256 + rest * rp + rest])
            o_ref[rp, k] = jnp.concatenate(parts, axis=1)
        return carry

    lax.fori_loop(0, d_ref.shape[1], level, 0)


CHUNKS = 4


def greet(lat, lev, levs):
    barrier = pltpu.get_barrier_semaphore()
    for i in range(1, levs):
        pl.semaphore_signal(barrier, inc=1, device_id=(lat, lax.rem(lev + i, levs)), device_id_type=MESH)
    pl.semaphore_wait(barrier, levs - 1)


def send(src, dst, ssem, rsem, lat, to):
    return pltpu.make_async_remote_copy(
        src_ref=src, dst_ref=dst, send_sem=ssem, recv_sem=rsem, device_id=(lat, to), device_id_type=MESH
    )


def forth_kernel(
    rest, levs, tr_ref, south_ref, north_ref, zon_ref, mer_ref, mern_ref, c_ref, slot_ref,
    r_ref, g_ref, col_ref, p_ref, a_ref, s1, r1, s2, r2, lsem,
):
    lat, lev = lax.axis_index("lat"), lax.axis_index("lev")
    block = tr_ref.shape[1]
    greet(lat, lev, levs)

    def level_copy(k, i):
        to = lax.rem(lev + i, levs)
        return send(g_ref.at[to, k], col_ref.at[lev, k], s1.at[k, i], r1.at[k, i], lat, to)

    def level_ready(k):
        for i in range(1, levs):
            level_copy(k, i).start()

    horizontal(tr_ref, south_ref, north_ref, zon_ref, mer_ref, mern_ref, g_ref, level_ready)
    own = pltpu.make_async_copy(g_ref.at[lev], col_ref.at[lev], lsem.at[0])
    own.start()
    own.wait()

    @pl.loop(0, block)
    def _(k):
        for i in range(1, levs):
            level_copy(k, i).wait()

    def tiles(r):
        return slice(2 * r, 2 * r + (3 if r == 3 else 2))

    def row_copy(r, i):
        to = lax.rem(lev + i, levs)
        return send(p_ref.at[tiles(r), to, :, 0:3], r_ref.at[tiles(r), :, lev, 0:3], s2.at[r, i], r2.at[r, i], lat, to)

    def row_ready(r):
        for i in range(1, levs):
            row_copy(r, i).start()

    select(rest, col_ref, c_ref, slot_ref, p_ref, a_ref, row_ready)
    own = pltpu.make_async_copy(p_ref.at[:, lev, :, 0:3], r_ref.at[:, :, lev, 0:3], lsem.at[1])
    own.start()
    own.wait()
    for r in range(4):
        for i in range(1, levs):
            row_copy(r, i).wait()


def back_kernel(
    rest, levs, order, r_ref, near_ref, far_ref, slot_ref,
    o_ref, y_ref, v_ref, w_ref, d_ref, own_ref, s1, r1, s2, r2, lsem,
):
    lat, lev = lax.axis_index("lat"), lax.axis_index("lev")
    lats = r_ref.shape[1]
    size = lats // CHUNKS
    greet(lat, lev, levs)

    def back_copy(q, i):
        to = lax.rem(lev + i, levs)
        part = slice(q * size, q * size + size)
        return send(y_ref.at[:, part, to, 0:3], v_ref.at[:, lev, part, 0:3], s1.at[q, i], r1.at[q, i], lat, to)

    @pl.loop(0, lats // 2)
    def _(n):
        steps, turn = n // 2, lax.rem(n, 2)
        chip = lax.rem(lat // 4 - steps + 4, 4) * 4 + lax.rem(lat // 2 + turn, 2) * 2
        for ref, core in ((near_ref, lax.rem(lat, 2)), (far_ref, lax.rem(lat + 1, 2))):
            hi, lo = split(unpacked(ref[n]))
            w_ref[0, chip + core] = hi
            w_ref[1, chip + core] = lo

    def mix(n):
        tiles = [r_ref[j, n].reshape(4 * levs, 128) for j in range(9)]
        rows = []
        for r in range(4):
            x = jnp.concatenate(tiles[2 * r : 2 * r + 3], axis=1)
            if r > 0:
                x = pltpu.roll(x, 384 - 32 * r, 1)
            rows.append(x[:, :order])
        hi, lo = split(jnp.concatenate(rows, axis=0))
        y = dot(hi, w_ref[0, n], NT) + dot(lo, w_ref[0, n], NT) + dot(hi, w_ref[1, n], NT)
        many = 4 * levs
        carried = None
        for r in range(4):
            x = jnp.concatenate([y[r * many : (r + 1) * many], jnp.zeros((many, 384 - order), F32)], axis=1)
            if r > 0:
                x = pltpu.roll(x, 32 * r, 1)
            for t in range(3):
                part = x[:, 128 * t : 128 * t + 128]
                if t == 0 and r > 0:
                    part = part + carried
                if t == 2 and r < 3:
                    carried = part
                    continue
                y_ref[2 * r + t, n] = part.reshape(levs, 4, 128)

    for q in range(CHUNKS):
        pl.loop(q * size, q * size + size)(mix)
        for i in range(1, levs):
            back_copy(q, i).start()
    own = pltpu.make_async_copy(y_ref.at[:, :, lev, 0:3], v_ref.at[:, lev, :, 0:3], lsem.at[0])
    own.start()
    own.wait()
    for q in range(CHUNKS):
        for i in range(1, levs):
            back_copy(q, i).wait()

    unselect(rest, v_ref, slot_ref, d_ref)

    def level_copy(i):
        to = lax.rem(lev + i, levs)
        return send(d_ref.at[to], own_ref.at[lev], s2.at[i], r2.at[i], lat, to)

    for i in range(1, levs):
        level_copy(i).start()
    own = pltpu.make_async_copy(d_ref.at[lev], own_ref.at[lev], lsem.at[1])
    own.start()
    own.wait()
    for i in range(1, levs):
        level_copy(i).wait()
    assemble(128 + rest, own_ref, o_ref)


def call(kernel, shape, count, scratch=(), limit=48, **params):
    return pl.pallas_call(
        kernel,
        out_shape=jax.ShapeDtypeStruct(shape, F32),
        in_specs=[VMEM] * count,
        out_specs=VMEM,
        scratch_shapes=list(scratch),
        compiler_params=pltpu.CompilerParams(vmem_limit_bytes=limit << 20, **params),
    )


def body(tracers, zonal, meridional, vertical, route, inverse):
    trac, levs_here, rows, width = tracers.shape
    lats, groups = lax.axis_size("lat"), lax.axis_size("lev")
    levels, _, lon = vertical.shape
    rest = lon - 128
    order = inverse.shape[2]
    matrix = call(reorder_kernel, (order * order // 128, 128), 1)(inverse[0, 0])
    across = lax.ppermute(matrix, "lat", [(i, i ^ 2) for i in range(lats)])
    pair = jnp.stack([matrix, across])
    turned = jnp.transpose(tracers, (2, 1, 0, 3))
    up = [(i, i + 1) for i in range(lats - 1)]
    down = [(i + 1, i) for i in range(lats - 1)]
    south = lax.ppermute(turned[rows - 3 :], "lat", up)
    north = lax.ppermute(turned[:3], "lat", down)
    mer_north = lax.ppermute(meridional[:, :1], "lat", down)
    targets = route[:, :, 0]
    before = jnp.arange(lon)[:, None] < jnp.arange(lon)[None, :]
    same = jnp.logical_and(targets[:, :, None] == targets[:, None, :], before[None])
    place = (targets % groups) * lats + targets // groups
    slots = place * 4 + jnp.sum(same.astype(jnp.int32), axis=1)
    slots = jnp.pad(slots, ((0, 0), (0, 256 - lon)), constant_values=-1)
    v = vertical.reshape(levels, 2, 2, lon)
    courant = jnp.concatenate(
        [v[:, 0, :, :128], v[:, 1, :, :128], v[:, 0, :, 128:], v[:, 1, :, 128:], jnp.zeros((levels, 2, 128 - 2 * rest), F32)],
        axis=-1,
    )
    south, north, mer_north, pair = lax.optimization_barrier((south, north, mer_north, pair))
    shifted = [lax.ppermute(pair, "lat", [(i, (i + 4 * d) % lats) for i in range(lats)]) for d in range(1, 4)]
    dma = pltpu.SemaphoreType.DMA
    levels_of = pltpu.VMEM((groups, levs_here, 8, 384), F32)
    received = call(
        functools.partial(forth_kernel, rest, groups),
        (9, lats, groups, 4, 128),
        8,
        [
            levels_of,
            levels_of,
            pltpu.VMEM((9, groups, lats, 4, 128), F32),
            pltpu.VMEM((4, 384, 512), BF16),
            dma((levs_here, groups)),
            dma((levs_here, groups)),
            dma((4, groups)),
            dma((4, groups)),
            dma((2,)),
        ],
        collective_id=0,
        has_side_effects=True,
    )(turned, south, north, zonal, meridional, mer_north, courant, slots)
    received, shifted = lax.optimization_barrier((received, shifted))
    near = jnp.concatenate([pair] + shifted, axis=0)
    far = lax.ppermute(near, "lat", [(i, i ^ 1) for i in range(lats)])
    whole = call(
        functools.partial(back_kernel, rest, groups, order),
        (2, levs_here, 8, width),
        4,
        [
            pltpu.VMEM((9, lats, groups, 4, 128), F32),
            pltpu.VMEM((9, groups, lats, 4, 128), F32),
            pltpu.VMEM((2, lats, order, order), BF16),
            levels_of,
            levels_of,
            dma((CHUNKS, groups)),
            dma((CHUNKS, groups)),
            dma((groups,)),
            dma((groups,)),
            dma((2,)),
        ],
        collective_id=1,
        has_side_effects=True,
    )(received, near, far, slots)
    whole = whole.reshape(2, levs_here, 2, trac, width)
    return jnp.transpose(whole, (3, 1, 0, 2, 4)).reshape(tracers.shape) - tracers


def solution(mesh):
    in_specs = (
        P(None, "lev", "lat", None),
        P("lev", "lat", None),
        P("lev", "lat", None),
        P(None, "lat", "lev"),
        P("lat", "lev", None),
        P("lat", "lev", None, None),
    )
    out_specs = P(None, "lev", "lat", None)
    return jax.shard_map(body, mesh=mesh, in_specs=in_specs, out_specs=out_specs, check_vma=False)
```

```python
import functools
import jax
import jax.numpy as jnp
from jax import lax
from jax.experimental import pallas as pl
from jax.experimental.pallas import tpu as pltpu
from jax.sharding import PartitionSpec as P

MESH = pl.DeviceIdType.MESH
F32 = jnp.float32
BF16 = jnp.bfloat16
VMEM = pl.BlockSpec(memory_space=pltpu.VMEM)
NT = (((1,), (1,)), ((), ()))
NN = (((1,), (0,)), ((), ()))


def dot(a, b, dims=NN):
    return lax.dot_general(a, b, dims, preferred_element_type=F32)


def split(x):
    hi = x.astype(BF16)
    lo = (x - hi.astype(F32)).astype(BF16)
    return hi, lo


def flux(c, e, s_low, s_here, k_low, k_here):
    up = c >= 0.0
    a = jnp.abs(c)
    s = jnp.where(up, -s_low, s_here)
    k = jnp.where(up, k_low, k_here)
    return c * (e + (0.5 * a) * (s + (1.0 - (2.0 / 3.0) * a) * k))


def face(q_m2, q_m1, q_0, q_p1):
    return (7.0 / 12.0) * (q_m1 + q_0) - (1.0 / 12.0) * (q_m2 + q_p1)


def horizontal(tr_ref, south_ref, north_ref, zon_ref, mer_ref, g_ref, ready):
    lat = lax.axis_index("lat")
    last = lax.axis_size("lat") - 1
    width = tr_ref.shape[3]
    groups = g_ref.shape[0]
    lon = width // groups
    sub = lax.broadcasted_iota(jnp.int32, (8, width), 0) < 4
    ext = -(-width // 128) * 128
    spare = ext - width
    half = spare // 3
    ksouth = (lat > 0).astype(F32)
    knorth = (lat < last).astype(F32)

    def swap(x):
        return pltpu.roll(x, 4, 0)

    def extend(x):
        return jnp.concatenate([x, x[:, :half], x[:, width - (spare - half):]], axis=1)

    def rolled(x, n):
        return pltpu.roll(x, n % ext, 1)

    def level(k, carry):
        row = [tr_ref[r, k] for r in range(4)]
        low = [south_ref[r, k] * ksouth for r in range(3)]
        high = [north_ref[r * tr_ref.shape[1] + k] * knorth for r in range(3)]
        pair = lambda a, b: jnp.concatenate([a, b], axis=0)
        q = [
            pair(low[0], low[0]),
            pair(low[1], low[2]),
            pair(row[0], row[1]),
            pair(row[2], row[3]),
            pair(high[0], high[1]),
            pair(high[2], high[2]),
        ]
        sq = [swap(x) for x in q]
        e = [face(q[p - 1], jnp.where(sub, sq[p - 1], sq[p]), q[p], jnp.where(sub, sq[p], sq[p + 1])) for p in range(1, 5)]
        se = [swap(x) for x in e]
        s, kk = [], []
        for p in range(4):
            right = jnp.where(sub, se[p], se[min(p + 1, 3)])
            s.append(right - e[p])
            kk.append(6.0 * q[p + 1] - 3.0 * (e[p] + right))
        ss = [swap(x) for x in s]
        sk = [swap(x) for x in kk]
        m = mer_ref[k]
        zero = jnp.zeros((8, width), F32)
        m0 = jnp.where(sub, m[0:1] * ksouth, m[1:2])
        m1 = jnp.where(sub, m[2:3], m[3:4])
        m2 = north_ref[3 * tr_ref.shape[1] + k // 4, pl.ds(k % 4, 1), :] * knorth + zero
        f = []
        for i, c in enumerate((m0, m1, m2)):
            p = i + 1
            f.append(
                flux(c, e[p], jnp.where(sub, ss[p - 1], ss[p]), s[p], jnp.where(sub, sk[p - 1], sk[p]), kk[p])
            )
        sf = [swap(x) for x in f]
        z = zon_ref[k]
        out = []
        for p in range(2):
            lat_change = f[p] - jnp.where(sub, sf[p], sf[p + 1])
            x = extend(q[p + 2])
            c = extend(jnp.where(sub, z[2 * p : 2 * p + 1], z[2 * p + 1 : 2 * p + 2]))
            le = face(rolled(x, 2), rolled(x, 1), x, rolled(x, -1))
            right = rolled(le, -1)
            ls = right - le
            lk = 6.0 * x - 3.0 * (le + right)
            lf = flux(c, le, rolled(ls, 1), ls, rolled(lk, 1), lk)
            lon_change = lf - rolled(lf, -1)
            out.append(q[p + 2] + lon_change[:, :width] + lat_change)
        rest = lon - 128
        pad = jnp.zeros((8, 128 - 2 * rest), F32)
        for g in range(groups):
            o = g * lon
            g_ref[g, k] = jnp.concatenate(
                [
                    out[0][:, o : o + 128],
                    out[1][:, o : o + 128],
                    out[0][:, o + 128 : o + lon],
                    out[1][:, o + 128 : o + lon],
                    pad,
                ],
                axis=1,
            )
        ready(k)
        return carry

    lax.fori_loop(0, tr_ref.shape[1], level, 0)


def selector(slot_ref, r):
    ids = lax.broadcasted_iota(jnp.int32, (512, 256), 0)
    return (ids == slot_ref[r : r + 1, :]).astype(F32).astype(BF16)


def select(rest, g_ref, c_ref, slot_ref, p_ref, a_ref, ready):
    block = g_ref.shape[1]
    levels = g_ref.shape[0] * block
    sub = lax.broadcasted_iota(jnp.int32, (8, 384), 0) < 4
    half = lax.broadcasted_iota(jnp.int32, (8, 256), 0) < 4
    zero = jnp.zeros((8, 384), F32)
    for r in range(4):
        if r > 0:
            a_ref[r, 0 : 32 * r, :] = jnp.zeros((32 * r, 512), BF16)
        if r < 3:
            a_ref[r, 32 * r + 288 : 384, :] = jnp.zeros((96 - 32 * r, 512), BF16)

    def q(k):
        return g_ref[k // block, k % block] if 0 <= k < levels else zero

    def e_at(k):
        return face(q(k - 2), q(k - 1), q(k), q(k + 1))

    left = e_at(0)
    f_here = zero
    held = []
    right = e_at(1)
    s, kk = right - left, 6.0 * q(0) - 3.0 * (left + right)
    for k in range(levels):
        if k + 1 < levels:
            nxt = e_at(k + 2)
            s1, k1 = nxt - right, 6.0 * q(k + 1) - 3.0 * (right + nxt)
            c = jnp.where(sub, c_ref[k + 1, 0:1, :], c_ref[k + 1, 1:2, :])
            f_next = flux(c, right, s, s1, kk, k1)
            right, s, kk = nxt, s1, k1
        else:
            f_next = zero
        held.append(q(k) + f_here - f_next)
        f_here = f_next
        if k % 4 == 3:
            for rp in range(2):
                x = []
                for h in held:
                    third = h[:, 256:384]
                    if rp == 1:
                        third = pltpu.roll(third, 128 - rest, 1)
                    x.append(jnp.concatenate([h[:, 128 * rp : 128 * rp + 128], third], axis=1))
                t = [pltpu.roll(v, 4, 0) for v in x]
                first = [jnp.where(half, x[0], t[1]), jnp.where(half, x[2], t[3])]
                second = [jnp.where(half, t[0], x[1]), jnp.where(half, t[2], x[3])]
                for r2, rows in enumerate((first, second)):
                    r = 2 * rp + r2
                    hi, lo = split(jnp.concatenate(rows, axis=0))
                    at = 32 * r + 4 * (k - 3)
                    a_ref[r, at : at + 16, 0:256] = hi
                    a_ref[r, at : at + 16, 256:512] = lo
            held = []
    carried = None
    for r in range(4):
        one = selector(slot_ref, r)
        out = dot(jnp.concatenate([one, one], axis=1), a_ref[r], NT)
        for t in range(3):
            part = out[:, 128 * t : 128 * t + 128]
            if t == 0 and r > 0:
                part = part + carried
            if t == 2 and r < 3:
                carried = part
                continue
            p_ref[2 * r + t] = part.reshape(p_ref.shape[1:])
        ready(r)


def reorder_kernel(m_ref, n_ref, o_ref):
    order = m_ref.shape[0]
    levels = order // 4
    x = lax.broadcasted_iota(jnp.int32, (order, order), 0)
    o = lax.broadcasted_iota(jnp.int32, (order, order), 1)
    pick = ((x & 3) * levels + (x >> 2) == o).astype(F32).astype(BF16)
    part = order // 4
    for n, ref in enumerate((m_ref, n_ref)):
        hi, lo = split(ref[...])
        rest = (ref[...] - hi.astype(F32) - lo.astype(F32)).astype(BF16)
        out = None
        for piece in (hi, lo, rest):
            term = dot(dot(pick, piece).astype(BF16), pick, NT)
            out = term if out is None else out + term
        o_ref[n, 0:order] = out[:, 0:128]
        o_ref[n, order : 2 * order] = out[:, 128:256]
        o_ref[n, 2 * order :] = jnp.concatenate([out[part * i : part * i + part, 256:] for i in range(4)], axis=1)


def unpacked(packed):
    part = packed.shape[0] // 9
    third = packed[8 * part :]
    lanes = third.shape[1] // 4
    third = jnp.concatenate([third[:, lanes * i : lanes * i + lanes] for i in range(4)], axis=0)
    return jnp.concatenate([packed[: 4 * part], packed[4 * part : 8 * part], third], axis=1)


def unselect(rest, v_ref, slot_ref, d_ref):
    lane = lax.broadcasted_iota(jnp.int32, (128, 512), 1)
    live = (lane & 3) < 3
    turned = [jnp.where(live, v_ref[j].reshape(512, 128).T, 0.0) for j in range(9)]
    turned = jnp.concatenate(turned, axis=0)
    whole = []
    for r in range(4):
        hi, lo = split(turned[288 * r : 288 * r + 288])
        one = selector(slot_ref, r)
        whole.append(dot(jnp.concatenate([hi, lo], axis=1), jnp.concatenate([one, one], axis=0)))
    sub = lax.broadcasted_iota(jnp.int32, (8, 256), 0) < 4
    lane = lax.broadcasted_iota(jnp.int32, (8, 128), 1)
    block = d_ref.shape[1]
    for n in range(d_ref.shape[0] * block // 2):
        even, odd = [], []
        for rp in range(2):
            x = whole[2 * rp][8 * n : 8 * n + 8]
            y = whole[2 * rp + 1][8 * n : 8 * n + 8]
            even.append(jnp.where(sub, x, pltpu.roll(y, 4, 0)))
            odd.append(jnp.where(sub, pltpu.roll(x, 4, 0), y))
        for i, (a, b) in enumerate((even, odd)):
            third = jnp.where(lane < rest, a[:, 128:], pltpu.roll(b[:, 128:], rest, 1))
            d_ref[(2 * n + i) // block, (2 * n + i) % block] = jnp.concatenate([a[:, :128], b[:, :128], third], axis=1)


def assemble(lon, d_ref, o_ref):
    groups = d_ref.shape[0]
    rest = lon - 128

    def level(k, carry):
        for rp in range(2):
            parts = []
            for g in range(groups):
                x = d_ref[g, k]
                parts.append(x[:, 128 * rp : 128 * rp + 128])
                parts.append(x[:, 256 + rest * rp : 256 + rest * rp + rest])
            o_ref[rp, k] = jnp.concatenate(parts, axis=1)
        return carry

    lax.fori_loop(0, d_ref.shape[1], level, 0)


CHUNKS = 4


def greet(lat, lev, levs):
    for i in range(1, levs):
        pl.semaphore_signal(
            pltpu.get_barrier_semaphore(), inc=1, device_id=(lat, lax.rem(lev + i, levs)), device_id_type=MESH
        )


def greeted(levs):
    pl.semaphore_wait(pltpu.get_barrier_semaphore(), levs - 1)


def send(src, dst, ssem, rsem, lat, to):
    return pltpu.make_async_remote_copy(
        src_ref=src, dst_ref=dst, send_sem=ssem, recv_sem=rsem, device_id=(lat, to), device_id_type=MESH
    )


def forth_kernel(
    rest, levs, tr_ref, south_ref, north_ref, zon_ref, mer_ref, c_ref, slot_ref,
    r_ref, g_ref, col_ref, p_ref, a_ref, s1, r1, s2, r2, lsem,
):
    lat, lev = lax.axis_index("lat"), lax.axis_index("lev")
    block = tr_ref.shape[1]
    greet(lat, lev, levs)
    greeted(levs)

    def level_copy(k, i):
        to = lax.rem(lev + i, levs)
        return send(g_ref.at[to, k], col_ref.at[lev, k], s1.at[k, i], r1.at[k, i], lat, to)

    def level_ready(k):
        for i in range(1, levs):
            level_copy(k, i).start()

    horizontal(tr_ref, south_ref, north_ref, zon_ref, mer_ref, g_ref, level_ready)
    own = pltpu.make_async_copy(g_ref.at[lev], col_ref.at[lev], lsem.at[0])
    own.start()
    own.wait()

    @pl.loop(0, block)
    def _(k):
        for i in range(1, levs):
            level_copy(k, i).wait()

    def tiles(r):
        return slice(2 * r, 2 * r + (3 if r == 3 else 2))

    def row_copy(r, i):
        to = lax.rem(lev + i, levs)
        return send(p_ref.at[tiles(r), to, :, 0:3], r_ref.at[tiles(r), :, lev, 0:3], s2.at[r, i], r2.at[r, i], lat, to)

    def row_ready(r):
        for i in range(1, levs):
            row_copy(r, i).start()

    select(rest, col_ref, c_ref, slot_ref, p_ref, a_ref, row_ready)
    own = pltpu.make_async_copy(p_ref.at[:, lev, :, 0:3], r_ref.at[:, :, lev, 0:3], lsem.at[1])
    own.start()
    own.wait()
    for r in range(4):
        for i in range(1, levs):
            row_copy(r, i).wait()


def back_kernel(
    rest, levs, order, r_ref, n0, n1, n2, n3, f0, f1, f2, f3, slot_ref,
    o_ref, y_ref, v_ref, w_ref, d_ref, own_ref, s1, r1, s2, r2, lsem,
):
    lat, lev = lax.axis_index("lat"), lax.axis_index("lev")
    size = r_ref.shape[1] // CHUNKS
    greet(lat, lev, levs)

    def back_copy(d, i):
        to = lax.rem(lev + i, levs)
        part = pl.ds(lax.rem(lat // 4 - d + 4, 4) * size, size)
        return send(y_ref.at[:, part, to, 0:3], v_ref.at[:, lev, part, 0:3], s1.at[d, i], r1.at[d, i], lat, to)

    def mix(n, at):
        tiles = [r_ref[j, n].reshape(4 * levs, 128) for j in range(9)]
        rows = []
        for r in range(4):
            x = jnp.concatenate(tiles[2 * r : 2 * r + 3], axis=1)
            if r > 0:
                x = pltpu.roll(x, 384 - 32 * r, 1)
            rows.append(x[:, :order])
        hi, lo = split(jnp.concatenate(rows, axis=0))
        y = dot(hi, w_ref[0, at], NT) + dot(lo, w_ref[0, at], NT) + dot(hi, w_ref[1, at], NT)
        many = 4 * levs
        carried = None
        for r in range(4):
            x = jnp.concatenate([y[r * many : (r + 1) * many], jnp.zeros((many, 384 - order), F32)], axis=1)
            if r > 0:
                x = pltpu.roll(x, 32 * r, 1)
            for t in range(3):
                part = x[:, 128 * t : 128 * t + 128]
                if t == 0 and r > 0:
                    part = part + carried
                if t == 2 and r < 3:
                    carried = part
                    continue
                y_ref[2 * r + t, n] = part.reshape(levs, 4, 128)

    for d, refs in enumerate(((n0, f0), (n1, f1), (n2, f2), (n3, f3))):
        base = lax.rem(lat // 4 - d + 4, 4) * size
        for at in range(4):
            hi, lo = split(unpacked(refs[at % 2][at // 2]))
            w_ref[0, at] = hi
            w_ref[1, at] = lo

        @pl.loop(0, size)
        def _(at):
            mix(base + lax.rem(lat // 2 + at // 2, 2) * 2 + lax.rem(lat + at, 2), at)

        if d == 0:
            greeted(levs)
        for i in range(1, levs):
            back_copy(d, i).start()
    own = pltpu.make_async_copy(y_ref.at[:, :, lev, 0:3], v_ref.at[:, lev, :, 0:3], lsem.at[0])
    own.start()
    own.wait()
    for q in range(CHUNKS):
        for i in range(1, levs):
            back_copy(q, i).wait()

    unselect(rest, v_ref, slot_ref, d_ref)

    def level_copy(i):
        to = lax.rem(lev + i, levs)
        return send(d_ref.at[to], own_ref.at[lev], s2.at[i], r2.at[i], lat, to)

    for i in range(1, levs):
        level_copy(i).start()
    own = pltpu.make_async_copy(d_ref.at[lev], own_ref.at[lev], lsem.at[1])
    own.start()
    own.wait()
    for i in range(1, levs):
        level_copy(i).wait()
    assemble(128 + rest, own_ref, o_ref)


def call(kernel, shape, count, scratch=(), limit=48, **params):
    return pl.pallas_call(
        kernel,
        out_shape=jax.ShapeDtypeStruct(shape, F32),
        in_specs=[VMEM] * count,
        out_specs=VMEM,
        scratch_shapes=list(scratch),
        compiler_params=pltpu.CompilerParams(vmem_limit_bytes=limit << 20, **params),
    )


def body(tracers, zonal, meridional, vertical, route, inverse):
    trac, levs_here, rows, width = tracers.shape
    lats, groups = lax.axis_size("lat"), lax.axis_size("lev")
    levels, _, lon = vertical.shape
    rest = lon - 128
    order = inverse.shape[2]
    own = inverse[0, 0]
    across = lax.ppermute(own, "lat", [(i, i ^ 2) for i in range(lats)])
    turned = jnp.transpose(tracers, (2, 1, 0, 3))
    up = [(i, i + 1) for i in range(lats - 1)]
    down = [(i + 1, i) for i in range(lats - 1)]
    south = lax.ppermute(turned[rows - 3 :], "lat", up)
    edge = jnp.pad(meridional[:, 0], ((0, -levs_here % 4), (0, 0))).reshape(-1, 4, width)
    north = lax.ppermute(
        jnp.concatenate([turned[:3].reshape(3 * levs_here, trac, width), edge], axis=0), "lat", down
    )
    pair = call(reorder_kernel, (2, order * order // 128, 128), 2)(own, across)
    targets = route[:, :, 0]
    before = jnp.arange(lon)[:, None] < jnp.arange(lon)[None, :]
    same = jnp.logical_and(targets[:, :, None] == targets[:, None, :], before[None])
    place = (targets % groups) * lats + targets // groups
    slots = place * 4 + jnp.sum(same.astype(jnp.int32), axis=1)
    slots = jnp.pad(slots, ((0, 0), (0, 256 - lon)), constant_values=-1)
    v = vertical.reshape(levels, 2, 2, lon)
    courant = jnp.concatenate(
        [v[:, 0, :, :128], v[:, 1, :, :128], v[:, 0, :, 128:], v[:, 1, :, 128:], jnp.zeros((levels, 2, 128 - 2 * rest), F32)],
        axis=-1,
    )
    shifted = [lax.ppermute(pair, "lat", [(i, (i + 4 * d) % lats) for i in range(lats)]) for d in range(1, 4)]
    other = [(i, i ^ 1) for i in range(lats)]
    far = [lax.ppermute(pair, "lat", other)]
    south, north, pair = lax.optimization_barrier((south, north, pair))
    dma = pltpu.SemaphoreType.DMA
    levels_of = pltpu.VMEM((groups, levs_here, 8, 384), F32)
    received = call(
        functools.partial(forth_kernel, rest, groups),
        (9, lats, groups, 4, 128),
        7,
        [
            levels_of,
            levels_of,
            pltpu.VMEM((9, groups, lats, 4, 128), F32),
            pltpu.VMEM((4, 384, 512), BF16),
            dma((levs_here, groups)),
            dma((levs_here, groups)),
            dma((4, groups)),
            dma((4, groups)),
            dma((2,)),
        ],
        collective_id=0,
        has_side_effects=True,
    )(turned, south, north, zonal, meridional, courant, slots)
    received, shifted = lax.optimization_barrier((received, shifted))
    far += [lax.ppermute(x, "lat", other) for x in shifted]
    whole = call(
        functools.partial(back_kernel, rest, groups, order),
        (2, levs_here, 8, width),
        10,
        [
            pltpu.VMEM((9, lats, groups, 4, 128), F32),
            pltpu.VMEM((9, groups, lats, 4, 128), F32),
            pltpu.VMEM((2, lats // CHUNKS, order, order), BF16),
            levels_of,
            levels_of,
            dma((CHUNKS, groups)),
            dma((CHUNKS, groups)),
            dma((groups,)),
            dma((groups,)),
            dma((2,)),
        ],
        collective_id=1,
        has_side_effects=True,
    )(received, pair, *shifted, *far, slots)
    whole = whole.reshape(2, levs_here, 2, trac, width)
    return jnp.transpose(whole, (3, 1, 0, 2, 4)).reshape(tracers.shape) - tracers


def solution(mesh):
    in_specs = (
        P(None, "lev", "lat", None),
        P("lev", "lat", None),
        P("lev", "lat", None),
        P(None, "lat", "lev"),
        P("lat", "lev", None),
        P("lat", "lev", None, None),
    )
    out_specs = P(None, "lev", "lat", None)
    return jax.shard_map(body, mesh=mesh, in_specs=in_specs, out_specs=out_specs, check_vma=False)
```

```python
import functools
import jax
import jax.numpy as jnp
from jax import lax
from jax.experimental import pallas as pl
from jax.experimental.pallas import tpu as pltpu
from jax.sharding import PartitionSpec as P

MESH = pl.DeviceIdType.MESH
F32 = jnp.float32
BF16 = jnp.bfloat16
VMEM = pl.BlockSpec(memory_space=pltpu.VMEM)
NT = (((1,), (1,)), ((), ()))
NN = (((1,), (0,)), ((), ()))


def dot(a, b, dims=NN):
    return lax.dot_general(a, b, dims, preferred_element_type=F32)


def split(x):
    hi = x.astype(BF16)
    lo = (x - hi.astype(F32)).astype(BF16)
    return hi, lo


def flux(c, e, s_low, s_here, k_low, k_here):
    up = c >= 0.0
    a = jnp.abs(c)
    s = jnp.where(up, -s_low, s_here)
    k = jnp.where(up, k_low, k_here)
    return c * (e + (0.5 * a) * (s + (1.0 - (2.0 / 3.0) * a) * k))


def face(q_m2, q_m1, q_0, q_p1):
    return (7.0 / 12.0) * (q_m1 + q_0) - (1.0 / 12.0) * (q_m2 + q_p1)


def horizontal(tr_ref, south_ref, north_ref, zon_ref, mer_ref, g_ref, ready):
    lat = lax.axis_index("lat")
    last = lax.axis_size("lat") - 1
    width = tr_ref.shape[3]
    groups = g_ref.shape[0]
    lon = width // groups
    sub = lax.broadcasted_iota(jnp.int32, (8, width), 0) < 4
    ext = -(-width // 128) * 128
    spare = ext - width
    half = spare // 3
    ksouth = (lat > 0).astype(F32)
    knorth = (lat < last).astype(F32)

    def swap(x):
        return pltpu.roll(x, 4, 0)

    def extend(x):
        return jnp.concatenate([x, x[:, :half], x[:, width - (spare - half):]], axis=1)

    def rolled(x, n):
        return pltpu.roll(x, n % ext, 1)

    def level(k, carry):
        row = [tr_ref[r, k] for r in range(4)]
        low = [south_ref[r, k] * ksouth for r in range(3)]
        high = [north_ref[r * tr_ref.shape[1] + k] * knorth for r in range(3)]
        pair = lambda a, b: jnp.concatenate([a, b], axis=0)
        q = [
            pair(low[0], low[0]),
            pair(low[1], low[2]),
            pair(row[0], row[1]),
            pair(row[2], row[3]),
            pair(high[0], high[1]),
            pair(high[2], high[2]),
        ]
        sq = [swap(x) for x in q]
        e = [face(q[p - 1], jnp.where(sub, sq[p - 1], sq[p]), q[p], jnp.where(sub, sq[p], sq[p + 1])) for p in range(1, 5)]
        se = [swap(x) for x in e]
        s, kk = [], []
        for p in range(4):
            right = jnp.where(sub, se[p], se[min(p + 1, 3)])
            s.append(right - e[p])
            kk.append(6.0 * q[p + 1] - 3.0 * (e[p] + right))
        ss = [swap(x) for x in s]
        sk = [swap(x) for x in kk]
        m = mer_ref[k]
        zero = jnp.zeros((8, width), F32)
        m0 = jnp.where(sub, m[0:1] * ksouth, m[1:2])
        m1 = jnp.where(sub, m[2:3], m[3:4])
        m2 = north_ref[3 * tr_ref.shape[1] + k // 4, pl.ds(k % 4, 1), :] * knorth + zero
        f = []
        for i, c in enumerate((m0, m1, m2)):
            p = i + 1
            f.append(
                flux(c, e[p], jnp.where(sub, ss[p - 1], ss[p]), s[p], jnp.where(sub, sk[p - 1], sk[p]), kk[p])
            )
        sf = [swap(x) for x in f]
        z = zon_ref[k]
        out = []
        for p in range(2):
            lat_change = f[p] - jnp.where(sub, sf[p], sf[p + 1])
            x = extend(q[p + 2])
            c = extend(jnp.where(sub, z[2 * p : 2 * p + 1], z[2 * p + 1 : 2 * p + 2]))
            le = face(rolled(x, 2), rolled(x, 1), x, rolled(x, -1))
            right = rolled(le, -1)
            ls = right - le
            lk = 6.0 * x - 3.0 * (le + right)
            lf = flux(c, le, rolled(ls, 1), ls, rolled(lk, 1), lk)
            lon_change = lf - rolled(lf, -1)
            out.append(q[p + 2] + lon_change[:, :width] + lat_change)
        rest = lon - 128
        pad = jnp.zeros((8, 128 - 2 * rest), F32)
        for g in range(groups):
            o = g * lon
            g_ref[g, k] = jnp.concatenate(
                [
                    out[0][:, o : o + 128],
                    out[1][:, o : o + 128],
                    out[0][:, o + 128 : o + lon],
                    out[1][:, o + 128 : o + lon],
                    pad,
                ],
                axis=1,
            )
        ready(k)
        return carry

    lax.fori_loop(0, tr_ref.shape[1], level, 0)


def selector(slots):
    ids = lax.broadcasted_iota(jnp.int32, (512, 256), 0)
    return (ids == slots).astype(F32).astype(BF16)


def select(rest, g_ref, c_ref, slot_ref, p_ref, a_ref, ready):
    block = g_ref.shape[1]
    levels = g_ref.shape[0] * block
    sub = lax.broadcasted_iota(jnp.int32, (8, 384), 0) < 4
    half = lax.broadcasted_iota(jnp.int32, (8, 256), 0) < 4
    zero = jnp.zeros((8, 384), F32)
    for r in range(4):
        if r > 0:
            a_ref[r, 0 : 32 * r, :] = jnp.zeros((32 * r, 512), BF16)
        if r < 3:
            a_ref[r, 32 * r + 288 : 384, :] = jnp.zeros((96 - 32 * r, 512), BF16)

    def q(k):
        return g_ref[k // block, k % block] if 0 <= k < levels else zero

    def e_at(k):
        return face(q(k - 2), q(k - 1), q(k), q(k + 1))

    left = e_at(0)
    f_here = zero
    held = []
    right = e_at(1)
    s, kk = right - left, 6.0 * q(0) - 3.0 * (left + right)
    for k in range(levels):
        if k + 1 < levels:
            nxt = e_at(k + 2)
            s1, k1 = nxt - right, 6.0 * q(k + 1) - 3.0 * (right + nxt)
            v = c_ref[k + 1]
            c0 = jnp.where(sub[:, : 128 + rest], v[0:1], v[1:2])
            c1 = jnp.where(sub[:, : 128 + rest], v[2:3], v[3:4])
            c = jnp.concatenate(
                [c0[:, :128], c1[:, :128], c0[:, 128:], c1[:, 128:], zero[:, : 128 - 2 * rest]], axis=1
            )
            f_next = flux(c, right, s, s1, kk, k1)
            right, s, kk = nxt, s1, k1
        else:
            f_next = zero
        held.append(q(k) + f_here - f_next)
        f_here = f_next
        if k % 4 == 3:
            for rp in range(2):
                x = []
                for h in held:
                    third = h[:, 256:384]
                    if rp == 1:
                        third = pltpu.roll(third, 128 - rest, 1)
                    x.append(jnp.concatenate([h[:, 128 * rp : 128 * rp + 128], third], axis=1))
                t = [pltpu.roll(v, 4, 0) for v in x]
                first = [jnp.where(half, x[0], t[1]), jnp.where(half, x[2], t[3])]
                second = [jnp.where(half, t[0], x[1]), jnp.where(half, t[2], x[3])]
                for r2, rows in enumerate((first, second)):
                    r = 2 * rp + r2
                    hi, lo = split(jnp.concatenate(rows, axis=0))
                    at = 32 * r + 4 * (k - 3)
                    a_ref[r, at : at + 16, 0:256] = hi
                    a_ref[r, at : at + 16, 256:512] = lo
            held = []
    carried = None
    for r in range(4):
        one = selector(slot_ref[r : r + 1, :])
        out = dot(jnp.concatenate([one, one], axis=1), a_ref[r], NT)
        for t in range(3):
            part = out[:, 128 * t : 128 * t + 128]
            if t == 0 and r > 0:
                part = part + carried
            if t == 2 and r < 3:
                carried = part
                continue
            p_ref[2 * r + t] = part.reshape(p_ref.shape[1:])
        ready(r)


def reorder_kernel(levs, m_ref, n_ref, o_ref):
    order = m_ref.shape[0]
    levels = order // 4
    block = levels // levs
    x = lax.broadcasted_iota(jnp.int32, (order, order), 0)
    o = lax.broadcasted_iota(jnp.int32, (order, order), 1)
    pick = ((x & 3) * levels + (x >> 2) == o).astype(F32).astype(BF16)
    main = (x & 3) * levels + block * (x >> 5) + ((x >> 2) & 7)
    last = (x & 3) * levels + block * ((x - 256) >> 2) + block - 1
    put = (jnp.where(x < 256, main, last) == o).astype(F32).astype(BF16)
    part = order // 4
    for n, ref in enumerate((m_ref, n_ref)):
        hi, lo = split(ref[...])
        rest = (ref[...] - hi.astype(F32) - lo.astype(F32)).astype(BF16)
        out = None
        for piece in (hi, lo, rest):
            term = dot(dot(put, piece).astype(BF16), pick, NT)
            out = term if out is None else out + term
        o_ref[n, 0:order] = out[:, 0:128]
        o_ref[n, order : 2 * order] = out[:, 128:256]
        o_ref[n, 2 * order :] = jnp.concatenate([out[part * i : part * i + part, 256:] for i in range(4)], axis=1)


def unpacked(packed):
    part = packed.shape[0] // 9
    third = packed[8 * part :]
    lanes = third.shape[1] // 4
    third = jnp.concatenate([third[:, lanes * i : lanes * i + lanes] for i in range(4)], axis=0)
    return jnp.concatenate([packed[: 4 * part], packed[4 * part : 8 * part], third], axis=1)


def turned_tile(v_ref, j):
    live = (lax.broadcasted_iota(jnp.int32, (128, 512), 1) & 3) < 3
    return jnp.where(live, v_ref[j].reshape(512, 128).T, 0.0)


def unselect(lon, g, tile, last, slot_ref, o_ref):
    for r in range(4):
        rows = jnp.concatenate([tile[32 * r : 32 * r + 32], last[16 * g : 16 * g + 16]], axis=0)
        hi, lo = split(rows)
        one = selector(slot_ref[g, r : r + 1, :])
        out = dot(jnp.concatenate([hi, lo], axis=1), jnp.concatenate([one, one], axis=0))
        at = slice(lon * g, lon * g + lon)
        o_ref[r, 0:8, :, at] = out[0:32, :lon].reshape(8, 4, lon)
        o_ref[r, 8, :, at] = out[32 + 4 * r : 36 + 4 * r, :lon]


CHUNKS = 4


def greet(lat, lev, levs):
    for i in range(1, levs):
        pl.semaphore_signal(
            pltpu.get_barrier_semaphore(), inc=1, device_id=(lat, lax.rem(lev + i, levs)), device_id_type=MESH
        )


def greeted(levs):
    pl.semaphore_wait(pltpu.get_barrier_semaphore(), levs - 1)


def send(src, dst, ssem, rsem, lat, to):
    return pltpu.make_async_remote_copy(
        src_ref=src, dst_ref=dst, send_sem=ssem, recv_sem=rsem, device_id=(lat, to), device_id_type=MESH
    )


def forth_kernel(
    rest, levs, tr_ref, south_ref, north_ref, zon_ref, mer_ref, c_ref, slot_ref,
    r_ref, all_ref, g_ref, col_ref, p_ref, a_ref, s1, r1, s2, r2, s3, r3, lsem,
):
    lat, lev = lax.axis_index("lat"), lax.axis_index("lev")
    block = tr_ref.shape[1]
    greet(lat, lev, levs)
    greeted(levs)

    def slot_copy(i):
        to = lax.rem(lev + i, levs)
        return send(slot_ref, all_ref.at[lev], s3.at[i], r3.at[i], lat, to)

    for i in range(1, levs):
        slot_copy(i).start()
    own_slots = pltpu.make_async_copy(slot_ref, all_ref.at[lev], lsem.at[2])
    own_slots.start()

    def level_copy(k, i):
        to = lax.rem(lev + i, levs)
        return send(g_ref.at[to, k], col_ref.at[lev, k], s1.at[k, i], r1.at[k, i], lat, to)

    def level_ready(k):
        for i in range(1, levs):
            level_copy(k, i).start()

    horizontal(tr_ref, south_ref, north_ref, zon_ref, mer_ref, g_ref, level_ready)
    own = pltpu.make_async_copy(g_ref.at[lev], col_ref.at[lev], lsem.at[0])
    own.start()
    own.wait()

    @pl.loop(0, block)
    def _(k):
        for i in range(1, levs):
            level_copy(k, i).wait()

    def tiles(r):
        return slice(2 * r, 2 * r + (3 if r == 3 else 2))

    def row_copy(r, i):
        to = lax.rem(lev + i, levs)
        return send(p_ref.at[tiles(r), to, :, 0:3], r_ref.at[tiles(r), :, lev, 0:3], s2.at[r, i], r2.at[r, i], lat, to)

    def row_ready(r):
        for i in range(1, levs):
            row_copy(r, i).start()

    select(rest, col_ref, c_ref, slot_ref, p_ref, a_ref, row_ready)
    own = pltpu.make_async_copy(p_ref.at[:, lev, :, 0:3], r_ref.at[:, :, lev, 0:3], lsem.at[1])
    own.start()
    own.wait()
    for r in range(4):
        for i in range(1, levs):
            row_copy(r, i).wait()
    own_slots.wait()
    for i in range(1, levs):
        slot_copy(i).wait()


def back_kernel(
    rest, levs, order, r_ref, n0, n1, n2, n3, f0, f1, f2, f3, slot_ref,
    o_ref, y_ref, v_ref, w_ref, z_ref, s1, r1, lsem,
):
    lat, lev = lax.axis_index("lat"), lax.axis_index("lev")
    size = r_ref.shape[1] // CHUNKS
    greet(lat, lev, levs)

    def back_copy(j, i):
        to = lax.rem(lev + i, levs)
        return send(y_ref.at[j, :, to, 0:3], v_ref.at[j, lev, :, 0:3], s1.at[j, i], r1.at[j, i], lat, to)

    def mix(n, at):
        tiles = [r_ref[j, n].reshape(4 * levs, 128) for j in range(9)]
        rows = []
        for r in range(4):
            x = jnp.concatenate(tiles[2 * r : 2 * r + 3], axis=1)
            if r > 0:
                x = pltpu.roll(x, 384 - 32 * r, 1)
            rows.append(x[:, :order])
        hi, lo = split(jnp.concatenate(rows, axis=0))
        y = dot(hi, w_ref[0, at], NT) + dot(lo, w_ref[0, at], NT) + dot(hi, w_ref[1, at], NT)
        many = 4 * levs
        quarter = lax.broadcasted_iota(jnp.int32, (many, 128), 1) >> 5
        for half in range(2):
            turns = []
            for r in range(4):
                tile = y[r * many : (r + 1) * many, 128 * half : 128 * half + 128]
                turns.append([tile] + [pltpu.roll(tile, 32 * m, 1) for m in range(1, 4)])
            for m in range(4):
                x = turns[3][(3 - m) % 4]
                for r in range(3):
                    x = jnp.where(quarter == r, turns[r][(r - m) % 4], x)
                y_ref[pl.ds(0, 8), n, 4 * half + m] = x.reshape(8, 4, 128)
        z = jnp.concatenate([y[r * many : (r + 1) * many, 256:] for r in range(4)], axis=1)
        z_ref[:, n] = z.reshape(8, 4, 128)

    for d, refs in enumerate(((n0, f0), (n1, f1), (n2, f2), (n3, f3))):
        base = lax.rem(lat // 4 - d + 4, 4) * size
        for at in range(4):
            hi, lo = split(unpacked(refs[at % 2][at // 2]))
            w_ref[0, at] = hi
            w_ref[1, at] = lo

        @pl.loop(0, size)
        def _(at):
            mix(base + lax.rem(lat // 2 + at // 2, 2) * 2 + lax.rem(lat + at, 2), at)

    lats = r_ref.shape[1]
    to_lane = lax.broadcasted_iota(jnp.int32, (256, 1024), 1)
    from_lane = lax.broadcasted_iota(jnp.int32, (256, 1024), 0) & 127
    wanted = ((to_lane >> 2) & 3) * 32 + (to_lane >> 7) * 4 + (to_lane & 3)
    move = (from_lane == wanted).astype(F32).astype(BF16)
    hi, lo = split(z_ref[...].reshape(8 * 4 * lats, 128))
    moved = dot(jnp.concatenate([hi, lo], axis=1), move)
    group = (lax.broadcasted_iota(jnp.int32, (4 * lats, 1024), 1) >> 4) & 7
    x = moved[: 4 * lats]
    for g in range(1, 8):
        x = jnp.where(group == g, moved[4 * lats * g : 4 * lats * (g + 1)], x)
    for l in range(8):
        y_ref[8, :, l] = x[:, 128 * l : 128 * l + 128].reshape(lats, 4, 128)

    own = pltpu.make_async_copy(y_ref.at[:, :, lev, 0:3], v_ref.at[:, lev, :, 0:3], lsem.at[0])
    own.start()
    greeted(levs)
    arrivals = [8] + list(range(8))
    for j in arrivals:
        for i in range(1, levs):
            back_copy(j, i).start()
    own.wait()
    last = None
    for j in arrivals:
        for i in range(1, levs):
            back_copy(j, i).wait()
        tile = turned_tile(v_ref, j)
        if j == 8:
            last = tile
        else:
            unselect(128 + rest, j, tile, last, slot_ref, o_ref)


def call(kernel, shape, count, scratch=(), limit=48, extra=None, **params):
    return pl.pallas_call(
        kernel,
        out_shape=jax.ShapeDtypeStruct(shape, F32) if extra is None else (jax.ShapeDtypeStruct(shape, F32), extra),
        in_specs=[VMEM] * count,
        out_specs=VMEM if extra is None else (VMEM, VMEM),
        scratch_shapes=list(scratch),
        compiler_params=pltpu.CompilerParams(vmem_limit_bytes=limit << 20, **params),
    )


def body(tracers, zonal, meridional, vertical, route, inverse):
    trac, levs_here, rows, width = tracers.shape
    lats, groups = lax.axis_size("lat"), lax.axis_size("lev")
    levels, _, lon = vertical.shape
    rest = lon - 128
    order = inverse.shape[2]
    own = inverse[0, 0]
    across = lax.ppermute(own, "lat", [(i, i ^ 2) for i in range(lats)])
    turned = jnp.transpose(tracers, (2, 1, 0, 3))
    up = [(i, i + 1) for i in range(lats - 1)]
    down = [(i + 1, i) for i in range(lats - 1)]
    south = lax.ppermute(turned[rows - 3 :], "lat", up)
    edge = jnp.pad(meridional[:, 0], ((0, -levs_here % 4), (0, 0))).reshape(-1, 4, width)
    north = lax.ppermute(
        jnp.concatenate([turned[:3].reshape(3 * levs_here, trac, width), edge], axis=0), "lat", down
    )
    pair = call(functools.partial(reorder_kernel, groups), (2, order * order // 128, 128), 2)(own, across)
    targets = route[:, :, 0]
    before = jnp.arange(lon)[:, None] < jnp.arange(lon)[None, :]
    same = jnp.logical_and(targets[:, :, None] == targets[:, None, :], before[None])
    place = (targets % groups) * lats + targets // groups
    slots = place * 4 + jnp.sum(same.astype(jnp.int32), axis=1)
    slots = jnp.pad(slots, ((0, 0), (0, 256 - lon)), constant_values=-1)
    shifted = [lax.ppermute(pair, "lat", [(i, (i + 4 * d) % lats) for i in range(lats)]) for d in range(1, 4)]
    other = [(i, i ^ 1) for i in range(lats)]
    far = [lax.ppermute(pair, "lat", other)]
    south, north, pair = lax.optimization_barrier((south, north, pair))
    dma = pltpu.SemaphoreType.DMA
    levels_of = pltpu.VMEM((groups, levs_here, 8, 384), F32)
    received, all_slots = call(
        functools.partial(forth_kernel, rest, groups),
        (9, lats, groups, 4, 128),
        7,
        [
            levels_of,
            levels_of,
            pltpu.VMEM((9, groups, lats, 4, 128), F32),
            pltpu.VMEM((4, 384, 512), BF16),
            dma((levs_here, groups)),
            dma((levs_here, groups)),
            dma((4, groups)),
            dma((4, groups)),
            dma((groups,)),
            dma((groups,)),
            dma((3,)),
        ],
        extra=jax.ShapeDtypeStruct((groups, 4, 256), jnp.int32),
        collective_id=0,
        has_side_effects=True,
    )(turned, south, north, zonal, meridional, vertical, slots)
    received, shifted = lax.optimization_barrier((received, shifted))
    far += [lax.ppermute(x, "lat", other) for x in shifted]
    whole = call(
        functools.partial(back_kernel, rest, groups, order),
        (4, levs_here, trac, width),
        10,
        [
            pltpu.VMEM((9, lats, groups, 4, 128), F32),
            pltpu.VMEM((9, groups, lats, 4, 128), F32),
            pltpu.VMEM((2, lats // CHUNKS, order, order), BF16),
            pltpu.VMEM((groups, lats, 4, 128), F32),
            dma((9, groups)),
            dma((9, groups)),
            dma((1,)),
        ],
        collective_id=1,
        has_side_effects=True,
    )(received, pair, *shifted, *far, all_slots)
    return jnp.transpose(whole, (2, 1, 0, 3)) - tracers


def solution(mesh):
    in_specs = (
        P(None, "lev", "lat", None),
        P("lev", "lat", None),
        P("lev", "lat", None),
        P(None, "lat", "lev"),
        P("lat", "lev", None),
        P("lat", "lev", None, None),
    )
    out_specs = P(None, "lev", "lat", None)
    return jax.shard_map(body, mesh=mesh, in_specs=in_specs, out_specs=out_specs, check_vma=False)
```

```python
import functools
import jax
import jax.numpy as jnp
from jax import lax
from jax.experimental import pallas as pl
from jax.experimental.pallas import tpu as pltpu
from jax.sharding import PartitionSpec as P

MESH = pl.DeviceIdType.MESH
F32 = jnp.float32
BF16 = jnp.bfloat16
VMEM = pl.BlockSpec(memory_space=pltpu.VMEM)
NT = (((1,), (1,)), ((), ()))
NN = (((1,), (0,)), ((), ()))


def dot(a, b, dims=NN):
    return lax.dot_general(a, b, dims, preferred_element_type=F32)


def split(x):
    hi = x.astype(BF16)
    lo = (x - hi.astype(F32)).astype(BF16)
    return hi, lo


def flux(c, e, s_low, s_here, k_low, k_here):
    up = c >= 0.0
    a = jnp.abs(c)
    s = jnp.where(up, -s_low, s_here)
    k = jnp.where(up, k_low, k_here)
    return c * (e + (0.5 * a) * (s + (1.0 - (2.0 / 3.0) * a) * k))


def face(q_m2, q_m1, q_0, q_p1):
    return (7.0 / 12.0) * (q_m1 + q_0) - (1.0 / 12.0) * (q_m2 + q_p1)


def horizontal(tr_ref, south_ref, north_ref, zon_ref, mer_ref, g_ref, ready):
    lat = lax.axis_index("lat")
    last = lax.axis_size("lat") - 1
    width = tr_ref.shape[3]
    groups = g_ref.shape[0]
    lon = width // groups
    sub = lax.broadcasted_iota(jnp.int32, (8, width), 0) < 4
    ext = -(-width // 128) * 128
    spare = ext - width
    half = spare // 3
    ksouth = (lat > 0).astype(F32)
    knorth = (lat < last).astype(F32)

    def swap(x):
        return pltpu.roll(x, 4, 0)

    def extend(x):
        return jnp.concatenate([x, x[:, :half], x[:, width - (spare - half):]], axis=1)

    def rolled(x, n):
        return pltpu.roll(x, n % ext, 1)

    def level(k, carry):
        row = [tr_ref[r, k] for r in range(4)]
        low = [south_ref[r, k] * ksouth for r in range(3)]
        high = [north_ref[r * tr_ref.shape[1] + k] * knorth for r in range(3)]
        pair = lambda a, b: jnp.concatenate([a, b], axis=0)
        q = [
            pair(low[0], low[0]),
            pair(low[1], low[2]),
            pair(row[0], row[1]),
            pair(row[2], row[3]),
            pair(high[0], high[1]),
            pair(high[2], high[2]),
        ]
        sq = [swap(x) for x in q]
        e = [face(q[p - 1], jnp.where(sub, sq[p - 1], sq[p]), q[p], jnp.where(sub, sq[p], sq[p + 1])) for p in range(1, 5)]
        se = [swap(x) for x in e]
        s, kk = [], []
        for p in range(4):
            right = jnp.where(sub, se[p], se[min(p + 1, 3)])
            s.append(right - e[p])
            kk.append(6.0 * q[p + 1] - 3.0 * (e[p] + right))
        ss = [swap(x) for x in s]
        sk = [swap(x) for x in kk]
        m = mer_ref[k]
        zero = jnp.zeros((8, width), F32)
        m0 = jnp.where(sub, m[0:1] * ksouth, m[1:2])
        m1 = jnp.where(sub, m[2:3], m[3:4])
        m2 = north_ref[3 * tr_ref.shape[1] + k // 4, pl.ds(k % 4, 1), :] * knorth + zero
        f = []
        for i, c in enumerate((m0, m1, m2)):
            p = i + 1
            f.append(
                flux(c, e[p], jnp.where(sub, ss[p - 1], ss[p]), s[p], jnp.where(sub, sk[p - 1], sk[p]), kk[p])
            )
        sf = [swap(x) for x in f]
        z = zon_ref[k]
        out = []
        for p in range(2):
            lat_change = f[p] - jnp.where(sub, sf[p], sf[p + 1])
            x = extend(q[p + 2])
            c = extend(jnp.where(sub, z[2 * p : 2 * p + 1], z[2 * p + 1 : 2 * p + 2]))
            le = face(rolled(x, 2), rolled(x, 1), x, rolled(x, -1))
            right = rolled(le, -1)
            ls = right - le
            lk = 6.0 * x - 3.0 * (le + right)
            lf = flux(c, le, rolled(ls, 1), ls, rolled(lk, 1), lk)
            lon_change = lf - rolled(lf, -1)
            out.append(q[p + 2] + lon_change[:, :width] + lat_change)
        rest = lon - 128
        pad = jnp.zeros((8, 128 - 2 * rest), F32)
        for g in range(groups):
            o = g * lon
            g_ref[g, k] = jnp.concatenate(
                [
                    out[0][:, o : o + 128],
                    out[1][:, o : o + 128],
                    out[0][:, o + 128 : o + lon],
                    out[1][:, o + 128 : o + lon],
                    pad,
                ],
                axis=1,
            )
        ready(k)
        return carry

    lax.fori_loop(0, tr_ref.shape[1], level, 0)


def selector(slots):
    ids = lax.broadcasted_iota(jnp.int32, (512, 256), 0)
    return (ids == slots).astype(F32).astype(BF16)


def select(rest, g_ref, c_ref, slot_ref, p_ref, a_ref, ready):
    block = g_ref.shape[1]
    levels = g_ref.shape[0] * block
    sub = lax.broadcasted_iota(jnp.int32, (8, 384), 0) < 4
    half = lax.broadcasted_iota(jnp.int32, (8, 256), 0) < 4
    zero = jnp.zeros((8, 384), F32)
    for r in range(4):
        if r > 0:
            a_ref[r, 0 : 32 * r, :] = jnp.zeros((32 * r, 512), BF16)
        if r < 3:
            a_ref[r, 32 * r + 288 : 384, :] = jnp.zeros((96 - 32 * r, 512), BF16)

    def q(k):
        return g_ref[k // block, k % block] if 0 <= k < levels else zero

    def e_at(k):
        return face(q(k - 2), q(k - 1), q(k), q(k + 1))

    left = e_at(0)
    f_here = zero
    held = []
    right = e_at(1)
    s, kk = right - left, 6.0 * q(0) - 3.0 * (left + right)
    for k in range(levels):
        if k + 1 < levels:
            nxt = e_at(k + 2)
            s1, k1 = nxt - right, 6.0 * q(k + 1) - 3.0 * (right + nxt)
            c = jnp.where(sub, c_ref[k + 1, 0:1, :], c_ref[k + 1, 1:2, :])
            f_next = flux(c, right, s, s1, kk, k1)
            right, s, kk = nxt, s1, k1
        else:
            f_next = zero
        held.append(q(k) + f_here - f_next)
        f_here = f_next
        if k % 4 == 3:
            for rp in range(2):
                x = []
                for h in held:
                    third = h[:, 256:384]
                    if rp == 1:
                        third = pltpu.roll(third, 128 - rest, 1)
                    x.append(jnp.concatenate([h[:, 128 * rp : 128 * rp + 128], third], axis=1))
                t = [pltpu.roll(v, 4, 0) for v in x]
                first = [jnp.where(half, x[0], t[1]), jnp.where(half, x[2], t[3])]
                second = [jnp.where(half, t[0], x[1]), jnp.where(half, t[2], x[3])]
                for r2, rows in enumerate((first, second)):
                    r = 2 * rp + r2
                    hi, lo = split(jnp.concatenate(rows, axis=0))
                    at = 32 * r + 4 * (k - 3)
                    a_ref[r, at : at + 16, 0:256] = hi
                    a_ref[r, at : at + 16, 256:512] = lo
            held = []
    carried = None
    for r in range(4):
        one = selector(slot_ref[r : r + 1, :])
        out = dot(jnp.concatenate([one, one], axis=1), a_ref[r], NT)
        for t in range(3):
            part = out[:, 128 * t : 128 * t + 128]
            if t == 0 and r > 0:
                part = part + carried
            if t == 2 and r < 3:
                carried = part
                continue
            p_ref[2 * r + t] = part.reshape(p_ref.shape[1:])
        ready(r)


def reorder_kernel(levs, m_ref, n_ref, o_ref):
    order = m_ref.shape[0]
    levels = order // 4
    block = levels // levs
    x = lax.broadcasted_iota(jnp.int32, (order, order), 0)
    o = lax.broadcasted_iota(jnp.int32, (order, order), 1)
    pick = ((x & 3) * levels + (x >> 2) == o).astype(F32).astype(BF16)
    main = (x & 3) * levels + block * (x >> 5) + ((x >> 2) & 7)
    last = (x & 3) * levels + block * ((x - 256) >> 2) + block - 1
    put = (jnp.where(x < 256, main, last) == o).astype(F32).astype(BF16)
    part = order // 4
    for n, ref in enumerate((m_ref, n_ref)):
        hi, lo = split(ref[...])
        rest = (ref[...] - hi.astype(F32) - lo.astype(F32)).astype(BF16)
        out = None
        for piece in (hi, lo, rest):
            term = dot(dot(put, piece).astype(BF16), pick, NT)
            out = term if out is None else out + term
        o_ref[n, 0:order] = out[:, 0:128]
        o_ref[n, order : 2 * order] = out[:, 128:256]
        o_ref[n, 2 * order :] = jnp.concatenate([out[part * i : part * i + part, 256:] for i in range(4)], axis=1)


def unpacked(packed):
    part = packed.shape[0] // 9
    third = packed[8 * part :]
    lanes = third.shape[1] // 4
    third = jnp.concatenate([third[:, lanes * i : lanes * i + lanes] for i in range(4)], axis=0)
    return jnp.concatenate([packed[: 4 * part], packed[4 * part : 8 * part], third], axis=1)


def turned_tile(v_ref, j):
    live = (lax.broadcasted_iota(jnp.int32, (128, 512), 1) & 3) < 3
    return jnp.where(live, v_ref[j].reshape(512, 128).T, 0.0)


def unselect(lon, g, tile, last, slot_ref, o_ref):
    for r in range(4):
        rows = jnp.concatenate([tile[32 * r : 32 * r + 32], last[16 * g : 16 * g + 16]], axis=0)
        hi, lo = split(rows)
        one = selector(slot_ref[g, r : r + 1, :])
        out = dot(jnp.concatenate([hi, lo], axis=1), jnp.concatenate([one, one], axis=0))
        at = slice(lon * g, lon * g + lon)
        o_ref[r, 0:8, :, at] = out[0:32, :lon].reshape(8, 4, lon)
        o_ref[r, 8, :, at] = out[32 + 4 * r : 36 + 4 * r, :lon]


CHUNKS = 4


def greet(lat, lev, levs):
    for i in range(1, levs):
        pl.semaphore_signal(
            pltpu.get_barrier_semaphore(), inc=1, device_id=(lat, lax.rem(lev + i, levs)), device_id_type=MESH
        )


def greeted(levs):
    pl.semaphore_wait(pltpu.get_barrier_semaphore(), levs - 1)


def send(src, dst, ssem, rsem, lat, to):
    return pltpu.make_async_remote_copy(
        src_ref=src, dst_ref=dst, send_sem=ssem, recv_sem=rsem, device_id=(lat, to), device_id_type=MESH
    )


def forth_kernel(
    rest, levs, tr_ref, south_ref, north_ref, zon_ref, mer_ref, c_ref, slot_ref,
    r_ref, all_ref, g_ref, col_ref, p_ref, a_ref, s1, r1, s2, r2, s3, r3, lsem,
):
    lat, lev = lax.axis_index("lat"), lax.axis_index("lev")
    block = tr_ref.shape[1]
    greet(lat, lev, levs)
    greeted(levs)

    def slot_copy(i):
        to = lax.rem(lev + i, levs)
        return send(slot_ref, all_ref.at[lev], s3.at[i], r3.at[i], lat, to)

    for i in range(1, levs):
        slot_copy(i).start()
    own_slots = pltpu.make_async_copy(slot_ref, all_ref.at[lev], lsem.at[2])
    own_slots.start()

    def level_copy(k, i):
        to = lax.rem(lev + i, levs)
        return send(g_ref.at[to, k], col_ref.at[lev, k], s1.at[k, i], r1.at[k, i], lat, to)

    def level_ready(k):
        for i in range(1, levs):
            level_copy(k, i).start()

    horizontal(tr_ref, south_ref, north_ref, zon_ref, mer_ref, g_ref, level_ready)
    own = pltpu.make_async_copy(g_ref.at[lev], col_ref.at[lev], lsem.at[0])
    own.start()
    own.wait()

    @pl.loop(0, block)
    def _(k):
        for i in range(1, levs):
            level_copy(k, i).wait()

    def tiles(r):
        return slice(2 * r, 2 * r + (3 if r == 3 else 2))

    def row_copy(r, i):
        to = lax.rem(lev + i, levs)
        return send(p_ref.at[tiles(r), to, :, 0:3], r_ref.at[tiles(r), :, lev, 0:3], s2.at[r, i], r2.at[r, i], lat, to)

    def row_ready(r):
        for i in range(1, levs):
            row_copy(r, i).start()

    select(rest, col_ref, c_ref, slot_ref, p_ref, a_ref, row_ready)
    own = pltpu.make_async_copy(p_ref.at[:, lev, :, 0:3], r_ref.at[:, :, lev, 0:3], lsem.at[1])
    own.start()
    own.wait()
    for r in range(4):
        for i in range(1, levs):
            row_copy(r, i).wait()
    own_slots.wait()
    for i in range(1, levs):
        slot_copy(i).wait()


def back_kernel(
    rest, levs, order, r_ref, n0, n1, n2, n3, f0, f1, f2, f3, slot_ref,
    o_ref, y_ref, v_ref, w_ref, z_ref, m_ref, move_ref, s1, r1, s2, r2, lsem, msem,
):
    lat, lev = lax.axis_index("lat"), lax.axis_index("lev")
    size = r_ref.shape[1] // CHUNKS
    greet(lat, lev, levs)

    fetches = []
    for n, ref in enumerate((n0, f0, n1, f1, n2, f2, n3, f3)):
        fetches.append(pltpu.make_async_copy(ref, m_ref.at[n], msem.at[n]))
        fetches[n].start()

    def base(d):
        return lax.rem(lat // 4 - d + 4, 4) * size

    def chunk_copy(d, i):
        to = lax.rem(lev + i, levs)
        part = pl.ds(base(d), size)
        return send(y_ref.at[:, part, to, 0:3], v_ref.at[:, lev, part, 0:3], s1.at[d, i], r1.at[d, i], lat, to)

    def tile_copy(j, i):
        to = lax.rem(lev + i, levs)
        part = pl.ds(base(CHUNKS - 1), size)
        return send(y_ref.at[j, part, to, 0:3], v_ref.at[j, lev, part, 0:3], s2.at[j, i], r2.at[j, i], lat, to)

    def own_copy(d):
        part = pl.ds(base(d), size)
        return pltpu.make_async_copy(y_ref.at[:, part, lev, 0:3], v_ref.at[:, lev, part, 0:3], lsem.at[d])

    to_lane = lax.broadcasted_iota(jnp.int32, (256, 1024), 1)
    from_lane = lax.broadcasted_iota(jnp.int32, (256, 1024), 0) & 127
    wanted = ((to_lane >> 2) & 3) * 32 + (to_lane >> 7) * 4 + (to_lane & 3)
    move_ref[...] = (from_lane == wanted).astype(F32).astype(BF16)

    def place_last(d):
        many = 4 * size
        hi, lo = split(z_ref[:, pl.ds(base(d), size)].reshape(8 * many, 128))
        moved = dot(jnp.concatenate([hi, lo], axis=1), move_ref[...])
        group = (lax.broadcasted_iota(jnp.int32, (many, 1024), 1) >> 4) & 7
        x = moved[:many]
        for g in range(1, 8):
            x = jnp.where(group == g, moved[many * g : many * (g + 1)], x)
        for l in range(8):
            y_ref[8, pl.ds(base(d), size), l] = x[:, 128 * l : 128 * l + 128].reshape(size, 4, 128)

    def mix(n, at):
        tiles = [r_ref[j, n].reshape(4 * levs, 128) for j in range(9)]
        rows = []
        for r in range(4):
            x = jnp.concatenate(tiles[2 * r : 2 * r + 3], axis=1)
            if r > 0:
                x = pltpu.roll(x, 384 - 32 * r, 1)
            rows.append(x[:, :order])
        hi, lo = split(jnp.concatenate(rows, axis=0))
        y = dot(hi, w_ref[0, at], NT) + dot(lo, w_ref[0, at], NT) + dot(hi, w_ref[1, at], NT)
        many = 4 * levs
        quarter = lax.broadcasted_iota(jnp.int32, (many, 128), 1) >> 5
        for half in range(2):
            turns = []
            for r in range(4):
                tile = y[r * many : (r + 1) * many, 128 * half : 128 * half + 128]
                turns.append([tile] + [pltpu.roll(tile, 32 * m, 1) for m in range(1, 4)])
            for m in range(4):
                x = turns[3][(3 - m) % 4]
                for r in range(3):
                    x = jnp.where(quarter == r, turns[r][(r - m) % 4], x)
                y_ref[pl.ds(0, 8), n, 4 * half + m] = x.reshape(8, 4, 128)
        z = jnp.concatenate([y[r * many : (r + 1) * many, 256:] for r in range(4)], axis=1)
        z_ref[:, n] = z.reshape(8, 4, 128)

    arrivals = [8] + list(range(8))
    for d in range(CHUNKS):
        fetches[2 * d].wait()
        fetches[2 * d + 1].wait()
        for at in range(4):
            hi, lo = split(unpacked(m_ref[2 * d + at % 2, at // 2]))
            w_ref[0, at] = hi
            w_ref[1, at] = lo

        @pl.loop(0, size)
        def _(at):
            mix(base(d) + lax.rem(lat // 2 + at // 2, 2) * 2 + lax.rem(lat + at, 2), at)

        place_last(d)
        own_copy(d).start()
        if d == 0:
            greeted(levs)
        if d < CHUNKS - 1:
            for i in range(1, levs):
                chunk_copy(d, i).start()
        else:
            for j in arrivals:
                for i in range(1, levs):
                    tile_copy(j, i).start()

    for d in range(CHUNKS):
        own_copy(d).wait()
    for d in range(CHUNKS - 1):
        for i in range(1, levs):
            chunk_copy(d, i).wait()
    last = None
    for j in arrivals:
        for i in range(1, levs):
            tile_copy(j, i).wait()
        tile = turned_tile(v_ref, j)
        if j == 8:
            last = tile
        else:
            unselect(128 + rest, j, tile, last, slot_ref, o_ref)


def call(kernel, shape, count, scratch=(), limit=48, extra=None, large=(), **params):
    return pl.pallas_call(
        kernel,
        out_shape=jax.ShapeDtypeStruct(shape, F32) if extra is None else (jax.ShapeDtypeStruct(shape, F32), extra),
        in_specs=[pl.BlockSpec(memory_space=pl.ANY) if n in large else VMEM for n in range(count)],
        out_specs=VMEM if extra is None else (VMEM, VMEM),
        scratch_shapes=list(scratch),
        compiler_params=pltpu.CompilerParams(vmem_limit_bytes=limit << 20, **params),
    )


def body(tracers, zonal, meridional, vertical, route, inverse):
    trac, levs_here, rows, width = tracers.shape
    lats, groups = lax.axis_size("lat"), lax.axis_size("lev")
    levels, _, lon = vertical.shape
    rest = lon - 128
    order = inverse.shape[2]
    own = inverse[0, 0]
    across = lax.ppermute(own, "lat", [(i, i ^ 2) for i in range(lats)])
    turned = jnp.transpose(tracers, (2, 1, 0, 3))
    up = [(i, i + 1) for i in range(lats - 1)]
    down = [(i + 1, i) for i in range(lats - 1)]
    south = lax.ppermute(turned[rows - 3 :], "lat", up)
    edge = jnp.pad(meridional[:, 0], ((0, -levs_here % 4), (0, 0))).reshape(-1, 4, width)
    north = lax.ppermute(
        jnp.concatenate([turned[:3].reshape(3 * levs_here, trac, width), edge], axis=0), "lat", down
    )
    pair = call(functools.partial(reorder_kernel, groups), (2, order * order // 128, 128), 2)(own, across)
    targets = route[:, :, 0]
    before = jnp.arange(lon)[:, None] < jnp.arange(lon)[None, :]
    same = jnp.logical_and(targets[:, :, None] == targets[:, None, :], before[None])
    place = (targets % groups) * lats + targets // groups
    slots = place * 4 + jnp.sum(same.astype(jnp.int32), axis=1)
    slots = jnp.pad(slots, ((0, 0), (0, 256 - lon)), constant_values=-1)
    v = vertical.reshape(levels, 2, 2, lon)
    courant = jnp.concatenate(
        [v[:, 0, :, :128], v[:, 1, :, :128], v[:, 0, :, 128:], v[:, 1, :, 128:], jnp.zeros((levels, 2, 128 - 2 * rest), F32)],
        axis=-1,
    )
    shifted = [lax.ppermute(pair, "lat", [(i, (i + 4 * d) % lats) for i in range(lats)]) for d in range(1, 4)]
    other = [(i, i ^ 1) for i in range(lats)]
    dma = pltpu.SemaphoreType.DMA
    levels_of = pltpu.VMEM((groups, levs_here, 8, 384), F32)
    received, all_slots = call(
        functools.partial(forth_kernel, rest, groups),
        (9, lats, groups, 4, 128),
        7,
        [
            levels_of,
            levels_of,
            pltpu.VMEM((9, groups, lats, 4, 128), F32),
            pltpu.VMEM((4, 384, 512), BF16),
            dma((levs_here, groups)),
            dma((levs_here, groups)),
            dma((4, groups)),
            dma((4, groups)),
            dma((groups,)),
            dma((groups,)),
            dma((3,)),
        ],
        extra=jax.ShapeDtypeStruct((groups, 4, 256), jnp.int32),
        collective_id=0,
        has_side_effects=True,
    )(turned, south, north, zonal, meridional, courant, slots)
    received, pair, shifted = lax.optimization_barrier((received, pair, shifted))
    far = [lax.ppermute(x, "lat", other) for x in [pair] + shifted]
    whole = call(
        functools.partial(back_kernel, rest, groups, order),
        (4, levs_here, trac, width),
        10,
        [
            pltpu.VMEM((9, lats, groups, 4, 128), F32),
            pltpu.VMEM((9, groups, lats, 4, 128), F32),
            pltpu.VMEM((2, lats // CHUNKS, order, order), BF16),
            pltpu.VMEM((groups, lats, 4, 128), F32),
            pltpu.VMEM((8,) + pair.shape, F32),
            pltpu.VMEM((256, 1024), BF16),
            dma((CHUNKS - 1, groups)),
            dma((CHUNKS - 1, groups)),
            dma((9, groups)),
            dma((9, groups)),
            dma((CHUNKS,)),
            dma((8,)),
        ],
        large=range(1, 9),
        collective_id=1,
        has_side_effects=True,
    )(received, pair, *shifted, *far, all_slots)
    return jnp.transpose(whole, (2, 1, 0, 3)) - tracers


def solution(mesh):
    in_specs = (
        P(None, "lev", "lat", None),
        P("lev", "lat", None),
        P("lev", "lat", None),
        P(None, "lat", "lev"),
        P("lat", "lev", None),
        P("lat", "lev", None, None),
    )
    out_specs = P(None, "lev", "lat", None)
    return jax.shard_map(body, mesh=mesh, in_specs=in_specs, out_specs=out_specs, check_vma=False)
```

```python
import functools
import jax
import jax.numpy as jnp
from jax import lax
from jax.experimental import pallas as pl
from jax.experimental.pallas import tpu as pltpu
from jax.sharding import PartitionSpec as P

MESH = pl.DeviceIdType.MESH
F32 = jnp.float32
BF16 = jnp.bfloat16
VMEM = pl.BlockSpec(memory_space=pltpu.VMEM)
NT = (((1,), (1,)), ((), ()))
NN = (((1,), (0,)), ((), ()))


def dot(a, b, dims=NN):
    return lax.dot_general(a, b, dims, preferred_element_type=F32)


def split(x):
    hi = x.astype(BF16)
    lo = (x - hi.astype(F32)).astype(BF16)
    return hi, lo


def flux(c, e, s_low, s_here, k_low, k_here):
    up = c >= 0.0
    a = jnp.abs(c)
    s = jnp.where(up, -s_low, s_here)
    k = jnp.where(up, k_low, k_here)
    return c * (e + (0.5 * a) * (s + (1.0 - (2.0 / 3.0) * a) * k))


def face(q_m2, q_m1, q_0, q_p1):
    return (7.0 / 12.0) * (q_m1 + q_0) - (1.0 / 12.0) * (q_m2 + q_p1)


def horizontal(tr_ref, south_ref, north_ref, zon_ref, mer_ref, g_ref, ready):
    lat = lax.axis_index("lat")
    last = lax.axis_size("lat") - 1
    width = tr_ref.shape[3]
    groups = g_ref.shape[0]
    lon = width // groups
    sub = lax.broadcasted_iota(jnp.int32, (8, width), 0) < 4
    ext = -(-width // 128) * 128
    spare = ext - width
    half = spare // 3
    ksouth = (lat > 0).astype(F32)
    knorth = (lat < last).astype(F32)

    def swap(x):
        return pltpu.roll(x, 4, 0)

    def extend(x):
        return jnp.concatenate([x, x[:, :half], x[:, width - (spare - half):]], axis=1)

    def rolled(x, n):
        return pltpu.roll(x, n % ext, 1)

    def level(k, carry):
        row = [tr_ref[r, k] for r in range(4)]
        low = [south_ref[r, k] * ksouth for r in range(3)]
        high = [north_ref[r * tr_ref.shape[1] + k] * knorth for r in range(3)]
        pair = lambda a, b: jnp.concatenate([a, b], axis=0)
        q = [
            pair(low[0], low[0]),
            pair(low[1], low[2]),
            pair(row[0], row[1]),
            pair(row[2], row[3]),
            pair(high[0], high[1]),
            pair(high[2], high[2]),
        ]
        sq = [swap(x) for x in q]
        e = [face(q[p - 1], jnp.where(sub, sq[p - 1], sq[p]), q[p], jnp.where(sub, sq[p], sq[p + 1])) for p in range(1, 5)]
        se = [swap(x) for x in e]
        s, kk = [], []
        for p in range(4):
            right = jnp.where(sub, se[p], se[min(p + 1, 3)])
            s.append(right - e[p])
            kk.append(6.0 * q[p + 1] - 3.0 * (e[p] + right))
        ss = [swap(x) for x in s]
        sk = [swap(x) for x in kk]
        m = mer_ref[k]
        zero = jnp.zeros((8, width), F32)
        m0 = jnp.where(sub, m[0:1] * ksouth, m[1:2])
        m1 = jnp.where(sub, m[2:3], m[3:4])
        m2 = north_ref[3 * tr_ref.shape[1] + k // 4, pl.ds(k % 4, 1), :] * knorth + zero
        f = []
        for i, c in enumerate((m0, m1, m2)):
            p = i + 1
            f.append(
                flux(c, e[p], jnp.where(sub, ss[p - 1], ss[p]), s[p], jnp.where(sub, sk[p - 1], sk[p]), kk[p])
            )
        sf = [swap(x) for x in f]
        z = zon_ref[k]
        out = []
        for p in range(2):
            lat_change = f[p] - jnp.where(sub, sf[p], sf[p + 1])
            x = extend(q[p + 2])
            c = extend(jnp.where(sub, z[2 * p : 2 * p + 1], z[2 * p + 1 : 2 * p + 2]))
            le = face(rolled(x, 2), rolled(x, 1), x, rolled(x, -1))
            right = rolled(le, -1)
            ls = right - le
            lk = 6.0 * x - 3.0 * (le + right)
            lf = flux(c, le, rolled(ls, 1), ls, rolled(lk, 1), lk)
            lon_change = lf - rolled(lf, -1)
            out.append(q[p + 2] + lon_change[:, :width] + lat_change)
        rest = lon - 128
        pad = jnp.zeros((8, 128 - 2 * rest), F32)
        for g in range(groups):
            o = g * lon
            g_ref[g, k] = jnp.concatenate(
                [
                    out[0][:, o : o + 128],
                    out[1][:, o : o + 128],
                    out[0][:, o + 128 : o + lon],
                    out[1][:, o + 128 : o + lon],
                    pad,
                ],
                axis=1,
            )
        ready(k)
        return carry

    lax.fori_loop(0, tr_ref.shape[1], level, 0)


def selector(slots):
    ids = lax.broadcasted_iota(jnp.int32, (512, 256), 0)
    return (ids == slots).astype(F32).astype(BF16)


def select(rest, g_ref, c_ref, slot_ref, p_ref, a_ref, ready):
    block = g_ref.shape[1]
    levels = g_ref.shape[0] * block
    sub = lax.broadcasted_iota(jnp.int32, (8, 384), 0) < 4
    half = lax.broadcasted_iota(jnp.int32, (8, 256), 0) < 4
    zero = jnp.zeros((8, 384), F32)
    for r in range(4):
        if r > 0:
            a_ref[r, 0 : 32 * r, :] = jnp.zeros((32 * r, 512), BF16)
        if r < 3:
            a_ref[r, 32 * r + 288 : 384, :] = jnp.zeros((96 - 32 * r, 512), BF16)

    def q(k):
        return g_ref[k // block, k % block] if 0 <= k < levels else zero

    def e_at(k):
        return face(q(k - 2), q(k - 1), q(k), q(k + 1))

    left = e_at(0)
    f_here = zero
    held = []
    right = e_at(1)
    s, kk = right - left, 6.0 * q(0) - 3.0 * (left + right)
    for k in range(levels):
        if k + 1 < levels:
            nxt = e_at(k + 2)
            s1, k1 = nxt - right, 6.0 * q(k + 1) - 3.0 * (right + nxt)
            c = jnp.where(sub, c_ref[k + 1, 0:1, :], c_ref[k + 1, 1:2, :])
            f_next = flux(c, right, s, s1, kk, k1)
            right, s, kk = nxt, s1, k1
        else:
            f_next = zero
        held.append(q(k) + f_here - f_next)
        f_here = f_next
        if k % 4 == 3:
            for rp in range(2):
                x = []
                for h in held:
                    third = h[:, 256:384]
                    if rp == 1:
                        third = pltpu.roll(third, 128 - rest, 1)
                    x.append(jnp.concatenate([h[:, 128 * rp : 128 * rp + 128], third], axis=1))
                t = [pltpu.roll(v, 4, 0) for v in x]
                first = [jnp.where(half, x[0], t[1]), jnp.where(half, x[2], t[3])]
                second = [jnp.where(half, t[0], x[1]), jnp.where(half, t[2], x[3])]
                for r2, rows in enumerate((first, second)):
                    r = 2 * rp + r2
                    hi, lo = split(jnp.concatenate(rows, axis=0))
                    at = 32 * r + 4 * (k - 3)
                    a_ref[r, at : at + 16, 0:256] = hi
                    a_ref[r, at : at + 16, 256:512] = lo
            held = []
    carried = None
    for r in range(4):
        one = selector(slot_ref[r : r + 1, :])
        out = dot(jnp.concatenate([one, one], axis=1), a_ref[r], NT)
        for t in range(3):
            part = out[:, 128 * t : 128 * t + 128]
            if t == 0 and r > 0:
                part = part + carried
            if t == 2 and r < 3:
                carried = part
                continue
            p_ref[2 * r + t] = part.reshape(p_ref.shape[1:])
        ready(r)


def reorder_kernel(levs, m_ref, n_ref, o_ref):
    order = m_ref.shape[0]
    levels = order // 4
    block = levels // levs
    x = lax.broadcasted_iota(jnp.int32, (order, order), 0)
    o = lax.broadcasted_iota(jnp.int32, (order, order), 1)
    pick = ((x & 3) * levels + (x >> 2) == o).astype(F32).astype(BF16)
    main = (x & 3) * levels + block * (x >> 5) + ((x >> 2) & 7)
    last = (x & 3) * levels + block * ((x - 256) >> 2) + block - 1
    put = (jnp.where(x < 256, main, last) == o).astype(F32).astype(BF16)
    part = order // 4
    for n, ref in enumerate((m_ref, n_ref)):
        hi, lo = split(ref[...])
        rest = (ref[...] - hi.astype(F32) - lo.astype(F32)).astype(BF16)
        out = None
        for piece in (hi, lo, rest):
            term = dot(dot(put, piece).astype(BF16), pick, NT)
            out = term if out is None else out + term
        o_ref[n, 0:order] = out[:, 0:128]
        o_ref[n, order : 2 * order] = out[:, 128:256]
        o_ref[n, 2 * order :] = jnp.concatenate([out[part * i : part * i + part, 256:] for i in range(4)], axis=1)


def unpacked(packed):
    part = packed.shape[0] // 9
    third = packed[8 * part :]
    lanes = third.shape[1] // 4
    third = jnp.concatenate([third[:, lanes * i : lanes * i + lanes] for i in range(4)], axis=0)
    return jnp.concatenate([packed[: 4 * part], packed[4 * part : 8 * part], third], axis=1)


def turned_tile(v_ref, j):
    live = (lax.broadcasted_iota(jnp.int32, (128, 512), 1) & 3) < 3
    return jnp.where(live, v_ref[j].reshape(512, 128).T, 0.0)


def unselect(lon, g, tile, last, slot_ref, o_ref):
    for r in range(4):
        rows = jnp.concatenate([tile[32 * r : 32 * r + 32], last[16 * g : 16 * g + 16]], axis=0)
        hi, lo = split(rows)
        one = selector(slot_ref[g, r : r + 1, :])
        out = dot(jnp.concatenate([hi, lo], axis=1), jnp.concatenate([one, one], axis=0))
        at = slice(lon * g, lon * g + lon)
        o_ref[r, 0:8, :, at] = out[0:32, :lon].reshape(8, 4, lon)
        o_ref[r, 8, :, at] = out[32 + 4 * r : 36 + 4 * r, :lon]


PIECES = ((0, 0, 2), (0, 1, 2), (1, None, 4), (2, None, 4), (3, None, 4))


def greet(lat, lev, levs):
    for i in range(1, levs):
        pl.semaphore_signal(
            pltpu.get_barrier_semaphore(), inc=1, device_id=(lat, lax.rem(lev + i, levs)), device_id_type=MESH
        )


def greeted(levs):
    pl.semaphore_wait(pltpu.get_barrier_semaphore(), levs - 1)


def send(src, dst, ssem, rsem, lat, to):
    return pltpu.make_async_remote_copy(
        src_ref=src, dst_ref=dst, send_sem=ssem, recv_sem=rsem, device_id=(lat, to), device_id_type=MESH
    )


def forth_kernel(
    rest, levs, tr_ref, south_ref, north_ref, zonal_ref, mer_ref, c_ref, slot_ref,
    r_ref, all_ref, zon_ref, g_ref, col_ref, p_ref, a_ref, s1, r1, s2, r2, s3, r3, lsem,
):
    lat, lev = lax.axis_index("lat"), lax.axis_index("lev")
    block = tr_ref.shape[1]
    greet(lat, lev, levs)
    fetch = pltpu.make_async_copy(zonal_ref, zon_ref, lsem.at[3])
    fetch.start()
    greeted(levs)

    def slot_copy(i):
        to = lax.rem(lev + i, levs)
        return send(slot_ref, all_ref.at[lev], s3.at[i], r3.at[i], lat, to)

    for i in range(1, levs):
        slot_copy(i).start()
    own_slots = pltpu.make_async_copy(slot_ref, all_ref.at[lev], lsem.at[2])
    own_slots.start()

    def level_copy(k, i):
        to = lax.rem(lev + i, levs)
        return send(g_ref.at[to, k], col_ref.at[lev, k], s1.at[k, i], r1.at[k, i], lat, to)

    def level_ready(k):
        for i in range(1, levs):
            level_copy(k, i).start()

    fetch.wait()
    horizontal(tr_ref, south_ref, north_ref, zon_ref, mer_ref, g_ref, level_ready)
    own = pltpu.make_async_copy(g_ref.at[lev], col_ref.at[lev], lsem.at[0])
    own.start()
    own.wait()

    @pl.loop(0, block)
    def _(k):
        for i in range(1, levs):
            level_copy(k, i).wait()

    def tiles(r):
        return slice(2 * r, 2 * r + (3 if r == 3 else 2))

    def row_copy(r, i):
        to = lax.rem(lev + i, levs)
        return send(p_ref.at[tiles(r), to, :, 0:3], r_ref.at[tiles(r), :, lev, 0:3], s2.at[r, i], r2.at[r, i], lat, to)

    def row_ready(r):
        for i in range(1, levs):
            row_copy(r, i).start()

    select(rest, col_ref, c_ref, slot_ref, p_ref, a_ref, row_ready)
    own = pltpu.make_async_copy(p_ref.at[:, lev, :, 0:3], r_ref.at[:, :, lev, 0:3], lsem.at[1])
    own.start()
    own.wait()
    for r in range(4):
        for i in range(1, levs):
            row_copy(r, i).wait()
    own_slots.wait()
    for i in range(1, levs):
        slot_copy(i).wait()


def back_kernel(
    rest, levs, order, r_ref, n0, n1, n2, n3, f0, f1, f2, f3, slot_ref,
    o_ref, y_ref, v_ref, w_ref, z_ref, m_ref, move_ref, s1, r1, s2, r2, lsem, msem,
):
    lat, lev = lax.axis_index("lat"), lax.axis_index("lev")
    greet(lat, lev, levs)

    fetches = []
    for n, ref in enumerate((n0, f0, n1, f1, n2, f2, n3, f3)):
        fetches.append(pltpu.make_async_copy(ref, m_ref.at[n], msem.at[n]))
        fetches[n].start()

    def begin(n):
        d, turn, _ = PIECES[n]
        at = lax.rem(lat // 4 - d + 4, 4) * 4
        return at if turn is None else at + lax.rem(lat // 2 + turn, 2) * 2

    def part(n):
        return pl.ds(begin(n), PIECES[n][2])

    def piece_copy(n, i):
        to = lax.rem(lev + i, levs)
        return send(y_ref.at[:, part(n), to, 0:3], v_ref.at[:, lev, part(n), 0:3], s1.at[n, i], r1.at[n, i], lat, to)

    def tile_copy(j, i):
        to = lax.rem(lev + i, levs)
        at = part(len(PIECES) - 1)
        return send(y_ref.at[j, at, to, 0:3], v_ref.at[j, lev, at, 0:3], s2.at[j, i], r2.at[j, i], lat, to)

    def own_copy(n):
        return pltpu.make_async_copy(y_ref.at[:, part(n), lev, 0:3], v_ref.at[:, lev, part(n), 0:3], lsem.at[n])

    to_lane = lax.broadcasted_iota(jnp.int32, (256, 1024), 1)
    from_lane = lax.broadcasted_iota(jnp.int32, (256, 1024), 0) & 127
    wanted = ((to_lane >> 2) & 3) * 32 + (to_lane >> 7) * 4 + (to_lane & 3)
    move_ref[...] = (from_lane == wanted).astype(F32).astype(BF16)

    def place_last(n):
        size = PIECES[n][2]
        many = 4 * size
        hi, lo = split(z_ref[:, part(n)].reshape(8 * many, 128))
        moved = dot(jnp.concatenate([hi, lo], axis=1), move_ref[...])
        group = (lax.broadcasted_iota(jnp.int32, (many, 1024), 1) >> 4) & 7
        x = moved[:many]
        for g in range(1, 8):
            x = jnp.where(group == g, moved[many * g : many * (g + 1)], x)
        for l in range(8):
            y_ref[8, part(n), l] = x[:, 128 * l : 128 * l + 128].reshape(size, 4, 128)

    def mix(n, at):
        tiles = [r_ref[j, n].reshape(4 * levs, 128) for j in range(9)]
        rows = []
        for r in range(4):
            x = jnp.concatenate(tiles[2 * r : 2 * r + 3], axis=1)
            if r > 0:
                x = pltpu.roll(x, 384 - 32 * r, 1)
            rows.append(x[:, :order])
        hi, lo = split(jnp.concatenate(rows, axis=0))
        y = dot(hi, w_ref[0, at], NT) + dot(lo, w_ref[0, at], NT) + dot(hi, w_ref[1, at], NT)
        many = 4 * levs
        quarter = lax.broadcasted_iota(jnp.int32, (many, 128), 1) >> 5
        for half in range(2):
            turns = []
            for r in range(4):
                tile = y[r * many : (r + 1) * many, 128 * half : 128 * half + 128]
                turns.append([tile] + [pltpu.roll(tile, 32 * m, 1) for m in range(1, 4)])
            for m in range(4):
                x = turns[3][(3 - m) % 4]
                for r in range(3):
                    x = jnp.where(quarter == r, turns[r][(r - m) % 4], x)
                y_ref[pl.ds(0, 8), n, 4 * half + m] = x.reshape(8, 4, 128)
        z = jnp.concatenate([y[r * many : (r + 1) * many, 256:] for r in range(4)], axis=1)
        z_ref[:, n] = z.reshape(8, 4, 128)

    arrivals = [8] + list(range(8))
    for n, (d, turn, size) in enumerate(PIECES):
        if turn != 1:
            fetches[2 * d].wait()
            fetches[2 * d + 1].wait()
        for at in range(size):
            hi, lo = split(unpacked(m_ref[2 * d + at % 2, at // 2 + (turn or 0)]))
            w_ref[0, at] = hi
            w_ref[1, at] = lo
        first = lax.rem(lat // 4 - d + 4, 4) * 4

        @pl.loop(0, size)
        def _(at):
            steps = at // 2 if turn is None else turn
            mix(first + lax.rem(lat // 2 + steps, 2) * 2 + lax.rem(lat + at, 2), at)

        place_last(n)
        own_copy(n).start()
        if n == 0:
            greeted(levs)
        if n < len(PIECES) - 1:
            for i in range(1, levs):
                piece_copy(n, i).start()
        else:
            for j in arrivals:
                for i in range(1, levs):
                    tile_copy(j, i).start()

    for n in range(len(PIECES)):
        own_copy(n).wait()
    for n in range(len(PIECES) - 1):
        for i in range(1, levs):
            piece_copy(n, i).wait()
    last = None
    for j in arrivals:
        for i in range(1, levs):
            tile_copy(j, i).wait()
        tile = turned_tile(v_ref, j)
        if j == 8:
            last = tile
        else:
            unselect(128 + rest, j, tile, last, slot_ref, o_ref)


def call(kernel, shape, count, scratch=(), limit=48, extra=None, large=(), **params):
    return pl.pallas_call(
        kernel,
        out_shape=jax.ShapeDtypeStruct(shape, F32) if extra is None else (jax.ShapeDtypeStruct(shape, F32), extra),
        in_specs=[pl.BlockSpec(memory_space=pl.ANY) if n in large else VMEM for n in range(count)],
        out_specs=VMEM if extra is None else (VMEM, VMEM),
        scratch_shapes=list(scratch),
        compiler_params=pltpu.CompilerParams(vmem_limit_bytes=limit << 20, **params),
    )


def body(tracers, zonal, meridional, vertical, route, inverse):
    trac, levs_here, rows, width = tracers.shape
    lats, groups = lax.axis_size("lat"), lax.axis_size("lev")
    levels, _, lon = vertical.shape
    rest = lon - 128
    order = inverse.shape[2]
    own = inverse[0, 0]
    across = lax.ppermute(own, "lat", [(i, i ^ 2) for i in range(lats)])
    turned = jnp.transpose(tracers, (2, 1, 0, 3))
    up = [(i, i + 1) for i in range(lats - 1)]
    down = [(i + 1, i) for i in range(lats - 1)]
    south = lax.ppermute(turned[rows - 3 :], "lat", up)
    edge = jnp.pad(meridional[:, 0], ((0, -levs_here % 4), (0, 0))).reshape(-1, 4, width)
    north = lax.ppermute(
        jnp.concatenate([turned[:3].reshape(3 * levs_here, trac, width), edge], axis=0), "lat", down
    )
    pair = call(functools.partial(reorder_kernel, groups), (2, order * order // 128, 128), 2, limit=12)(own, across)
    targets = route[:, :, 0]
    before = jnp.arange(lon)[:, None] < jnp.arange(lon)[None, :]
    same = jnp.logical_and(targets[:, :, None] == targets[:, None, :], before[None])
    place = (targets % groups) * lats + targets // groups
    slots = place * 4 + jnp.sum(same.astype(jnp.int32), axis=1)
    slots = jnp.pad(slots, ((0, 0), (0, 256 - lon)), constant_values=-1)
    v = vertical.reshape(levels, 2, 2, lon)
    courant = jnp.concatenate(
        [v[:, 0, :, :128], v[:, 1, :, :128], v[:, 0, :, 128:], v[:, 1, :, 128:], jnp.zeros((levels, 2, 128 - 2 * rest), F32)],
        axis=-1,
    )
    shifted = [lax.ppermute(pair, "lat", [(i, (i + 4 * d) % lats) for i in range(lats)]) for d in range(1, 4)]
    other = [(i, i ^ 1) for i in range(lats)]
    dma = pltpu.SemaphoreType.DMA
    levels_of = pltpu.VMEM((groups, levs_here, 8, 384), F32)
    received, all_slots = call(
        functools.partial(forth_kernel, rest, groups),
        (9, lats, groups, 4, 128),
        7,
        [
            pltpu.VMEM(zonal.shape, F32),
            levels_of,
            levels_of,
            pltpu.VMEM((9, groups, lats, 4, 128), F32),
            pltpu.VMEM((4, 384, 512), BF16),
            dma((levs_here, groups)),
            dma((levs_here, groups)),
            dma((4, groups)),
            dma((4, groups)),
            dma((groups,)),
            dma((groups,)),
            dma((4,)),
        ],
        extra=jax.ShapeDtypeStruct((groups, 4, 256), jnp.int32),
        limit=24,
        large=(3,),
        collective_id=0,
        has_side_effects=True,
    )(turned, south, north, zonal, meridional, courant, slots)
    received, pair, shifted = lax.optimization_barrier((received, pair, shifted))
    far = [lax.ppermute(x, "lat", other) for x in [pair] + shifted]
    whole = call(
        functools.partial(back_kernel, rest, groups, order),
        (4, levs_here, trac, width),
        10,
        [
            pltpu.VMEM((9, lats, groups, 4, 128), F32),
            pltpu.VMEM((9, groups, lats, 4, 128), F32),
            pltpu.VMEM((2, 4, order, order), BF16),
            pltpu.VMEM((groups, lats, 4, 128), F32),
            pltpu.VMEM((8,) + pair.shape, F32),
            pltpu.VMEM((256, 1024), BF16),
            dma((len(PIECES) - 1, groups)),
            dma((len(PIECES) - 1, groups)),
            dma((9, groups)),
            dma((9, groups)),
            dma((len(PIECES),)),
            dma((8,)),
        ],
        large=range(1, 9),
        limit=28,
        collective_id=1,
        has_side_effects=True,
    )(received, pair, *shifted, *far, all_slots)
    return jnp.transpose(whole, (2, 1, 0, 3)) - tracers


def solution(mesh):
    in_specs = (
        P(None, "lev", "lat", None),
        P("lev", "lat", None),
        P("lev", "lat", None),
        P(None, "lat", "lev"),
        P("lat", "lev", None),
        P("lat", "lev", None, None),
    )
    out_specs = P(None, "lev", "lat", None)
    return jax.shard_map(body, mesh=mesh, in_specs=in_specs, out_specs=out_specs, check_vma=False)
```

```python
import functools
import jax
import jax.numpy as jnp
from jax import lax
from jax.experimental import pallas as pl
from jax.experimental.pallas import tpu as pltpu
from jax.sharding import PartitionSpec as P

MESH = pl.DeviceIdType.MESH
F32 = jnp.float32
BF16 = jnp.bfloat16
VMEM = pl.BlockSpec(memory_space=pltpu.VMEM)
NT = (((1,), (1,)), ((), ()))
NN = (((1,), (0,)), ((), ()))


def dot(a, b, dims=NN):
    return lax.dot_general(a, b, dims, preferred_element_type=F32)


def split(x):
    hi = x.astype(BF16)
    lo = (x - hi.astype(F32)).astype(BF16)
    return hi, lo


def flux(c, e, s_low, s_here, k_low, k_here):
    up = c >= 0.0
    a = jnp.abs(c)
    s = jnp.where(up, -s_low, s_here)
    k = jnp.where(up, k_low, k_here)
    return c * (e + (0.5 * a) * (s + (1.0 - (2.0 / 3.0) * a) * k))


def face(q_m2, q_m1, q_0, q_p1):
    return (7.0 / 12.0) * (q_m1 + q_0) - (1.0 / 12.0) * (q_m2 + q_p1)


def horizontal(tr_ref, south_ref, north_ref, both_ref, g_ref, ready):
    lat = lax.axis_index("lat")
    last = lax.axis_size("lat") - 1
    width = tr_ref.shape[3]
    groups = g_ref.shape[0]
    lon = width // groups
    sub = lax.broadcasted_iota(jnp.int32, (8, width), 0) < 4
    ext = -(-width // 128) * 128
    spare = ext - width
    half = spare // 3
    ksouth = (lat > 0).astype(F32)
    knorth = (lat < last).astype(F32)

    def swap(x):
        return pltpu.roll(x, 4, 0)

    def extend(x):
        return jnp.concatenate([x, x[:, :half], x[:, width - (spare - half):]], axis=1)

    def rolled(x, n):
        return pltpu.roll(x, n % ext, 1)

    def level(k, carry):
        row = [tr_ref[r, k] for r in range(4)]
        low = [south_ref[r, k] * ksouth for r in range(3)]
        high = [north_ref[r * tr_ref.shape[1] + k] * knorth for r in range(3)]
        pair = lambda a, b: jnp.concatenate([a, b], axis=0)
        q = [
            pair(low[0], low[0]),
            pair(low[1], low[2]),
            pair(row[0], row[1]),
            pair(row[2], row[3]),
            pair(high[0], high[1]),
            pair(high[2], high[2]),
        ]
        sq = [swap(x) for x in q]
        e = [face(q[p - 1], jnp.where(sub, sq[p - 1], sq[p]), q[p], jnp.where(sub, sq[p], sq[p + 1])) for p in range(1, 5)]
        se = [swap(x) for x in e]
        s, kk = [], []
        for p in range(4):
            right = jnp.where(sub, se[p], se[min(p + 1, 3)])
            s.append(right - e[p])
            kk.append(6.0 * q[p + 1] - 3.0 * (e[p] + right))
        ss = [swap(x) for x in s]
        sk = [swap(x) for x in kk]
        m = both_ref[1, k]
        zero = jnp.zeros((8, width), F32)
        m0 = jnp.where(sub, m[0:1] * ksouth, m[1:2])
        m1 = jnp.where(sub, m[2:3], m[3:4])
        m2 = north_ref[3 * tr_ref.shape[1] + k // 4, pl.ds(k % 4, 1), :] * knorth + zero
        f = []
        for i, c in enumerate((m0, m1, m2)):
            p = i + 1
            f.append(
                flux(c, e[p], jnp.where(sub, ss[p - 1], ss[p]), s[p], jnp.where(sub, sk[p - 1], sk[p]), kk[p])
            )
        sf = [swap(x) for x in f]
        z = both_ref[0, k]
        out = []
        for p in range(2):
            lat_change = f[p] - jnp.where(sub, sf[p], sf[p + 1])
            x = extend(q[p + 2])
            c = extend(jnp.where(sub, z[2 * p : 2 * p + 1], z[2 * p + 1 : 2 * p + 2]))
            le = face(rolled(x, 2), rolled(x, 1), x, rolled(x, -1))
            right = rolled(le, -1)
            ls = right - le
            lk = 6.0 * x - 3.0 * (le + right)
            lf = flux(c, le, rolled(ls, 1), ls, rolled(lk, 1), lk)
            lon_change = lf - rolled(lf, -1)
            out.append(q[p + 2] + lon_change[:, :width] + lat_change)
        rest = lon - 128
        pad = jnp.zeros((8, 128 - 2 * rest), F32)
        for g in range(groups):
            o = g * lon
            g_ref[g, k] = jnp.concatenate(
                [
                    out[0][:, o : o + 128],
                    out[1][:, o : o + 128],
                    out[0][:, o + 128 : o + lon],
                    out[1][:, o + 128 : o + lon],
                    pad,
                ],
                axis=1,
            )
        ready(k)
        return carry

    lax.fori_loop(0, tr_ref.shape[1], level, 0)


def selector(slots):
    ids = lax.broadcasted_iota(jnp.int32, (512, 256), 0)
    return (ids == slots).astype(F32).astype(BF16)


def select(rest, g_ref, c_ref, slot_ref, p_ref, a_ref, ready):
    block = g_ref.shape[1]
    levels = g_ref.shape[0] * block
    sub = lax.broadcasted_iota(jnp.int32, (8, 384), 0) < 4
    half = lax.broadcasted_iota(jnp.int32, (8, 256), 0) < 4
    zero = jnp.zeros((8, 384), F32)
    for r in range(4):
        if r > 0:
            a_ref[r, 0 : 32 * r, :] = jnp.zeros((32 * r, 512), BF16)
        if r < 3:
            a_ref[r, 32 * r + 288 : 384, :] = jnp.zeros((96 - 32 * r, 512), BF16)

    def q(k):
        return g_ref[k // block, k % block] if 0 <= k < levels else zero

    def e_at(k):
        return face(q(k - 2), q(k - 1), q(k), q(k + 1))

    left = e_at(0)
    f_here = zero
    held = []
    right = e_at(1)
    s, kk = right - left, 6.0 * q(0) - 3.0 * (left + right)
    for k in range(levels):
        if k + 1 < levels:
            nxt = e_at(k + 2)
            s1, k1 = nxt - right, 6.0 * q(k + 1) - 3.0 * (right + nxt)
            c = jnp.where(sub, c_ref[k + 1, 0:1, :], c_ref[k + 1, 1:2, :])
            f_next = flux(c, right, s, s1, kk, k1)
            right, s, kk = nxt, s1, k1
        else:
            f_next = zero
        held.append(q(k) + f_here - f_next)
        f_here = f_next
        if k % 4 == 3:
            for rp in range(2):
                x = []
                for h in held:
                    third = h[:, 256:384]
                    if rp == 1:
                        third = pltpu.roll(third, 128 - rest, 1)
                    x.append(jnp.concatenate([h[:, 128 * rp : 128 * rp + 128], third], axis=1))
                t = [pltpu.roll(v, 4, 0) for v in x]
                first = [jnp.where(half, x[0], t[1]), jnp.where(half, x[2], t[3])]
                second = [jnp.where(half, t[0], x[1]), jnp.where(half, t[2], x[3])]
                for r2, rows in enumerate((first, second)):
                    r = 2 * rp + r2
                    hi, lo = split(jnp.concatenate(rows, axis=0))
                    at = 32 * r + 4 * (k - 3)
                    a_ref[r, at : at + 16, 0:256] = hi
                    a_ref[r, at : at + 16, 256:512] = lo
            held = []
    carried = None
    for r in range(4):
        one = selector(slot_ref[r : r + 1, :])
        out = dot(jnp.concatenate([one, one], axis=1), a_ref[r], NT)
        for t in range(3):
            part = out[:, 128 * t : 128 * t + 128]
            if t == 0 and r > 0:
                part = part + carried
            if t == 2 and r < 3:
                carried = part
                continue
            p_ref[2 * r + t] = part.reshape(p_ref.shape[1:])
        ready(r)


def reorder_kernel(levs, m_ref, o_ref):
    order = m_ref.shape[1]
    levels = order // 4
    block = levels // levs
    x = lax.broadcasted_iota(jnp.int32, (order, order), 0)
    o = lax.broadcasted_iota(jnp.int32, (order, order), 1)
    pick = ((x & 3) * levels + (x >> 2) == o).astype(F32).astype(BF16)
    main = (x & 3) * levels + block * (x >> 5) + ((x >> 2) & 7)
    last = (x & 3) * levels + block * ((x - 256) >> 2) + block - 1
    put = (jnp.where(x < 256, main, last) == o).astype(F32).astype(BF16)
    part = order // 4
    for n in range(2):
        hi, lo = split(m_ref[n])
        rest = (m_ref[n] - hi.astype(F32) - lo.astype(F32)).astype(BF16)
        out = None
        for piece in (hi, lo, rest):
            term = dot(dot(put, piece).astype(BF16), pick, NT)
            out = term if out is None else out + term
        o_ref[n, 0:order] = out[:, 0:128]
        o_ref[n, order : 2 * order] = out[:, 128:256]
        o_ref[n, 2 * order :] = jnp.concatenate([out[part * i : part * i + part, 256:] for i in range(4)], axis=1)


def unpacked(packed):
    part = packed.shape[0] // 9
    third = packed[8 * part :]
    lanes = third.shape[1] // 4
    third = jnp.concatenate([third[:, lanes * i : lanes * i + lanes] for i in range(4)], axis=0)
    return jnp.concatenate([packed[: 4 * part], packed[4 * part : 8 * part], third], axis=1)


def turned_tile(v_ref, j):
    live = (lax.broadcasted_iota(jnp.int32, (128, 512), 1) & 3) < 3
    return jnp.where(live, v_ref[j].reshape(512, 128).T, 0.0)


def unselect(lon, g, tile, last, slot_ref, o_ref):
    for r in range(4):
        rows = jnp.concatenate([tile[32 * r : 32 * r + 32], last[16 * g : 16 * g + 16]], axis=0)
        hi, lo = split(rows)
        one = selector(slot_ref[g, r : r + 1, :])
        out = dot(jnp.concatenate([hi, lo], axis=1), jnp.concatenate([one, one], axis=0))
        at = slice(lon * g, lon * g + lon)
        o_ref[r, 0:8, :, at] = out[0:32, :lon].reshape(8, 4, lon)
        o_ref[r, 8, :, at] = out[32 + 4 * r : 36 + 4 * r, :lon]


PIECES = ((0, 0, 2), (0, 1, 2), (1, None, 4), (2, None, 4), (3, None, 4))


def greet(lat, lev, levs):
    for i in range(1, levs):
        pl.semaphore_signal(
            pltpu.get_barrier_semaphore(), inc=1, device_id=(lat, lax.rem(lev + i, levs)), device_id_type=MESH
        )


def greeted(levs):
    pl.semaphore_wait(pltpu.get_barrier_semaphore(), levs - 1)


def send(src, dst, ssem, rsem, lat, to):
    return pltpu.make_async_remote_copy(
        src_ref=src, dst_ref=dst, send_sem=ssem, recv_sem=rsem, device_id=(lat, to), device_id_type=MESH
    )


def forth_kernel(
    rest, levs, tr_ref, south_ref, north_ref, both_ref, c_ref, slot_ref,
    r_ref, all_ref, g_ref, col_ref, p_ref, a_ref, s1, r1, s2, r2, s3, r3, lsem,
):
    lat, lev = lax.axis_index("lat"), lax.axis_index("lev")
    block = tr_ref.shape[1]
    greet(lat, lev, levs)
    greeted(levs)

    def slot_copy(i):
        to = lax.rem(lev + i, levs)
        return send(slot_ref, all_ref.at[lev], s3.at[i], r3.at[i], lat, to)

    for i in range(1, levs):
        slot_copy(i).start()
    own_slots = pltpu.make_async_copy(slot_ref, all_ref.at[lev], lsem.at[2])
    own_slots.start()

    def level_copy(k, i):
        to = lax.rem(lev + i, levs)
        return send(g_ref.at[to, k], col_ref.at[lev, k], s1.at[k, i], r1.at[k, i], lat, to)

    def level_ready(k):
        for i in range(1, levs):
            level_copy(k, i).start()

    horizontal(tr_ref, south_ref, north_ref, both_ref, g_ref, level_ready)
    own = pltpu.make_async_copy(g_ref.at[lev], col_ref.at[lev], lsem.at[0])
    own.start()
    own.wait()

    @pl.loop(0, block)
    def _(k):
        for i in range(1, levs):
            level_copy(k, i).wait()

    def tiles(r):
        return slice(2 * r, 2 * r + (3 if r == 3 else 2))

    def row_copy(r, i):
        to = lax.rem(lev + i, levs)
        return send(p_ref.at[tiles(r), to, :, 0:3], r_ref.at[tiles(r), :, lev, 0:3], s2.at[r, i], r2.at[r, i], lat, to)

    def row_ready(r):
        for i in range(1, levs):
            row_copy(r, i).start()

    select(rest, col_ref, c_ref, slot_ref, p_ref, a_ref, row_ready)
    own = pltpu.make_async_copy(p_ref.at[:, lev, :, 0:3], r_ref.at[:, :, lev, 0:3], lsem.at[1])
    own.start()
    own.wait()
    for r in range(4):
        for i in range(1, levs):
            row_copy(r, i).wait()
    own_slots.wait()
    for i in range(1, levs):
        slot_copy(i).wait()


def back_kernel(
    rest, levs, order, r_ref, n0, n1, n2, n3, f0, f1, f2, f3, slot_ref,
    o_ref, y_ref, v_ref, w_ref, z_ref, m_ref, move_ref, s1, r1, s2, r2, lsem, msem,
):
    lat, lev = lax.axis_index("lat"), lax.axis_index("lev")
    greet(lat, lev, levs)

    fetches = []
    for n, ref in enumerate((n0, f0, n1, f1, n2, f2, n3, f3)):
        fetches.append(pltpu.make_async_copy(ref, m_ref.at[n], msem.at[n]))
        fetches[n].start()

    def begin(n):
        d, turn, _ = PIECES[n]
        at = lax.rem(lat // 4 - d + 4, 4) * 4
        return at if turn is None else at + lax.rem(lat // 2 + turn, 2) * 2

    def part(n):
        return pl.ds(begin(n), PIECES[n][2])

    def piece_copy(n, i):
        to = lax.rem(lev + i, levs)
        return send(y_ref.at[:, part(n), to, 0:3], v_ref.at[:, lev, part(n), 0:3], s1.at[n, i], r1.at[n, i], lat, to)

    def tile_copy(j, i):
        to = lax.rem(lev + i, levs)
        at = part(len(PIECES) - 1)
        return send(y_ref.at[j, at, to, 0:3], v_ref.at[j, lev, at, 0:3], s2.at[j, i], r2.at[j, i], lat, to)

    def own_copy(n):
        return pltpu.make_async_copy(y_ref.at[:, part(n), lev, 0:3], v_ref.at[:, lev, part(n), 0:3], lsem.at[n])

    to_lane = lax.broadcasted_iota(jnp.int32, (256, 1024), 1)
    from_lane = lax.broadcasted_iota(jnp.int32, (256, 1024), 0) & 127
    wanted = ((to_lane >> 2) & 3) * 32 + (to_lane >> 7) * 4 + (to_lane & 3)
    move_ref[...] = (from_lane == wanted).astype(F32).astype(BF16)

    def place_last(n):
        size = PIECES[n][2]
        many = 4 * size
        hi, lo = split(z_ref[:, part(n)].reshape(8 * many, 128))
        moved = dot(jnp.concatenate([hi, lo], axis=1), move_ref[...])
        group = (lax.broadcasted_iota(jnp.int32, (many, 1024), 1) >> 4) & 7
        x = moved[:many]
        for g in range(1, 8):
            x = jnp.where(group == g, moved[many * g : many * (g + 1)], x)
        for l in range(8):
            y_ref[8, part(n), l] = x[:, 128 * l : 128 * l + 128].reshape(size, 4, 128)

    def mix(n, at):
        tiles = [r_ref[j, n].reshape(4 * levs, 128) for j in range(9)]
        rows = []
        for r in range(4):
            x = jnp.concatenate(tiles[2 * r : 2 * r + 3], axis=1)
            if r > 0:
                x = pltpu.roll(x, 384 - 32 * r, 1)
            rows.append(x[:, :order])
        hi, lo = split(jnp.concatenate(rows, axis=0))
        y = dot(hi, w_ref[0, at], NT) + dot(lo, w_ref[0, at], NT) + dot(hi, w_ref[1, at], NT)
        many = 4 * levs
        quarter = lax.broadcasted_iota(jnp.int32, (many, 128), 1) >> 5
        for half in range(2):
            turns = []
            for r in range(4):
                tile = y[r * many : (r + 1) * many, 128 * half : 128 * half + 128]
                turns.append([tile] + [pltpu.roll(tile, 32 * m, 1) for m in range(1, 4)])
            for m in range(4):
                x = turns[3][(3 - m) % 4]
                for r in range(3):
                    x = jnp.where(quarter == r, turns[r][(r - m) % 4], x)
                y_ref[pl.ds(0, 8), n, 4 * half + m] = x.reshape(8, 4, 128)
        z = jnp.concatenate([y[r * many : (r + 1) * many, 256:] for r in range(4)], axis=1)
        z_ref[:, n] = z.reshape(8, 4, 128)

    arrivals = [8] + list(range(8))
    for n, (d, turn, size) in enumerate(PIECES):
        if turn != 1:
            fetches[2 * d].wait()
            fetches[2 * d + 1].wait()
        for at in range(size):
            hi, lo = split(unpacked(m_ref[2 * d + at % 2, at // 2 + (turn or 0)]))
            w_ref[0, at] = hi
            w_ref[1, at] = lo
        first = lax.rem(lat // 4 - d + 4, 4) * 4

        @pl.loop(0, size)
        def _(at):
            steps = at // 2 if turn is None else turn
            mix(first + lax.rem(lat // 2 + steps, 2) * 2 + lax.rem(lat + at, 2), at)

        place_last(n)
        own_copy(n).start()
        if n == 0:
            greeted(levs)
        if n < len(PIECES) - 1:
            for i in range(1, levs):
                piece_copy(n, i).start()
        else:
            for j in arrivals:
                for i in range(1, levs):
                    tile_copy(j, i).start()

    for n in range(len(PIECES)):
        own_copy(n).wait()
    for n in range(len(PIECES) - 1):
        for i in range(1, levs):
            piece_copy(n, i).wait()
    last = None
    for j in arrivals:
        for i in range(1, levs):
            tile_copy(j, i).wait()
        tile = turned_tile(v_ref, j)
        if j == 8:
            last = tile
        else:
            unselect(128 + rest, j, tile, last, slot_ref, o_ref)


def call(kernel, shape, count, scratch=(), limit=48, extra=None, large=(), **params):
    return pl.pallas_call(
        kernel,
        out_shape=jax.ShapeDtypeStruct(shape, F32) if extra is None else (jax.ShapeDtypeStruct(shape, F32), extra),
        in_specs=[pl.BlockSpec(memory_space=pl.ANY) if n in large else VMEM for n in range(count)],
        out_specs=VMEM if extra is None else (VMEM, VMEM),
        scratch_shapes=list(scratch),
        compiler_params=pltpu.CompilerParams(vmem_limit_bytes=limit << 20, **params),
    )


def body(tracers, zonal, meridional, vertical, route, inverse):
    trac, levs_here, rows, width = tracers.shape
    lats, groups = lax.axis_size("lat"), lax.axis_size("lev")
    levels, _, lon = vertical.shape
    rest = lon - 128
    order = inverse.shape[2]
    own = inverse[0, 0]
    across = lax.ppermute(own, "lat", [(i, i ^ 2) for i in range(lats)])
    turned = jnp.transpose(tracers, (2, 1, 0, 3))
    up = [(i, i + 1) for i in range(lats - 1)]
    down = [(i + 1, i) for i in range(lats - 1)]
    south = lax.ppermute(turned[rows - 3 :], "lat", up)
    edge = jnp.pad(meridional[:, 0], ((0, -levs_here % 4), (0, 0))).reshape(-1, 4, width)
    north = lax.ppermute(
        jnp.concatenate([turned[:3].reshape(3 * levs_here, trac, width), edge], axis=0), "lat", down
    )
    pair = call(functools.partial(reorder_kernel, groups), (2, order * order // 128, 128), 1, limit=12)(jnp.stack([own, across]))
    targets = route[:, :, 0]
    before = jnp.arange(lon)[:, None] < jnp.arange(lon)[None, :]
    same = jnp.logical_and(targets[:, :, None] == targets[:, None, :], before[None])
    place = (targets % groups) * lats + targets // groups
    slots = place * 4 + jnp.sum(same.astype(jnp.int32), axis=1)
    slots = jnp.pad(slots, ((0, 0), (0, 256 - lon)), constant_values=-1)
    v = vertical.reshape(levels, 2, 2, lon)
    courant = jnp.concatenate(
        [v[:, 0, :, :128], v[:, 1, :, :128], v[:, 0, :, 128:], v[:, 1, :, 128:], jnp.zeros((levels, 2, 128 - 2 * rest), F32)],
        axis=-1,
    )
    shifted = [lax.ppermute(pair, "lat", [(i, (i + 4 * d) % lats) for i in range(lats)]) for d in range(1, 4)]
    other = [(i, i ^ 1) for i in range(lats)]
    dma = pltpu.SemaphoreType.DMA
    levels_of = pltpu.VMEM((groups, levs_here, 8, 384), F32)
    received, all_slots = call(
        functools.partial(forth_kernel, rest, groups),
        (9, lats, groups, 4, 128),
        6,
        [
            levels_of,
            levels_of,
            pltpu.VMEM((9, groups, lats, 4, 128), F32),
            pltpu.VMEM((4, 384, 512), BF16),
            dma((levs_here, groups)),
            dma((levs_here, groups)),
            dma((4, groups)),
            dma((4, groups)),
            dma((groups,)),
            dma((groups,)),
            dma((3,)),
        ],
        extra=jax.ShapeDtypeStruct((groups, 4, 256), jnp.int32),
        limit=24,
        collective_id=0,
        has_side_effects=True,
    )(turned, south, north, jnp.stack([zonal, meridional]), courant, slots)
    received, pair, shifted = lax.optimization_barrier((received, pair, shifted))
    far = [lax.ppermute(x, "lat", other) for x in [pair] + shifted]
    whole = call(
        functools.partial(back_kernel, rest, groups, order),
        (4, levs_here, trac, width),
        10,
        [
            pltpu.VMEM((9, lats, groups, 4, 128), F32),
            pltpu.VMEM((9, groups, lats, 4, 128), F32),
            pltpu.VMEM((2, 4, order, order), BF16),
            pltpu.VMEM((groups, lats, 4, 128), F32),
            pltpu.VMEM((8,) + pair.shape, F32),
            pltpu.VMEM((256, 1024), BF16),
            dma((len(PIECES) - 1, groups)),
            dma((len(PIECES) - 1, groups)),
            dma((9, groups)),
            dma((9, groups)),
            dma((len(PIECES),)),
            dma((8,)),
        ],
        large=range(1, 9),
        limit=28,
        collective_id=1,
        has_side_effects=True,
    )(received, pair, *shifted, *far, all_slots)
    return jnp.transpose(whole, (2, 1, 0, 3)) - tracers


def solution(mesh):
    in_specs = (
        P(None, "lev", "lat", None),
        P("lev", "lat", None),
        P("lev", "lat", None),
        P(None, "lat", "lev"),
        P("lat", "lev", None),
        P("lat", "lev", None, None),
    )
    out_specs = P(None, "lev", "lat", None)
    return jax.shard_map(body, mesh=mesh, in_specs=in_specs, out_specs=out_specs, check_vma=False)
```

```python
import functools
import jax
import jax.numpy as jnp
from jax import lax
from jax.experimental import pallas as pl
from jax.experimental.pallas import tpu as pltpu
from jax.sharding import PartitionSpec as P

MESH = pl.DeviceIdType.MESH
F32 = jnp.float32
BF16 = jnp.bfloat16
VMEM = pl.BlockSpec(memory_space=pltpu.VMEM)
NT = (((1,), (1,)), ((), ()))
NN = (((1,), (0,)), ((), ()))


def dot(a, b, dims=NN):
    return lax.dot_general(a, b, dims, preferred_element_type=F32)


def split(x):
    hi = x.astype(BF16)
    lo = (x - hi.astype(F32)).astype(BF16)
    return hi, lo


def flux(c, e, s_low, s_here, k_low, k_here):
    up = c >= 0.0
    a = jnp.abs(c)
    s = jnp.where(up, -s_low, s_here)
    k = jnp.where(up, k_low, k_here)
    return c * (e + (0.5 * a) * (s + (1.0 - (2.0 / 3.0) * a) * k))


def face(q_m2, q_m1, q_0, q_p1):
    return (7.0 / 12.0) * (q_m1 + q_0) - (1.0 / 12.0) * (q_m2 + q_p1)


def horizontal(tr_ref, south_ref, north_ref, both_ref, g_ref, ready):
    lat = lax.axis_index("lat")
    last = lax.axis_size("lat") - 1
    width = tr_ref.shape[3]
    groups = g_ref.shape[0]
    lon = width // groups
    sub = lax.broadcasted_iota(jnp.int32, (8, width), 0) < 4
    ext = -(-width // 128) * 128
    spare = ext - width
    half = spare // 3
    ksouth = (lat > 0).astype(F32)
    knorth = (lat < last).astype(F32)

    def swap(x):
        return pltpu.roll(x, 4, 0)

    def extend(x):
        return jnp.concatenate([x, x[:, :half], x[:, width - (spare - half):]], axis=1)

    def rolled(x, n):
        return pltpu.roll(x, n % ext, 1)

    def level(k, carry):
        row = [tr_ref[r, k] for r in range(4)]
        low = [south_ref[r, k] * ksouth for r in range(3)]
        high = [north_ref[r * tr_ref.shape[1] + k] * knorth for r in range(3)]
        pair = lambda a, b: jnp.concatenate([a, b], axis=0)
        q = [
            pair(low[0], low[0]),
            pair(low[1], low[2]),
            pair(row[0], row[1]),
            pair(row[2], row[3]),
            pair(high[0], high[1]),
            pair(high[2], high[2]),
        ]
        sq = [swap(x) for x in q]
        e = [face(q[p - 1], jnp.where(sub, sq[p - 1], sq[p]), q[p], jnp.where(sub, sq[p], sq[p + 1])) for p in range(1, 5)]
        se = [swap(x) for x in e]
        s, kk = [], []
        for p in range(4):
            right = jnp.where(sub, se[p], se[min(p + 1, 3)])
            s.append(right - e[p])
            kk.append(6.0 * q[p + 1] - 3.0 * (e[p] + right))
        ss = [swap(x) for x in s]
        sk = [swap(x) for x in kk]
        m = both_ref[1, k]
        zero = jnp.zeros((8, width), F32)
        m0 = jnp.where(sub, m[0:1] * ksouth, m[1:2])
        m1 = jnp.where(sub, m[2:3], m[3:4])
        m2 = north_ref[3 * tr_ref.shape[1] + k // 4, pl.ds(k % 4, 1), :] * knorth + zero
        f = []
        for i, c in enumerate((m0, m1, m2)):
            p = i + 1
            f.append(
                flux(c, e[p], jnp.where(sub, ss[p - 1], ss[p]), s[p], jnp.where(sub, sk[p - 1], sk[p]), kk[p])
            )
        sf = [swap(x) for x in f]
        z = both_ref[0, k]
        out = []
        for p in range(2):
            lat_change = f[p] - jnp.where(sub, sf[p], sf[p + 1])
            x = extend(q[p + 2])
            c = extend(jnp.where(sub, z[2 * p : 2 * p + 1], z[2 * p + 1 : 2 * p + 2]))
            le = face(rolled(x, 2), rolled(x, 1), x, rolled(x, -1))
            right = rolled(le, -1)
            ls = right - le
            lk = 6.0 * x - 3.0 * (le + right)
            lf = flux(c, le, rolled(ls, 1), ls, rolled(lk, 1), lk)
            lon_change = lf - rolled(lf, -1)
            out.append(q[p + 2] + lon_change[:, :width] + lat_change)
        rest = lon - 128
        pad = jnp.zeros((8, 128 - 2 * rest), F32)
        for g in range(groups):
            o = g * lon
            g_ref[g, k] = jnp.concatenate(
                [
                    out[0][:, o : o + 128],
                    out[1][:, o : o + 128],
                    out[0][:, o + 128 : o + lon],
                    out[1][:, o + 128 : o + lon],
                    pad,
                ],
                axis=1,
            )
        ready(k)
        return carry

    lax.fori_loop(0, tr_ref.shape[1], level, 0)


def selector(slots):
    ids = lax.broadcasted_iota(jnp.int32, (512, 256), 0)
    return (ids == slots).astype(F32).astype(BF16)


def select(rest, g_ref, c_ref, slot_ref, p_ref, a_ref, ready):
    block = g_ref.shape[1]
    levels = g_ref.shape[0] * block
    sub = lax.broadcasted_iota(jnp.int32, (8, 384), 0) < 4
    half = lax.broadcasted_iota(jnp.int32, (8, 256), 0) < 4
    zero = jnp.zeros((8, 384), F32)
    for r in range(4):
        if r > 0:
            a_ref[r, 0 : 32 * r, :] = jnp.zeros((32 * r, 512), BF16)
        if r < 3:
            a_ref[r, 32 * r + 288 : 384, :] = jnp.zeros((96 - 32 * r, 512), BF16)

    def q(k):
        return g_ref[k // block, k % block] if 0 <= k < levels else zero

    def e_at(k):
        return face(q(k - 2), q(k - 1), q(k), q(k + 1))

    left = e_at(0)
    f_here = zero
    held = []
    right = e_at(1)
    s, kk = right - left, 6.0 * q(0) - 3.0 * (left + right)
    for k in range(levels):
        if k + 1 < levels:
            nxt = e_at(k + 2)
            s1, k1 = nxt - right, 6.0 * q(k + 1) - 3.0 * (right + nxt)
            c = jnp.where(sub, c_ref[k + 1, 0:1, :], c_ref[k + 1, 1:2, :])
            f_next = flux(c, right, s, s1, kk, k1)
            right, s, kk = nxt, s1, k1
        else:
            f_next = zero
        held.append(q(k) + f_here - f_next)
        f_here = f_next
        if k % 4 == 3:
            for rp in range(2):
                x = []
                for h in held:
                    third = h[:, 256:384]
                    if rp == 1:
                        third = pltpu.roll(third, 128 - rest, 1)
                    x.append(jnp.concatenate([h[:, 128 * rp : 128 * rp + 128], third], axis=1))
                t = [pltpu.roll(v, 4, 0) for v in x]
                first = [jnp.where(half, x[0], t[1]), jnp.where(half, x[2], t[3])]
                second = [jnp.where(half, t[0], x[1]), jnp.where(half, t[2], x[3])]
                for r2, rows in enumerate((first, second)):
                    r = 2 * rp + r2
                    hi, lo = split(jnp.concatenate(rows, axis=0))
                    at = 32 * r + 4 * (k - 3)
                    a_ref[r, at : at + 16, 0:256] = hi
                    a_ref[r, at : at + 16, 256:512] = lo
            held = []
    carried = None
    for r in range(4):
        one = selector(slot_ref[r : r + 1, :])
        out = dot(jnp.concatenate([one, one], axis=1), a_ref[r], NT)
        for t in range(3):
            part = out[:, 128 * t : 128 * t + 128]
            if t == 0 and r > 0:
                part = part + carried
            if t == 2 and r < 3:
                carried = part
                continue
            p_ref[2 * r + t] = part.reshape(p_ref.shape[1:])
        ready(r)


def reorder_kernel(levs, m_ref, o_ref):
    order = m_ref.shape[1]
    levels = order // 4
    block = levels // levs
    x = lax.broadcasted_iota(jnp.int32, (order, order), 0)
    o = lax.broadcasted_iota(jnp.int32, (order, order), 1)
    pick = ((x & 3) * levels + (x >> 2) == o).astype(F32).astype(BF16)
    main = (x & 3) * levels + block * (x >> 5) + ((x >> 2) & 7)
    last = (x & 3) * levels + block * ((x - 256) >> 2) + block - 1
    put = (jnp.where(x < 256, main, last) == o).astype(F32).astype(BF16)
    part = order // 4
    for n in range(2):
        hi, lo = split(m_ref[n])
        rest = (m_ref[n] - hi.astype(F32) - lo.astype(F32)).astype(BF16)
        out = None
        for piece in (hi, lo, rest):
            term = dot(dot(put, piece).astype(BF16), pick, NT)
            out = term if out is None else out + term
        o_ref[n, 0:order] = out[:, 0:128]
        o_ref[n, order : 2 * order] = out[:, 128:256]
        o_ref[n, 2 * order :] = jnp.concatenate([out[part * i : part * i + part, 256:] for i in range(4)], axis=1)


def unpacked(packed):
    part = packed.shape[0] // 9
    third = packed[8 * part :]
    lanes = third.shape[1] // 4
    third = jnp.concatenate([third[:, lanes * i : lanes * i + lanes] for i in range(4)], axis=0)
    return jnp.concatenate([packed[: 4 * part], packed[4 * part : 8 * part], third], axis=1)


def turned_tile(v_ref, j):
    live = (lax.broadcasted_iota(jnp.int32, (128, 512), 1) & 3) < 3
    return jnp.where(live, v_ref[j].reshape(512, 128).T, 0.0)


def unselect(lon, g, tile, last, slot_ref, o_ref):
    for r in range(4):
        rows = jnp.concatenate([tile[32 * r : 32 * r + 32], last[16 * g : 16 * g + 16]], axis=0)
        hi, lo = split(rows)
        one = selector(slot_ref[g, r : r + 1, :])
        out = dot(jnp.concatenate([hi, lo], axis=1), jnp.concatenate([one, one], axis=0))
        at = slice(lon * g, lon * g + lon)
        o_ref[r, 0:8, :, at] = out[0:32, :lon].reshape(8, 4, lon)
        o_ref[r, 8, :, at] = out[32 + 4 * r : 36 + 4 * r, :lon]


PIECES = ((0, 0, 2), (0, 1, 2), (1, None, 4), (2, None, 4), (3, None, 4))


def greet(lat, lev, levs):
    for i in range(1, levs):
        pl.semaphore_signal(
            pltpu.get_barrier_semaphore(), inc=1, device_id=(lat, lax.rem(lev + i, levs)), device_id_type=MESH
        )


def greeted(levs):
    pl.semaphore_wait(pltpu.get_barrier_semaphore(), levs - 1)


def send(src, dst, ssem, rsem, lat, to):
    return pltpu.make_async_remote_copy(
        src_ref=src, dst_ref=dst, send_sem=ssem, recv_sem=rsem, device_id=(lat, to), device_id_type=MESH
    )


def forth_kernel(
    rest, levs, tr_ref, south_ref, north_ref, both_ref, c_ref, slot_ref,
    r_ref, all_ref, g_ref, col_ref, p_ref, a_ref, s1, r1, s2, r2, s3, r3, lsem,
):
    lat, lev = lax.axis_index("lat"), lax.axis_index("lev")
    block = tr_ref.shape[1]
    greet(lat, lev, levs)
    greeted(levs)

    def slot_copy(i):
        to = lax.rem(lev + i, levs)
        return send(slot_ref, all_ref.at[lev], s3.at[i], r3.at[i], lat, to)

    for i in range(1, levs):
        slot_copy(i).start()
    own_slots = pltpu.make_async_copy(slot_ref, all_ref.at[lev], lsem.at[2])
    own_slots.start()

    def level_copy(k, i):
        to = lax.rem(lev + i, levs)
        return send(g_ref.at[to, k], col_ref.at[lev, k], s1.at[k, i], r1.at[k, i], lat, to)

    def level_ready(k):
        for i in range(1, levs):
            level_copy(k, i).start()

    horizontal(tr_ref, south_ref, north_ref, both_ref, g_ref, level_ready)
    own = pltpu.make_async_copy(g_ref.at[lev], col_ref.at[lev], lsem.at[0])
    own.start()
    own.wait()

    @pl.loop(0, block)
    def _(k):
        for i in range(1, levs):
            level_copy(k, i).wait()

    def tiles(r):
        return slice(2 * r, 2 * r + (3 if r == 3 else 2))

    def row_copy(r, i):
        to = lax.rem(lev + i, levs)
        return send(p_ref.at[tiles(r), to, :, 0:3], r_ref.at[tiles(r), :, lev, 0:3], s2.at[r, i], r2.at[r, i], lat, to)

    def row_ready(r):
        for i in range(1, levs):
            row_copy(r, i).start()

    select(rest, col_ref, c_ref, slot_ref, p_ref, a_ref, row_ready)
    own = pltpu.make_async_copy(p_ref.at[:, lev, :, 0:3], r_ref.at[:, :, lev, 0:3], lsem.at[1])
    own.start()
    own.wait()
    for r in range(4):
        for i in range(1, levs):
            row_copy(r, i).wait()
    own_slots.wait()
    for i in range(1, levs):
        slot_copy(i).wait()


def back_kernel(
    rest, levs, order, r_ref, n0, n1, n2, n3, f0, f1, f2, f3, slot_ref,
    o_ref, y_ref, v_ref, w_ref, z_ref, m_ref, move_ref, s1, r1, s2, r2, lsem, msem,
):
    lat, lev = lax.axis_index("lat"), lax.axis_index("lev")
    greet(lat, lev, levs)

    fetches = []
    for n, ref in enumerate((n0, f0, n1, f1, n2, f2, n3, f3)):
        fetches.append(pltpu.make_async_copy(ref, m_ref.at[n], msem.at[n]))
        fetches[n].start()

    def begin(n):
        d, turn, _ = PIECES[n]
        at = lax.rem(lat // 4 - d + 4, 4) * 4
        return at if turn is None else at + lax.rem(lat // 2 + turn, 2) * 2

    def part(n):
        return pl.ds(begin(n), PIECES[n][2])

    def piece_copy(n, i):
        to = lax.rem(lev + i, levs)
        return send(y_ref.at[:, part(n), to, 0:3], v_ref.at[:, lev, part(n), 0:3], s1.at[n, i], r1.at[n, i], lat, to)

    def tile_copy(j, i):
        to = lax.rem(lev + i, levs)
        at = part(len(PIECES) - 1)
        return send(y_ref.at[j, at, to, 0:3], v_ref.at[j, lev, at, 0:3], s2.at[j, i], r2.at[j, i], lat, to)

    def own_copy(n):
        return pltpu.make_async_copy(y_ref.at[:, part(n), lev, 0:3], v_ref.at[:, lev, part(n), 0:3], lsem.at[n])

    to_lane = lax.broadcasted_iota(jnp.int32, (256, 1024), 1)
    from_lane = lax.broadcasted_iota(jnp.int32, (256, 1024), 0) & 127
    wanted = ((to_lane >> 2) & 3) * 32 + (to_lane >> 7) * 4 + (to_lane & 3)
    move_ref[...] = (from_lane == wanted).astype(F32).astype(BF16)

    def place_last(n):
        size = PIECES[n][2]
        many = 4 * size
        hi, lo = split(z_ref[:, part(n)].reshape(8 * many, 128))
        moved = dot(jnp.concatenate([hi, lo], axis=1), move_ref[...])
        group = (lax.broadcasted_iota(jnp.int32, (many, 1024), 1) >> 4) & 7
        x = moved[:many]
        for g in range(1, 8):
            x = jnp.where(group == g, moved[many * g : many * (g + 1)], x)
        for l in range(8):
            y_ref[8, part(n), l] = x[:, 128 * l : 128 * l + 128].reshape(size, 4, 128)

    def mix(n, at):
        tiles = [r_ref[j, n].reshape(4 * levs, 128) for j in range(9)]
        rows = []
        for r in range(4):
            x = jnp.concatenate(tiles[2 * r : 2 * r + 3], axis=1)
            if r > 0:
                x = pltpu.roll(x, 384 - 32 * r, 1)
            rows.append(x[:, :order])
        hi, lo = split(jnp.concatenate(rows, axis=0))
        y = dot(hi, w_ref[0, at], NT) + dot(lo, w_ref[0, at], NT) + dot(hi, w_ref[1, at], NT)
        many = 4 * levs
        quarter = lax.broadcasted_iota(jnp.int32, (many, 128), 1) >> 5
        for half in range(2):
            turns = []
            for r in range(4):
                tile = y[r * many : (r + 1) * many, 128 * half : 128 * half + 128]
                turns.append([tile] + [pltpu.roll(tile, 32 * m, 1) for m in range(1, 4)])
            for m in range(4):
                x = turns[3][(3 - m) % 4]
                for r in range(3):
                    x = jnp.where(quarter == r, turns[r][(r - m) % 4], x)
                y_ref[pl.ds(0, 8), n, 4 * half + m] = x.reshape(8, 4, 128)
        z = jnp.concatenate([y[r * many : (r + 1) * many, 256:] for r in range(4)], axis=1)
        z_ref[:, n] = z.reshape(8, 4, 128)

    arrivals = [8] + list(range(8))
    for n, (d, turn, size) in enumerate(PIECES):
        if turn != 1:
            fetches[2 * d].wait()
            fetches[2 * d + 1].wait()
        for at in range(size):
            hi, lo = split(unpacked(m_ref[2 * d + at % 2, at // 2 + (turn or 0)]))
            w_ref[0, at] = hi
            w_ref[1, at] = lo
        first = lax.rem(lat // 4 - d + 4, 4) * 4

        @pl.loop(0, size)
        def _(at):
            steps = at // 2 if turn is None else turn
            mix(first + lax.rem(lat // 2 + steps, 2) * 2 + lax.rem(lat + at, 2), at)

        place_last(n)
        own_copy(n).start()
        if n == 0:
            greeted(levs)
        if n < len(PIECES) - 1:
            for i in range(1, levs):
                piece_copy(n, i).start()
        else:
            for j in arrivals:
                for i in range(1, levs):
                    tile_copy(j, i).start()

    for n in range(len(PIECES)):
        own_copy(n).wait()
    for n in range(len(PIECES) - 1):
        for i in range(1, levs):
            piece_copy(n, i).wait()
    last = None
    for j in arrivals:
        for i in range(1, levs):
            tile_copy(j, i).wait()
        tile = turned_tile(v_ref, j)
        if j == 8:
            last = tile
        else:
            unselect(128 + rest, j, tile, last, slot_ref, o_ref)


def call(kernel, shape, count, scratch=(), limit=48, extra=None, large=(), **params):
    return pl.pallas_call(
        kernel,
        out_shape=jax.ShapeDtypeStruct(shape, F32) if extra is None else (jax.ShapeDtypeStruct(shape, F32), extra),
        in_specs=[pl.BlockSpec(memory_space=pl.ANY) if n in large else VMEM for n in range(count)],
        out_specs=VMEM if extra is None else (VMEM, VMEM),
        scratch_shapes=list(scratch),
        compiler_params=pltpu.CompilerParams(vmem_limit_bytes=limit << 20, **params),
    )


def body(tracers, zonal, meridional, vertical, route, inverse):
    trac, levs_here, rows, width = tracers.shape
    lats, groups = lax.axis_size("lat"), lax.axis_size("lev")
    levels, _, lon = vertical.shape
    rest = lon - 128
    order = inverse.shape[2]
    own = inverse[0, 0]
    across = lax.ppermute(own, "lat", [(i, i ^ 2) for i in range(lats)])
    turned = jnp.transpose(tracers, (2, 1, 0, 3))
    up = [(i, i + 1) for i in range(lats - 1)]
    down = [(i + 1, i) for i in range(lats - 1)]
    south = lax.ppermute(turned[rows - 3 :], "lat", up)
    edge = jnp.pad(meridional[:, 0], ((0, -levs_here % 4), (0, 0))).reshape(-1, 4, width)
    north = lax.ppermute(
        jnp.concatenate([turned[:3].reshape(3 * levs_here, trac, width), edge], axis=0), "lat", down
    )
    pair = call(functools.partial(reorder_kernel, groups), (2, order * order // 128, 128), 1, limit=12)(jnp.stack([own, across]))
    targets = route[:, :, 0]
    before = jnp.arange(lon)[:, None] < jnp.arange(lon)[None, :]
    same = jnp.logical_and(targets[:, :, None] == targets[:, None, :], before[None])
    place = (targets % groups) * lats + targets // groups
    slots = place * 4 + jnp.sum(same.astype(jnp.int32), axis=1)
    slots = jnp.pad(slots, ((0, 0), (0, 256 - lon)), constant_values=-1)
    v = vertical.reshape(levels, 2, 2, lon)
    courant = jnp.concatenate(
        [v[:, 0, :, :128], v[:, 1, :, :128], v[:, 0, :, 128:], v[:, 1, :, 128:], jnp.zeros((levels, 2, 128 - 2 * rest), F32)],
        axis=-1,
    )
    south, north, pair, courant = lax.optimization_barrier((south, north, pair, courant))
    shifted = [lax.ppermute(pair, "lat", [(i, (i + 4 * d) % lats) for i in range(lats)]) for d in range(1, 4)]
    other = [(i, i ^ 1) for i in range(lats)]
    dma = pltpu.SemaphoreType.DMA
    levels_of = pltpu.VMEM((groups, levs_here, 8, 384), F32)
    received, all_slots = call(
        functools.partial(forth_kernel, rest, groups),
        (9, lats, groups, 4, 128),
        6,
        [
            levels_of,
            levels_of,
            pltpu.VMEM((9, groups, lats, 4, 128), F32),
            pltpu.VMEM((4, 384, 512), BF16),
            dma((levs_here, groups)),
            dma((levs_here, groups)),
            dma((4, groups)),
            dma((4, groups)),
            dma((groups,)),
            dma((groups,)),
            dma((3,)),
        ],
        extra=jax.ShapeDtypeStruct((groups, 4, 256), jnp.int32),
        limit=24,
        collective_id=0,
        has_side_effects=True,
    )(turned, south, north, jnp.stack([zonal, meridional]), courant, slots)
    received, pair, shifted = lax.optimization_barrier((received, pair, shifted))
    far = [lax.ppermute(x, "lat", other) for x in [pair] + shifted]
    whole = call(
        functools.partial(back_kernel, rest, groups, order),
        (4, levs_here, trac, width),
        10,
        [
            pltpu.VMEM((9, lats, groups, 4, 128), F32),
            pltpu.VMEM((9, groups, lats, 4, 128), F32),
            pltpu.VMEM((2, 4, order, order), BF16),
            pltpu.VMEM((groups, lats, 4, 128), F32),
            pltpu.VMEM((8,) + pair.shape, F32),
            pltpu.VMEM((256, 1024), BF16),
            dma((len(PIECES) - 1, groups)),
            dma((len(PIECES) - 1, groups)),
            dma((9, groups)),
            dma((9, groups)),
            dma((len(PIECES),)),
            dma((8,)),
        ],
        large=range(1, 9),
        limit=28,
        collective_id=1,
        has_side_effects=True,
    )(received, pair, *shifted, *far, all_slots)
    return jnp.transpose(whole, (2, 1, 0, 3)) - tracers


def solution(mesh):
    in_specs = (
        P(None, "lev", "lat", None),
        P("lev", "lat", None),
        P("lev", "lat", None),
        P(None, "lat", "lev"),
        P("lat", "lev", None),
        P("lat", "lev", None, None),
    )
    out_specs = P(None, "lev", "lat", None)
    return jax.shard_map(body, mesh=mesh, in_specs=in_specs, out_specs=out_specs, check_vma=False)
```

```python
import functools
import jax
import jax.numpy as jnp
from jax import lax
from jax.experimental import pallas as pl
from jax.experimental.pallas import tpu as pltpu
from jax.sharding import PartitionSpec as P

MESH = pl.DeviceIdType.MESH
F32 = jnp.float32
BF16 = jnp.bfloat16
VMEM = pl.BlockSpec(memory_space=pltpu.VMEM)
NT = (((1,), (1,)), ((), ()))
NN = (((1,), (0,)), ((), ()))


def dot(a, b, dims=NN):
    return lax.dot_general(a, b, dims, preferred_element_type=F32)


def split(x):
    hi = x.astype(BF16)
    lo = (x - hi.astype(F32)).astype(BF16)
    return hi, lo


def flux(c, e, s_low, s_here, k_low, k_here):
    up = c >= 0.0
    a = jnp.abs(c)
    s = jnp.where(up, -s_low, s_here)
    k = jnp.where(up, k_low, k_here)
    return c * (e + (0.5 * a) * (s + (1.0 - (2.0 / 3.0) * a) * k))


def face(q_m2, q_m1, q_0, q_p1):
    return (7.0 / 12.0) * (q_m1 + q_0) - (1.0 / 12.0) * (q_m2 + q_p1)


def horizontal(tr_ref, south_ref, north_ref, both_ref, g_ref, ready):
    lat = lax.axis_index("lat")
    last = lax.axis_size("lat") - 1
    width = tr_ref.shape[3]
    groups = g_ref.shape[0]
    lon = width // groups
    sub = lax.broadcasted_iota(jnp.int32, (8, width), 0) < 4
    ext = -(-width // 128) * 128
    spare = ext - width
    half = spare // 3
    ksouth = (lat > 0).astype(F32)
    knorth = (lat < last).astype(F32)

    def swap(x):
        return pltpu.roll(x, 4, 0)

    def extend(x):
        return jnp.concatenate([x, x[:, :half], x[:, width - (spare - half):]], axis=1)

    def rolled(x, n):
        return pltpu.roll(x, n % ext, 1)

    def level(k, carry):
        row = [tr_ref[r, k] for r in range(4)]
        low = [south_ref[r, k] * ksouth for r in range(3)]
        high = [north_ref[r * tr_ref.shape[1] + k] * knorth for r in range(3)]
        pair = lambda a, b: jnp.concatenate([a, b], axis=0)
        q = [
            pair(low[0], low[0]),
            pair(low[1], low[2]),
            pair(row[0], row[1]),
            pair(row[2], row[3]),
            pair(high[0], high[1]),
            pair(high[2], high[2]),
        ]
        sq = [swap(x) for x in q]
        e = [face(q[p - 1], jnp.where(sub, sq[p - 1], sq[p]), q[p], jnp.where(sub, sq[p], sq[p + 1])) for p in range(1, 5)]
        se = [swap(x) for x in e]
        s, kk = [], []
        for p in range(4):
            right = jnp.where(sub, se[p], se[min(p + 1, 3)])
            s.append(right - e[p])
            kk.append(6.0 * q[p + 1] - 3.0 * (e[p] + right))
        ss = [swap(x) for x in s]
        sk = [swap(x) for x in kk]
        m = both_ref[1, k]
        zero = jnp.zeros((8, width), F32)
        m0 = jnp.where(sub, m[0:1] * ksouth, m[1:2])
        m1 = jnp.where(sub, m[2:3], m[3:4])
        m2 = north_ref[3 * tr_ref.shape[1] + k // 4, pl.ds(k % 4, 1), :] * knorth + zero
        f = []
        for i, c in enumerate((m0, m1, m2)):
            p = i + 1
            f.append(
                flux(c, e[p], jnp.where(sub, ss[p - 1], ss[p]), s[p], jnp.where(sub, sk[p - 1], sk[p]), kk[p])
            )
        sf = [swap(x) for x in f]
        z = both_ref[0, k]
        out = []
        for p in range(2):
            lat_change = f[p] - jnp.where(sub, sf[p], sf[p + 1])
            x = extend(q[p + 2])
            c = extend(jnp.where(sub, z[2 * p : 2 * p + 1], z[2 * p + 1 : 2 * p + 2]))
            le = face(rolled(x, 2), rolled(x, 1), x, rolled(x, -1))
            right = rolled(le, -1)
            ls = right - le
            lk = 6.0 * x - 3.0 * (le + right)
            lf = flux(c, le, rolled(ls, 1), ls, rolled(lk, 1), lk)
            lon_change = lf - rolled(lf, -1)
            out.append(q[p + 2] + lon_change[:, :width] + lat_change)
        rest = lon - 128
        pad = jnp.zeros((8, 128 - 2 * rest), F32)
        for g in range(groups):
            o = g * lon
            g_ref[g, k] = jnp.concatenate(
                [
                    out[0][:, o : o + 128],
                    out[1][:, o : o + 128],
                    out[0][:, o + 128 : o + lon],
                    out[1][:, o + 128 : o + lon],
                    pad,
                ],
                axis=1,
            )
        ready(k)
        return carry

    lax.fori_loop(0, tr_ref.shape[1], level, 0)


def selector(slots):
    ids = lax.broadcasted_iota(jnp.int32, (512, 256), 0)
    return (ids == slots).astype(F32).astype(BF16)


def select(rest, g_ref, c_ref, slot_ref, p_ref, a_ref, ready):
    block = g_ref.shape[1]
    levels = g_ref.shape[0] * block
    sub = lax.broadcasted_iota(jnp.int32, (8, 384), 0) < 4
    half = lax.broadcasted_iota(jnp.int32, (8, 256), 0) < 4
    zero = jnp.zeros((8, 384), F32)
    for r in range(4):
        if r > 0:
            a_ref[r, 0 : 32 * r, :] = jnp.zeros((32 * r, 512), BF16)
        if r < 3:
            a_ref[r, 32 * r + 288 : 384, :] = jnp.zeros((96 - 32 * r, 512), BF16)

    def q(k):
        return g_ref[k // block, k % block] if 0 <= k < levels else zero

    def e_at(k):
        return face(q(k - 2), q(k - 1), q(k), q(k + 1))

    left = e_at(0)
    f_here = zero
    held = []
    right = e_at(1)
    s, kk = right - left, 6.0 * q(0) - 3.0 * (left + right)
    for k in range(levels):
        if k + 1 < levels:
            nxt = e_at(k + 2)
            s1, k1 = nxt - right, 6.0 * q(k + 1) - 3.0 * (right + nxt)
            c = jnp.where(sub, c_ref[k + 1, 0:1, :], c_ref[k + 1, 1:2, :])
            f_next = flux(c, right, s, s1, kk, k1)
            right, s, kk = nxt, s1, k1
        else:
            f_next = zero
        held.append(q(k) + f_here - f_next)
        f_here = f_next
        if k % 4 == 3:
            for rp in range(2):
                x = []
                for h in held:
                    third = h[:, 256:384]
                    if rp == 1:
                        third = pltpu.roll(third, 128 - rest, 1)
                    x.append(jnp.concatenate([h[:, 128 * rp : 128 * rp + 128], third], axis=1))
                t = [pltpu.roll(v, 4, 0) for v in x]
                first = [jnp.where(half, x[0], t[1]), jnp.where(half, x[2], t[3])]
                second = [jnp.where(half, t[0], x[1]), jnp.where(half, t[2], x[3])]
                for r2, rows in enumerate((first, second)):
                    r = 2 * rp + r2
                    hi, lo = split(jnp.concatenate(rows, axis=0))
                    at = 32 * r + 4 * (k - 3)
                    a_ref[r, at : at + 16, 0:256] = hi
                    a_ref[r, at : at + 16, 256:512] = lo
            held = []
    carried = None
    for r in range(4):
        one = selector(slot_ref[r : r + 1, :])
        out = dot(jnp.concatenate([one, one], axis=1), a_ref[r], NT)
        for t in range(3):
            part = out[:, 128 * t : 128 * t + 128]
            if t == 0 and r > 0:
                part = part + carried
            if t == 2 and r < 3:
                carried = part
                continue
            p_ref[2 * r + t] = part.reshape(p_ref.shape[1:])
        ready(r)


def reorder_kernel(levs, m_ref, o_ref):
    order = m_ref.shape[1]
    levels = order // 4
    block = levels // levs
    x = lax.broadcasted_iota(jnp.int32, (order, order), 0)
    o = lax.broadcasted_iota(jnp.int32, (order, order), 1)
    pick = ((x & 3) * levels + (x >> 2) == o).astype(F32).astype(BF16)
    main = (x & 3) * levels + block * (x >> 5) + ((x >> 2) & 7)
    last = (x & 3) * levels + block * ((x - 256) >> 2) + block - 1
    put = (jnp.where(x < 256, main, last) == o).astype(F32).astype(BF16)
    part = order // 4
    for n in range(2):
        hi, lo = split(m_ref[n])
        rest = (m_ref[n] - hi.astype(F32) - lo.astype(F32)).astype(BF16)
        out = None
        for piece in (hi, lo, rest):
            term = dot(dot(put, piece).astype(BF16), pick, NT)
            out = term if out is None else out + term
        o_ref[n, 0:order] = out[:, 0:128]
        o_ref[n, order : 2 * order] = out[:, 128:256]
        o_ref[n, 2 * order :] = jnp.concatenate([out[part * i : part * i + part, 256:] for i in range(4)], axis=1)


def unpacked(packed):
    part = packed.shape[0] // 9
    third = packed[8 * part :]
    lanes = third.shape[1] // 4
    third = jnp.concatenate([third[:, lanes * i : lanes * i + lanes] for i in range(4)], axis=0)
    return jnp.concatenate([packed[: 4 * part], packed[4 * part : 8 * part], third], axis=1)


def turned_tile(v_ref, j):
    live = (lax.broadcasted_iota(jnp.int32, (128, 512), 1) & 3) < 3
    return jnp.where(live, v_ref[j].reshape(512, 128).T, 0.0)


def unselect(lon, g, tile, last, slot_ref, o_ref):
    for r in range(4):
        rows = jnp.concatenate([tile[32 * r : 32 * r + 32], last[16 * g : 16 * g + 16]], axis=0)
        hi, lo = split(rows)
        one = selector(slot_ref[g, r : r + 1, :])
        out = dot(jnp.concatenate([hi, lo], axis=1), jnp.concatenate([one, one], axis=0))
        at = slice(lon * g, lon * g + lon)
        for t in range(4):
            for k in range(8):
                o_ref[t, k, r : r + 1, at] = out[4 * k + t : 4 * k + t + 1, :lon]
            o_ref[t, 8, r : r + 1, at] = out[32 + 4 * r + t : 33 + 4 * r + t, :lon]


PIECES = ((0, 0, 2), (0, 1, 2), (1, None, 4), (2, None, 4), (3, None, 4))


def greet(lat, lev, levs):
    for i in range(1, levs):
        pl.semaphore_signal(
            pltpu.get_barrier_semaphore(), inc=1, device_id=(lat, lax.rem(lev + i, levs)), device_id_type=MESH
        )


def greeted(levs):
    pl.semaphore_wait(pltpu.get_barrier_semaphore(), levs - 1)


def send(src, dst, ssem, rsem, lat, to):
    return pltpu.make_async_remote_copy(
        src_ref=src, dst_ref=dst, send_sem=ssem, recv_sem=rsem, device_id=(lat, to), device_id_type=MESH
    )


def forth_kernel(
    rest, levs, tr_ref, south_ref, north_ref, both_ref, c_ref, slot_ref,
    r_ref, all_ref, g_ref, col_ref, p_ref, a_ref, s1, r1, s2, r2, s3, r3, lsem,
):
    lat, lev = lax.axis_index("lat"), lax.axis_index("lev")
    block = tr_ref.shape[1]
    greet(lat, lev, levs)
    greeted(levs)

    def slot_copy(i):
        to = lax.rem(lev + i, levs)
        return send(slot_ref, all_ref.at[lev], s3.at[i], r3.at[i], lat, to)

    for i in range(1, levs):
        slot_copy(i).start()
    own_slots = pltpu.make_async_copy(slot_ref, all_ref.at[lev], lsem.at[2])
    own_slots.start()

    def level_copy(k, i):
        to = lax.rem(lev + i, levs)
        return send(g_ref.at[to, k], col_ref.at[lev, k], s1.at[k, i], r1.at[k, i], lat, to)

    def level_ready(k):
        for i in range(1, levs):
            level_copy(k, i).start()

    horizontal(tr_ref, south_ref, north_ref, both_ref, g_ref, level_ready)
    own = pltpu.make_async_copy(g_ref.at[lev], col_ref.at[lev], lsem.at[0])
    own.start()
    own.wait()

    @pl.loop(0, block)
    def _(k):
        for i in range(1, levs):
            level_copy(k, i).wait()

    def tiles(r):
        return slice(2 * r, 2 * r + (3 if r == 3 else 2))

    def row_copy(r, i):
        to = lax.rem(lev + i, levs)
        return send(p_ref.at[tiles(r), to, :, 0:3], r_ref.at[tiles(r), :, lev, 0:3], s2.at[r, i], r2.at[r, i], lat, to)

    def row_ready(r):
        for i in range(1, levs):
            row_copy(r, i).start()

    select(rest, col_ref, c_ref, slot_ref, p_ref, a_ref, row_ready)
    own = pltpu.make_async_copy(p_ref.at[:, lev, :, 0:3], r_ref.at[:, :, lev, 0:3], lsem.at[1])
    own.start()
    own.wait()
    for r in range(4):
        for i in range(1, levs):
            row_copy(r, i).wait()
    own_slots.wait()
    for i in range(1, levs):
        slot_copy(i).wait()


def back_kernel(
    rest, levs, order, r_ref, n0, n1, n2, n3, f0, f1, f2, f3, slot_ref,
    o_ref, y_ref, v_ref, w_ref, z_ref, m_ref, move_ref, s1, r1, s2, r2, lsem, msem,
):
    lat, lev = lax.axis_index("lat"), lax.axis_index("lev")
    greet(lat, lev, levs)

    fetches = []
    for n, ref in enumerate((n0, f0, n1, f1, n2, f2, n3, f3)):
        fetches.append(pltpu.make_async_copy(ref, m_ref.at[n], msem.at[n]))
        fetches[n].start()

    def begin(n):
        d, turn, _ = PIECES[n]
        at = lax.rem(lat // 4 - d + 4, 4) * 4
        return at if turn is None else at + lax.rem(lat // 2 + turn, 2) * 2

    def part(n):
        return pl.ds(begin(n), PIECES[n][2])

    def piece_copy(n, i):
        to = lax.rem(lev + i, levs)
        return send(y_ref.at[:, part(n), to, 0:3], v_ref.at[:, lev, part(n), 0:3], s1.at[n, i], r1.at[n, i], lat, to)

    def tile_copy(j, i):
        to = lax.rem(lev + i, levs)
        at = part(len(PIECES) - 1)
        return send(y_ref.at[j, at, to, 0:3], v_ref.at[j, lev, at, 0:3], s2.at[j, i], r2.at[j, i], lat, to)

    def own_copy(n):
        return pltpu.make_async_copy(y_ref.at[:, part(n), lev, 0:3], v_ref.at[:, lev, part(n), 0:3], lsem.at[n])

    to_lane = lax.broadcasted_iota(jnp.int32, (256, 1024), 1)
    from_lane = lax.broadcasted_iota(jnp.int32, (256, 1024), 0) & 127
    wanted = ((to_lane >> 2) & 3) * 32 + (to_lane >> 7) * 4 + (to_lane & 3)
    move_ref[...] = (from_lane == wanted).astype(F32).astype(BF16)

    def place_last(n):
        size = PIECES[n][2]
        many = 4 * size
        hi, lo = split(z_ref[:, part(n)].reshape(8 * many, 128))
        moved = dot(jnp.concatenate([hi, lo], axis=1), move_ref[...])
        group = (lax.broadcasted_iota(jnp.int32, (many, 1024), 1) >> 4) & 7
        x = moved[:many]
        for g in range(1, 8):
            x = jnp.where(group == g, moved[many * g : many * (g + 1)], x)
        for l in range(8):
            y_ref[8, part(n), l] = x[:, 128 * l : 128 * l + 128].reshape(size, 4, 128)

    def mix(n, at):
        tiles = [r_ref[j, n].reshape(4 * levs, 128) for j in range(9)]
        rows = []
        for r in range(4):
            x = jnp.concatenate(tiles[2 * r : 2 * r + 3], axis=1)
            if r > 0:
                x = pltpu.roll(x, 384 - 32 * r, 1)
            rows.append(x[:, :order])
        hi, lo = split(jnp.concatenate(rows, axis=0))
        y = dot(hi, w_ref[0, at], NT) + dot(lo, w_ref[0, at], NT) + dot(hi, w_ref[1, at], NT)
        many = 4 * levs
        quarter = lax.broadcasted_iota(jnp.int32, (many, 128), 1) >> 5
        for half in range(2):
            turns = []
            for r in range(4):
                tile = y[r * many : (r + 1) * many, 128 * half : 128 * half + 128]
                turns.append([tile] + [pltpu.roll(tile, 32 * m, 1) for m in range(1, 4)])
            for m in range(4):
                x = turns[3][(3 - m) % 4]
                for r in range(3):
                    x = jnp.where(quarter == r, turns[r][(r - m) % 4], x)
                y_ref[pl.ds(0, 8), n, 4 * half + m] = x.reshape(8, 4, 128)
        z = jnp.concatenate([y[r * many : (r + 1) * many, 256:] for r in range(4)], axis=1)
        z_ref[:, n] = z.reshape(8, 4, 128)

    arrivals = [8] + list(range(8))
    for n, (d, turn, size) in enumerate(PIECES):
        if turn != 1:
            fetches[2 * d].wait()
            fetches[2 * d + 1].wait()
        for at in range(size):
            hi, lo = split(unpacked(m_ref[2 * d + at % 2, at // 2 + (turn or 0)]))
            w_ref[0, at] = hi
            w_ref[1, at] = lo
        first = lax.rem(lat // 4 - d + 4, 4) * 4

        @pl.loop(0, size)
        def _(at):
            steps = at // 2 if turn is None else turn
            mix(first + lax.rem(lat // 2 + steps, 2) * 2 + lax.rem(lat + at, 2), at)

        place_last(n)
        own_copy(n).start()
        if n == 0:
            greeted(levs)
        if n < len(PIECES) - 1:
            for i in range(1, levs):
                piece_copy(n, i).start()
        else:
            for j in arrivals:
                for i in range(1, levs):
                    tile_copy(j, i).start()

    for n in range(len(PIECES)):
        own_copy(n).wait()
    for n in range(len(PIECES) - 1):
        for i in range(1, levs):
            piece_copy(n, i).wait()
    last = None
    for j in arrivals:
        for i in range(1, levs):
            tile_copy(j, i).wait()
        tile = turned_tile(v_ref, j)
        if j == 8:
            last = tile
        else:
            unselect(128 + rest, j, tile, last, slot_ref, o_ref)


def call(kernel, shape, count, scratch=(), limit=48, extra=None, large=(), **params):
    return pl.pallas_call(
        kernel,
        out_shape=jax.ShapeDtypeStruct(shape, F32) if extra is None else (jax.ShapeDtypeStruct(shape, F32), extra),
        in_specs=[pl.BlockSpec(memory_space=pl.ANY) if n in large else VMEM for n in range(count)],
        out_specs=VMEM if extra is None else (VMEM, VMEM),
        scratch_shapes=list(scratch),
        compiler_params=pltpu.CompilerParams(vmem_limit_bytes=limit << 20, **params),
    )


def body(tracers, zonal, meridional, vertical, route, inverse):
    trac, levs_here, rows, width = tracers.shape
    lats, groups = lax.axis_size("lat"), lax.axis_size("lev")
    levels, _, lon = vertical.shape
    rest = lon - 128
    order = inverse.shape[2]
    own = inverse[0, 0]
    across = lax.ppermute(own, "lat", [(i, i ^ 2) for i in range(lats)])
    turned = jnp.transpose(tracers, (2, 1, 0, 3))
    up = [(i, i + 1) for i in range(lats - 1)]
    down = [(i + 1, i) for i in range(lats - 1)]
    south = lax.ppermute(turned[rows - 3 :], "lat", up)
    edge = jnp.pad(meridional[:, 0], ((0, -levs_here % 4), (0, 0))).reshape(-1, 4, width)
    north = lax.ppermute(
        jnp.concatenate([turned[:3].reshape(3 * levs_here, trac, width), edge], axis=0), "lat", down
    )
    pair = call(functools.partial(reorder_kernel, groups), (2, order * order // 128, 128), 1, limit=12)(jnp.stack([own, across]))
    targets = route[:, :, 0]
    before = jnp.arange(lon)[:, None] < jnp.arange(lon)[None, :]
    same = jnp.logical_and(targets[:, :, None] == targets[:, None, :], before[None])
    place = (targets % groups) * lats + targets // groups
    slots = place * 4 + jnp.sum(same.astype(jnp.int32), axis=1)
    slots = jnp.pad(slots, ((0, 0), (0, 256 - lon)), constant_values=-1)
    v = vertical.reshape(levels, 2, 2, lon)
    courant = jnp.concatenate(
        [v[:, 0, :, :128], v[:, 1, :, :128], v[:, 0, :, 128:], v[:, 1, :, 128:], jnp.zeros((levels, 2, 128 - 2 * rest), F32)],
        axis=-1,
    )
    both = jnp.stack([zonal, meridional])
    south, north, pair, courant, both = lax.optimization_barrier((south, north, pair, courant, both))
    shifted = [lax.ppermute(pair, "lat", [(i, (i + 4 * d) % lats) for i in range(lats)]) for d in range(1, 4)]
    other = [(i, i ^ 1) for i in range(lats)]
    dma = pltpu.SemaphoreType.DMA
    levels_of = pltpu.VMEM((groups, levs_here, 8, 384), F32)
    received, all_slots = call(
        functools.partial(forth_kernel, rest, groups),
        (9, lats, groups, 4, 128),
        6,
        [
            levels_of,
            levels_of,
            pltpu.VMEM((9, groups, lats, 4, 128), F32),
            pltpu.VMEM((4, 384, 512), BF16),
            dma((levs_here, groups)),
            dma((levs_here, groups)),
            dma((4, groups)),
            dma((4, groups)),
            dma((groups,)),
            dma((groups,)),
            dma((3,)),
        ],
        extra=jax.ShapeDtypeStruct((groups, 4, 256), jnp.int32),
        limit=24,
        collective_id=0,
        has_side_effects=True,
    )(turned, south, north, both, courant, slots)
    received, pair, shifted = lax.optimization_barrier((received, pair, shifted))
    far = [lax.ppermute(x, "lat", other) for x in [pair] + shifted]
    whole = call(
        functools.partial(back_kernel, rest, groups, order),
        (trac, levs_here, rows, width),
        10,
        [
            pltpu.VMEM((9, lats, groups, 4, 128), F32),
            pltpu.VMEM((9, groups, lats, 4, 128), F32),
            pltpu.VMEM((2, 4, order, order), BF16),
            pltpu.VMEM((groups, lats, 4, 128), F32),
            pltpu.VMEM((8,) + pair.shape, F32),
            pltpu.VMEM((256, 1024), BF16),
            dma((len(PIECES) - 1, groups)),
            dma((len(PIECES) - 1, groups)),
            dma((9, groups)),
            dma((9, groups)),
            dma((len(PIECES),)),
            dma((8,)),
        ],
        large=range(1, 9),
        limit=28,
        collective_id=1,
        has_side_effects=True,
    )(received, pair, *shifted, *far, all_slots)
    return whole - tracers


def solution(mesh):
    in_specs = (
        P(None, "lev", "lat", None),
        P("lev", "lat", None),
        P("lev", "lat", None),
        P(None, "lat", "lev"),
        P("lat", "lev", None),
        P("lat", "lev", None, None),
    )
    out_specs = P(None, "lev", "lat", None)
    return jax.shard_map(body, mesh=mesh, in_specs=in_specs, out_specs=out_specs, check_vma=False)
```

```python
import functools
import jax
import jax.numpy as jnp
from jax import lax
from jax.experimental import pallas as pl
from jax.experimental.pallas import tpu as pltpu
from jax.sharding import PartitionSpec as P

MESH = pl.DeviceIdType.MESH
F32 = jnp.float32
BF16 = jnp.bfloat16
VMEM = pl.BlockSpec(memory_space=pltpu.VMEM)
NT = (((1,), (1,)), ((), ()))
NN = (((1,), (0,)), ((), ()))


def dot(a, b, dims=NN):
    return lax.dot_general(a, b, dims, preferred_element_type=F32)


def split(x):
    hi = x.astype(BF16)
    lo = (x - hi.astype(F32)).astype(BF16)
    return hi, lo


def flux(c, e, s_low, s_here, k_low, k_here):
    up = c >= 0.0
    a = jnp.abs(c)
    s = jnp.where(up, -s_low, s_here)
    k = jnp.where(up, k_low, k_here)
    return c * (e + (0.5 * a) * (s + (1.0 - (2.0 / 3.0) * a) * k))


def face(q_m2, q_m1, q_0, q_p1):
    return (7.0 / 12.0) * (q_m1 + q_0) - (1.0 / 12.0) * (q_m2 + q_p1)


def horizontal(tr_ref, south_ref, north_ref, both_ref, g_ref, ready):
    lat = lax.axis_index("lat")
    last = lax.axis_size("lat") - 1
    width = tr_ref.shape[3]
    groups = g_ref.shape[0]
    lon = width // groups
    sub = lax.broadcasted_iota(jnp.int32, (8, width), 0) < 4
    ext = -(-width // 128) * 128
    spare = ext - width
    half = spare // 3
    ksouth = (lat > 0).astype(F32)
    knorth = (lat < last).astype(F32)

    def swap(x):
        return pltpu.roll(x, 4, 0)

    def extend(x):
        return jnp.concatenate([x, x[:, :half], x[:, width - (spare - half):]], axis=1)

    def rolled(x, n):
        return pltpu.roll(x, n % ext, 1)

    def level(k, carry):
        row = [tr_ref[r, k] for r in range(4)]
        low = [south_ref[r, k] * ksouth for r in range(3)]
        high = [north_ref[r * tr_ref.shape[1] + k] * knorth for r in range(3)]
        pair = lambda a, b: jnp.concatenate([a, b], axis=0)
        q = [
            pair(low[0], low[0]),
            pair(low[1], low[2]),
            pair(row[0], row[1]),
            pair(row[2], row[3]),
            pair(high[0], high[1]),
            pair(high[2], high[2]),
        ]
        sq = [swap(x) for x in q]
        e = [face(q[p - 1], jnp.where(sub, sq[p - 1], sq[p]), q[p], jnp.where(sub, sq[p], sq[p + 1])) for p in range(1, 5)]
        se = [swap(x) for x in e]
        s, kk = [], []
        for p in range(4):
            right = jnp.where(sub, se[p], se[min(p + 1, 3)])
            s.append(right - e[p])
            kk.append(6.0 * q[p + 1] - 3.0 * (e[p] + right))
        ss = [swap(x) for x in s]
        sk = [swap(x) for x in kk]
        m = both_ref[1, k]
        zero = jnp.zeros((8, width), F32)
        m0 = jnp.where(sub, m[0:1] * ksouth, m[1:2])
        m1 = jnp.where(sub, m[2:3], m[3:4])
        m2 = north_ref[3 * tr_ref.shape[1] + k // 4, pl.ds(k % 4, 1), :] * knorth + zero
        f = []
        for i, c in enumerate((m0, m1, m2)):
            p = i + 1
            f.append(
                flux(c, e[p], jnp.where(sub, ss[p - 1], ss[p]), s[p], jnp.where(sub, sk[p - 1], sk[p]), kk[p])
            )
        sf = [swap(x) for x in f]
        z = both_ref[0, k]
        out = []
        for p in range(2):
            lat_change = f[p] - jnp.where(sub, sf[p], sf[p + 1])
            x = extend(q[p + 2])
            c = extend(jnp.where(sub, z[2 * p : 2 * p + 1], z[2 * p + 1 : 2 * p + 2]))
            le = face(rolled(x, 2), rolled(x, 1), x, rolled(x, -1))
            right = rolled(le, -1)
            ls = right - le
            lk = 6.0 * x - 3.0 * (le + right)
            lf = flux(c, le, rolled(ls, 1), ls, rolled(lk, 1), lk)
            lon_change = lf - rolled(lf, -1)
            out.append(q[p + 2] + lon_change[:, :width] + lat_change)
        rest = lon - 128
        pad = jnp.zeros((8, 128 - 2 * rest), F32)
        for g in range(groups):
            o = g * lon
            g_ref[g, k] = jnp.concatenate(
                [
                    out[0][:, o : o + 128],
                    out[1][:, o : o + 128],
                    out[0][:, o + 128 : o + lon],
                    out[1][:, o + 128 : o + lon],
                    pad,
                ],
                axis=1,
            )
        ready(k)
        return carry

    lax.fori_loop(0, tr_ref.shape[1], level, 0)


def selector(slots):
    ids = lax.broadcasted_iota(jnp.int32, (512, 256), 0)
    return (ids == slots).astype(F32).astype(BF16)


def select(rest, g_ref, c_ref, slot_ref, p_ref, a_ref, ready):
    block = g_ref.shape[1]
    levels = g_ref.shape[0] * block
    sub = lax.broadcasted_iota(jnp.int32, (8, 384), 0) < 4
    half = lax.broadcasted_iota(jnp.int32, (8, 256), 0) < 4
    zero = jnp.zeros((8, 384), F32)
    for r in range(4):
        if r > 0:
            a_ref[r, 0 : 32 * r, :] = jnp.zeros((32 * r, 512), BF16)
        if r < 3:
            a_ref[r, 32 * r + 288 : 384, :] = jnp.zeros((96 - 32 * r, 512), BF16)

    def q(k):
        return g_ref[k // block, k % block] if 0 <= k < levels else zero

    def e_at(k):
        return face(q(k - 2), q(k - 1), q(k), q(k + 1))

    left = e_at(0)
    f_here = zero
    held = []
    right = e_at(1)
    s, kk = right - left, 6.0 * q(0) - 3.0 * (left + right)
    for k in range(levels):
        if k + 1 < levels:
            nxt = e_at(k + 2)
            s1, k1 = nxt - right, 6.0 * q(k + 1) - 3.0 * (right + nxt)
            c = jnp.where(sub, c_ref[k + 1, 0:1, :], c_ref[k + 1, 1:2, :])
            f_next = flux(c, right, s, s1, kk, k1)
            right, s, kk = nxt, s1, k1
        else:
            f_next = zero
        held.append(q(k) + f_here - f_next)
        f_here = f_next
        if k % 4 == 3:
            for rp in range(2):
                x = []
                for h in held:
                    third = h[:, 256:384]
                    if rp == 1:
                        third = pltpu.roll(third, 128 - rest, 1)
                    x.append(jnp.concatenate([h[:, 128 * rp : 128 * rp + 128], third], axis=1))
                t = [pltpu.roll(v, 4, 0) for v in x]
                first = [jnp.where(half, x[0], t[1]), jnp.where(half, x[2], t[3])]
                second = [jnp.where(half, t[0], x[1]), jnp.where(half, t[2], x[3])]
                for r2, rows in enumerate((first, second)):
                    r = 2 * rp + r2
                    hi, lo = split(jnp.concatenate(rows, axis=0))
                    at = 32 * r + 4 * (k - 3)
                    a_ref[r, at : at + 16, 0:256] = hi
                    a_ref[r, at : at + 16, 256:512] = lo
            held = []
    carried = None
    for r in range(4):
        one = selector(slot_ref[r : r + 1, :])
        out = dot(jnp.concatenate([one, one], axis=1), a_ref[r], NT)
        for t in range(3):
            part = out[:, 128 * t : 128 * t + 128]
            if t == 0 and r > 0:
                part = part + carried
            if t == 2 and r < 3:
                carried = part
                continue
            p_ref[2 * r + t] = part.reshape(p_ref.shape[1:])
        ready(r)


def reorder_kernel(levs, m_ref, o_ref):
    order = m_ref.shape[1]
    levels = order // 4
    block = levels // levs
    x = lax.broadcasted_iota(jnp.int32, (order, order), 0)
    o = lax.broadcasted_iota(jnp.int32, (order, order), 1)
    pick = ((x & 3) * levels + (x >> 2) == o).astype(F32).astype(BF16)
    main = (x & 3) * levels + block * (x >> 5) + ((x >> 2) & 7)
    last = (x & 3) * levels + block * ((x - 256) >> 2) + block - 1
    put = (jnp.where(x < 256, main, last) == o).astype(F32).astype(BF16)
    part = order // 4
    for n in range(2):
        hi, lo = split(m_ref[n])
        rest = (m_ref[n] - hi.astype(F32) - lo.astype(F32)).astype(BF16)
        out = None
        for piece in (hi, lo, rest):
            term = dot(dot(put, piece).astype(BF16), pick, NT)
            out = term if out is None else out + term
        o_ref[n, 0:order] = out[:, 0:128]
        o_ref[n, order : 2 * order] = out[:, 128:256]
        o_ref[n, 2 * order :] = jnp.concatenate([out[part * i : part * i + part, 256:] for i in range(4)], axis=1)


def unpacked(packed):
    part = packed.shape[0] // 9
    third = packed[8 * part :]
    lanes = third.shape[1] // 4
    third = jnp.concatenate([third[:, lanes * i : lanes * i + lanes] for i in range(4)], axis=0)
    return jnp.concatenate([packed[: 4 * part], packed[4 * part : 8 * part], third], axis=1)


def turned_tile(v_ref, j):
    live = (lax.broadcasted_iota(jnp.int32, (128, 512), 1) & 3) < 3
    return jnp.where(live, v_ref[j].reshape(512, 128).T, 0.0)


def unselect(lon, g, tile, last, slot_ref, o_ref):
    for r in range(4):
        rows = jnp.concatenate([tile[32 * r : 32 * r + 32], last[16 * g : 16 * g + 16]], axis=0)
        hi, lo = split(rows)
        one = selector(slot_ref[g, r : r + 1, :])
        out = dot(jnp.concatenate([hi, lo], axis=1), jnp.concatenate([one, one], axis=0))
        at = slice(lon * g, lon * g + lon)
        for t in range(4):
            for k in range(8):
                o_ref[t, k, r : r + 1, at] = out[4 * k + t : 4 * k + t + 1, :lon]
            o_ref[t, 8, r : r + 1, at] = out[32 + 4 * r + t : 33 + 4 * r + t, :lon]


PIECES = ((0, 0, 0, 1), (0, 0, 1, 1), (0, 1, None, 2), (1, None, None, 4), (2, None, None, 4), (3, None, None, 4))


def greet(lat, lev, levs):
    for i in range(1, levs):
        pl.semaphore_signal(
            pltpu.get_barrier_semaphore(), inc=1, device_id=(lat, lax.rem(lev + i, levs)), device_id_type=MESH
        )


def greeted(levs):
    pl.semaphore_wait(pltpu.get_barrier_semaphore(), levs - 1)


def send(src, dst, ssem, rsem, lat, to):
    return pltpu.make_async_remote_copy(
        src_ref=src, dst_ref=dst, send_sem=ssem, recv_sem=rsem, device_id=(lat, to), device_id_type=MESH
    )


def forth_kernel(
    rest, levs, tr_ref, south_ref, north_ref, both_ref, c_ref, slot_ref,
    r_ref, all_ref, g_ref, col_ref, p_ref, a_ref, s1, r1, s2, r2, s3, r3, lsem,
):
    lat, lev = lax.axis_index("lat"), lax.axis_index("lev")
    block = tr_ref.shape[1]
    greet(lat, lev, levs)
    greeted(levs)

    def slot_copy(i):
        to = lax.rem(lev + i, levs)
        return send(slot_ref, all_ref.at[lev], s3.at[i], r3.at[i], lat, to)

    for i in range(1, levs):
        slot_copy(i).start()
    own_slots = pltpu.make_async_copy(slot_ref, all_ref.at[lev], lsem.at[2])
    own_slots.start()

    def level_copy(k, i):
        to = lax.rem(lev + i, levs)
        return send(g_ref.at[to, k], col_ref.at[lev, k], s1.at[k, i], r1.at[k, i], lat, to)

    def level_ready(k):
        for i in range(1, levs):
            level_copy(k, i).start()

    horizontal(tr_ref, south_ref, north_ref, both_ref, g_ref, level_ready)
    own = pltpu.make_async_copy(g_ref.at[lev], col_ref.at[lev], lsem.at[0])
    own.start()
    own.wait()

    @pl.loop(0, block)
    def _(k):
        for i in range(1, levs):
            level_copy(k, i).wait()

    def tiles(r):
        return slice(2 * r, 2 * r + (3 if r == 3 else 2))

    def row_copy(r, i):
        to = lax.rem(lev + i, levs)
        return send(p_ref.at[tiles(r), to, :, 0:3], r_ref.at[tiles(r), :, lev, 0:3], s2.at[r, i], r2.at[r, i], lat, to)

    def row_ready(r):
        for i in range(1, levs):
            row_copy(r, i).start()

    select(rest, col_ref, c_ref, slot_ref, p_ref, a_ref, row_ready)
    own = pltpu.make_async_copy(p_ref.at[:, lev, :, 0:3], r_ref.at[:, :, lev, 0:3], lsem.at[1])
    own.start()
    own.wait()
    for r in range(4):
        for i in range(1, levs):
            row_copy(r, i).wait()
    own_slots.wait()
    for i in range(1, levs):
        slot_copy(i).wait()


def back_kernel(
    rest, levs, order, r_ref, n0, n1, n2, n3, f0, f1, f2, f3, slot_ref,
    o_ref, y_ref, v_ref, w_ref, z_ref, m_ref, move_ref, s1, r1, s2, r2, lsem, msem,
):
    lat, lev = lax.axis_index("lat"), lax.axis_index("lev")
    greet(lat, lev, levs)

    fetches = []
    for n, ref in enumerate((n0, f0, n1, f1, n2, f2, n3, f3)):
        fetches.append(pltpu.make_async_copy(ref, m_ref.at[n], msem.at[n]))
        fetches[n].start()

    def begin(n):
        d, turn, core, _ = PIECES[n]
        at = lax.rem(lat // 4 - d + 4, 4) * 4
        if turn is not None:
            at = at + lax.rem(lat // 2 + turn, 2) * 2
        return at if core is None else at + lax.rem(lat + core, 2)

    def part(n):
        return pl.ds(begin(n), PIECES[n][3])

    def piece_copy(n, i):
        to = lax.rem(lev + i, levs)
        return send(y_ref.at[:, part(n), to, 0:3], v_ref.at[:, lev, part(n), 0:3], s1.at[n, i], r1.at[n, i], lat, to)

    def tile_copy(j, i):
        to = lax.rem(lev + i, levs)
        at = part(len(PIECES) - 1)
        return send(y_ref.at[j, at, to, 0:3], v_ref.at[j, lev, at, 0:3], s2.at[j, i], r2.at[j, i], lat, to)

    def own_copy(n):
        return pltpu.make_async_copy(y_ref.at[:, part(n), lev, 0:3], v_ref.at[:, lev, part(n), 0:3], lsem.at[n])

    to_lane = lax.broadcasted_iota(jnp.int32, (256, 1024), 1)
    from_lane = lax.broadcasted_iota(jnp.int32, (256, 1024), 0) & 127
    wanted = ((to_lane >> 2) & 3) * 32 + (to_lane >> 7) * 4 + (to_lane & 3)
    move_ref[...] = (from_lane == wanted).astype(F32).astype(BF16)

    def place_last(n):
        size = PIECES[n][3]
        many = 4 * size
        hi, lo = split(z_ref[:, part(n)].reshape(8 * many, 128))
        moved = dot(jnp.concatenate([hi, lo], axis=1), move_ref[...])
        group = (lax.broadcasted_iota(jnp.int32, (many, 1024), 1) >> 4) & 7
        x = moved[:many]
        for g in range(1, 8):
            x = jnp.where(group == g, moved[many * g : many * (g + 1)], x)
        for l in range(8):
            y_ref[8, part(n), l] = x[:, 128 * l : 128 * l + 128].reshape(size, 4, 128)

    def mix(n, at):
        tiles = [r_ref[j, n].reshape(4 * levs, 128) for j in range(9)]
        rows = []
        for r in range(4):
            x = jnp.concatenate(tiles[2 * r : 2 * r + 3], axis=1)
            if r > 0:
                x = pltpu.roll(x, 384 - 32 * r, 1)
            rows.append(x[:, :order])
        hi, lo = split(jnp.concatenate(rows, axis=0))
        y = dot(hi, w_ref[0, at], NT) + dot(lo, w_ref[0, at], NT) + dot(hi, w_ref[1, at], NT)
        many = 4 * levs
        quarter = lax.broadcasted_iota(jnp.int32, (many, 128), 1) >> 5
        for half in range(2):
            turns = []
            for r in range(4):
                tile = y[r * many : (r + 1) * many, 128 * half : 128 * half + 128]
                turns.append([tile] + [pltpu.roll(tile, 32 * m, 1) for m in range(1, 4)])
            for m in range(4):
                x = turns[3][(3 - m) % 4]
                for r in range(3):
                    x = jnp.where(quarter == r, turns[r][(r - m) % 4], x)
                y_ref[pl.ds(0, 8), n, 4 * half + m] = x.reshape(8, 4, 128)
        z = jnp.concatenate([y[r * many : (r + 1) * many, 256:] for r in range(4)], axis=1)
        z_ref[:, n] = z.reshape(8, 4, 128)

    arrivals = [8] + list(range(8))
    fetched = set()
    for n, (d, turn, core, size) in enumerate(PIECES):
        for ref in (2 * d, 2 * d + 1) if core is None else (2 * d + core,):
            if ref not in fetched:
                fetched.add(ref)
                fetches[ref].wait()
        for at in range(size):
            hi, lo = split(unpacked(m_ref[2 * d + (at % 2 if core is None else core), at // 2 + (turn or 0)]))
            w_ref[0, at] = hi
            w_ref[1, at] = lo
        first = lax.rem(lat // 4 - d + 4, 4) * 4

        @pl.loop(0, size)
        def _(at):
            steps = at // 2 if turn is None else turn
            mix(first + lax.rem(lat // 2 + steps, 2) * 2 + lax.rem(lat + at + (core or 0), 2), at)

        place_last(n)
        own_copy(n).start()
        if n == 0:
            greeted(levs)
        if n < len(PIECES) - 1:
            for i in range(1, levs):
                piece_copy(n, i).start()
        else:
            for j in arrivals:
                for i in range(1, levs):
                    tile_copy(j, i).start()

    for n in range(len(PIECES)):
        own_copy(n).wait()
    for n in range(len(PIECES) - 1):
        for i in range(1, levs):
            piece_copy(n, i).wait()
    last = None
    for j in arrivals:
        for i in range(1, levs):
            tile_copy(j, i).wait()
        tile = turned_tile(v_ref, j)
        if j == 8:
            last = tile
        else:
            unselect(128 + rest, j, tile, last, slot_ref, o_ref)


def call(kernel, shape, count, scratch=(), limit=48, extra=None, large=(), **params):
    return pl.pallas_call(
        kernel,
        out_shape=jax.ShapeDtypeStruct(shape, F32) if extra is None else (jax.ShapeDtypeStruct(shape, F32), extra),
        in_specs=[pl.BlockSpec(memory_space=pl.ANY) if n in large else VMEM for n in range(count)],
        out_specs=VMEM if extra is None else (VMEM, VMEM),
        scratch_shapes=list(scratch),
        compiler_params=pltpu.CompilerParams(vmem_limit_bytes=limit << 20, **params),
    )


def body(tracers, zonal, meridional, vertical, route, inverse):
    trac, levs_here, rows, width = tracers.shape
    lats, groups = lax.axis_size("lat"), lax.axis_size("lev")
    levels, _, lon = vertical.shape
    rest = lon - 128
    order = inverse.shape[2]
    own = inverse[0, 0]
    across = lax.ppermute(own, "lat", [(i, i ^ 2) for i in range(lats)])
    turned = jnp.transpose(tracers, (2, 1, 0, 3))
    up = [(i, i + 1) for i in range(lats - 1)]
    down = [(i + 1, i) for i in range(lats - 1)]
    south = lax.ppermute(turned[rows - 3 :], "lat", up)
    edge = jnp.pad(meridional[:, 0], ((0, -levs_here % 4), (0, 0))).reshape(-1, 4, width)
    north = lax.ppermute(
        jnp.concatenate([turned[:3].reshape(3 * levs_here, trac, width), edge], axis=0), "lat", down
    )
    pair = call(functools.partial(reorder_kernel, groups), (2, order * order // 128, 128), 1, limit=12)(jnp.stack([own, across]))
    targets = route[:, :, 0]
    before = jnp.arange(lon)[:, None] < jnp.arange(lon)[None, :]
    same = jnp.logical_and(targets[:, :, None] == targets[:, None, :], before[None])
    place = (targets % groups) * lats + targets // groups
    slots = place * 4 + jnp.sum(same.astype(jnp.int32), axis=1)
    slots = jnp.pad(slots, ((0, 0), (0, 256 - lon)), constant_values=-1)
    v = vertical.reshape(levels, 2, 2, lon)
    courant = jnp.concatenate(
        [v[:, 0, :, :128], v[:, 1, :, :128], v[:, 0, :, 128:], v[:, 1, :, 128:], jnp.zeros((levels, 2, 128 - 2 * rest), F32)],
        axis=-1,
    )
    south, north, pair, courant = lax.optimization_barrier((south, north, pair, courant))
    shifted = [lax.ppermute(pair, "lat", [(i, (i + 4 * d) % lats) for i in range(lats)]) for d in range(1, 4)]
    other = [(i, i ^ 1) for i in range(lats)]
    dma = pltpu.SemaphoreType.DMA
    levels_of = pltpu.VMEM((groups, levs_here, 8, 384), F32)
    received, all_slots = call(
        functools.partial(forth_kernel, rest, groups),
        (9, lats, groups, 4, 128),
        6,
        [
            levels_of,
            levels_of,
            pltpu.VMEM((9, groups, lats, 4, 128), F32),
            pltpu.VMEM((4, 384, 512), BF16),
            dma((levs_here, groups)),
            dma((levs_here, groups)),
            dma((4, groups)),
            dma((4, groups)),
            dma((groups,)),
            dma((groups,)),
            dma((3,)),
        ],
        extra=jax.ShapeDtypeStruct((groups, 4, 256), jnp.int32),
        limit=24,
        collective_id=0,
        has_side_effects=True,
    )(turned, south, north, jnp.stack([zonal, meridional]), courant, slots)
    received, pair, shifted = lax.optimization_barrier((received, pair, shifted))
    far = [lax.ppermute(x, "lat", other) for x in [pair] + shifted]
    whole = call(
        functools.partial(back_kernel, rest, groups, order),
        (trac, levs_here, rows, width),
        10,
        [
            pltpu.VMEM((9, lats, groups, 4, 128), F32),
            pltpu.VMEM((9, groups, lats, 4, 128), F32),
            pltpu.VMEM((2, 4, order, order), BF16),
            pltpu.VMEM((groups, lats, 4, 128), F32),
            pltpu.VMEM((8,) + pair.shape, F32),
            pltpu.VMEM((256, 1024), BF16),
            dma((len(PIECES) - 1, groups)),
            dma((len(PIECES) - 1, groups)),
            dma((9, groups)),
            dma((9, groups)),
            dma((len(PIECES),)),
            dma((8,)),
        ],
        large=range(1, 9),
        limit=28,
        collective_id=1,
        has_side_effects=True,
    )(received, pair, *shifted, *far, all_slots)
    return whole - tracers


def solution(mesh):
    in_specs = (
        P(None, "lev", "lat", None),
        P("lev", "lat", None),
        P("lev", "lat", None),
        P(None, "lat", "lev"),
        P("lat", "lev", None),
        P("lat", "lev", None, None),
    )
    out_specs = P(None, "lev", "lat", None)
    return jax.shard_map(body, mesh=mesh, in_specs=in_specs, out_specs=out_specs, check_vma=False)
```

```python
import functools
import jax
import jax.numpy as jnp
from jax import lax
from jax.experimental import pallas as pl
from jax.experimental.pallas import tpu as pltpu
from jax.sharding import PartitionSpec as P

MESH = pl.DeviceIdType.MESH
F32 = jnp.float32
BF16 = jnp.bfloat16
VMEM = pl.BlockSpec(memory_space=pltpu.VMEM)
NT = (((1,), (1,)), ((), ()))
NN = (((1,), (0,)), ((), ()))


def dot(a, b, dims=NN):
    return lax.dot_general(a, b, dims, preferred_element_type=F32)


def split(x):
    hi = x.astype(BF16)
    lo = (x - hi.astype(F32)).astype(BF16)
    return hi, lo


def flux(c, e, s_low, s_here, k_low, k_here):
    up = c >= 0.0
    a = jnp.abs(c)
    s = jnp.where(up, -s_low, s_here)
    k = jnp.where(up, k_low, k_here)
    return c * (e + (0.5 * a) * (s + (1.0 - (2.0 / 3.0) * a) * k))


def face(q_m2, q_m1, q_0, q_p1):
    return (7.0 / 12.0) * (q_m1 + q_0) - (1.0 / 12.0) * (q_m2 + q_p1)


def horizontal(tr_ref, south_ref, north_ref, both_ref, g_ref, ready):
    lat = lax.axis_index("lat")
    last = lax.axis_size("lat") - 1
    width = tr_ref.shape[3]
    groups = g_ref.shape[0]
    lon = width // groups
    sub = lax.broadcasted_iota(jnp.int32, (8, width), 0) < 4
    ext = -(-width // 128) * 128
    spare = ext - width
    half = spare // 3
    ksouth = (lat > 0).astype(F32)
    knorth = (lat < last).astype(F32)

    def swap(x):
        return pltpu.roll(x, 4, 0)

    def extend(x):
        return jnp.concatenate([x, x[:, :half], x[:, width - (spare - half):]], axis=1)

    def rolled(x, n):
        return pltpu.roll(x, n % ext, 1)

    def level(k, carry):
        row = [tr_ref[r, k] for r in range(4)]
        low = [south_ref[r, k] * ksouth for r in range(3)]
        high = [north_ref[r * tr_ref.shape[1] + k] * knorth for r in range(3)]
        pair = lambda a, b: jnp.concatenate([a, b], axis=0)
        q = [
            pair(low[0], low[0]),
            pair(low[1], low[2]),
            pair(row[0], row[1]),
            pair(row[2], row[3]),
            pair(high[0], high[1]),
            pair(high[2], high[2]),
        ]
        sq = [swap(x) for x in q]
        e = [face(q[p - 1], jnp.where(sub, sq[p - 1], sq[p]), q[p], jnp.where(sub, sq[p], sq[p + 1])) for p in range(1, 5)]
        se = [swap(x) for x in e]
        s, kk = [], []
        for p in range(4):
            right = jnp.where(sub, se[p], se[min(p + 1, 3)])
            s.append(right - e[p])
            kk.append(6.0 * q[p + 1] - 3.0 * (e[p] + right))
        ss = [swap(x) for x in s]
        sk = [swap(x) for x in kk]
        m = both_ref[1, k]
        zero = jnp.zeros((8, width), F32)
        m0 = jnp.where(sub, m[0:1] * ksouth, m[1:2])
        m1 = jnp.where(sub, m[2:3], m[3:4])
        m2 = north_ref[3 * tr_ref.shape[1] + k // 4, pl.ds(k % 4, 1), :] * knorth + zero
        f = []
        for i, c in enumerate((m0, m1, m2)):
            p = i + 1
            f.append(
                flux(c, e[p], jnp.where(sub, ss[p - 1], ss[p]), s[p], jnp.where(sub, sk[p - 1], sk[p]), kk[p])
            )
        sf = [swap(x) for x in f]
        z = both_ref[0, k]
        out = []
        for p in range(2):
            lat_change = f[p] - jnp.where(sub, sf[p], sf[p + 1])
            x = extend(q[p + 2])
            c = extend(jnp.where(sub, z[2 * p : 2 * p + 1], z[2 * p + 1 : 2 * p + 2]))
            le = face(rolled(x, 2), rolled(x, 1), x, rolled(x, -1))
            right = rolled(le, -1)
            ls = right - le
            lk = 6.0 * x - 3.0 * (le + right)
            lf = flux(c, le, rolled(ls, 1), ls, rolled(lk, 1), lk)
            lon_change = lf - rolled(lf, -1)
            out.append(q[p + 2] + lon_change[:, :width] + lat_change)
        rest = lon - 128
        pad = jnp.zeros((8, 128 - 2 * rest), F32)
        for g in range(groups):
            o = g * lon
            g_ref[g, k] = jnp.concatenate(
                [
                    out[0][:, o : o + 128],
                    out[1][:, o : o + 128],
                    out[0][:, o + 128 : o + lon],
                    out[1][:, o + 128 : o + lon],
                    pad,
                ],
                axis=1,
            )
        ready(k)
        return carry

    lax.fori_loop(0, tr_ref.shape[1], level, 0)


def selector(slots):
    ids = lax.broadcasted_iota(jnp.int32, (512, 256), 0)
    return (ids == slots).astype(F32).astype(BF16)


def select(rest, g_ref, c_ref, slot_ref, p_ref, a_ref, ready):
    block = g_ref.shape[1]
    levels = g_ref.shape[0] * block
    sub = lax.broadcasted_iota(jnp.int32, (8, 384), 0) < 4
    half = lax.broadcasted_iota(jnp.int32, (8, 256), 0) < 4
    zero = jnp.zeros((8, 384), F32)
    for r in range(4):
        if r > 0:
            a_ref[r, 0 : 32 * r, :] = jnp.zeros((32 * r, 512), BF16)
        if r < 3:
            a_ref[r, 32 * r + 288 : 384, :] = jnp.zeros((96 - 32 * r, 512), BF16)

    def q(k):
        return g_ref[k // block, k % block] if 0 <= k < levels else zero

    def e_at(k):
        return face(q(k - 2), q(k - 1), q(k), q(k + 1))

    left = e_at(0)
    f_here = zero
    held = []
    right = e_at(1)
    s, kk = right - left, 6.0 * q(0) - 3.0 * (left + right)
    for k in range(levels):
        if k + 1 < levels:
            nxt = e_at(k + 2)
            s1, k1 = nxt - right, 6.0 * q(k + 1) - 3.0 * (right + nxt)
            c = jnp.where(sub, c_ref[k + 1, 0:1, :], c_ref[k + 1, 1:2, :])
            f_next = flux(c, right, s, s1, kk, k1)
            right, s, kk = nxt, s1, k1
        else:
            f_next = zero
        held.append(q(k) + f_here - f_next)
        f_here = f_next
        if k % 4 == 3:
            for rp in range(2):
                x = []
                for h in held:
                    third = h[:, 256:384]
                    if rp == 1:
                        third = pltpu.roll(third, 128 - rest, 1)
                    x.append(jnp.concatenate([h[:, 128 * rp : 128 * rp + 128], third], axis=1))
                t = [pltpu.roll(v, 4, 0) for v in x]
                first = [jnp.where(half, x[0], t[1]), jnp.where(half, x[2], t[3])]
                second = [jnp.where(half, t[0], x[1]), jnp.where(half, t[2], x[3])]
                for r2, rows in enumerate((first, second)):
                    r = 2 * rp + r2
                    hi, lo = split(jnp.concatenate(rows, axis=0))
                    at = 32 * r + 4 * (k - 3)
                    a_ref[r, at : at + 16, 0:256] = hi
                    a_ref[r, at : at + 16, 256:512] = lo
            held = []
    carried = None
    for r in range(4):
        one = selector(slot_ref[r : r + 1, :])
        out = dot(jnp.concatenate([one, one], axis=1), a_ref[r], NT)
        for t in range(3):
            part = out[:, 128 * t : 128 * t + 128]
            if t == 0 and r > 0:
                part = part + carried
            if t == 2 and r < 3:
                carried = part
                continue
            p_ref[2 * r + t] = part.reshape(p_ref.shape[1:])
        ready(r)


def reorder_kernel(levs, m_ref, o_ref):
    order = m_ref.shape[1]
    levels = order // 4
    block = levels // levs
    x = lax.broadcasted_iota(jnp.int32, (order, order), 0)
    o = lax.broadcasted_iota(jnp.int32, (order, order), 1)
    pick = ((x & 3) * levels + (x >> 2) == o).astype(F32).astype(BF16)
    main = (x & 3) * levels + block * (x >> 5) + ((x >> 2) & 7)
    last = (x & 3) * levels + block * ((x - 256) >> 2) + block - 1
    put = (jnp.where(x < 256, main, last) == o).astype(F32).astype(BF16)
    part = order // 4
    for n in range(2):
        hi, lo = split(m_ref[n])
        rest = (m_ref[n] - hi.astype(F32) - lo.astype(F32)).astype(BF16)
        out = None
        for piece in (hi, lo, rest):
            term = dot(dot(put, piece).astype(BF16), pick, NT)
            out = term if out is None else out + term
        o_ref[n, 0:order] = out[:, 0:128]
        o_ref[n, order : 2 * order] = out[:, 128:256]
        o_ref[n, 2 * order :] = jnp.concatenate([out[part * i : part * i + part, 256:] for i in range(4)], axis=1)


def unpacked(packed):
    part = packed.shape[0] // 9
    third = packed[8 * part :]
    lanes = third.shape[1] // 4
    third = jnp.concatenate([third[:, lanes * i : lanes * i + lanes] for i in range(4)], axis=0)
    return jnp.concatenate([packed[: 4 * part], packed[4 * part : 8 * part], third], axis=1)


def turned_tile(v_ref, j):
    live = (lax.broadcasted_iota(jnp.int32, (128, 512), 1) & 3) < 3
    return jnp.where(live, v_ref[j].reshape(512, 128).T, 0.0)


def unselect(lon, g, tile, last, slot_ref, o_ref):
    for r in range(4):
        rows = jnp.concatenate([tile[32 * r : 32 * r + 32], last[16 * g : 16 * g + 16]], axis=0)
        hi, lo = split(rows)
        one = selector(slot_ref[g, r : r + 1, :])
        out = dot(jnp.concatenate([hi, lo], axis=1), jnp.concatenate([one, one], axis=0))
        at = slice(lon * g, lon * g + lon)
        for t in range(4):
            for k in range(8):
                o_ref[t, k, r : r + 1, at] = out[4 * k + t : 4 * k + t + 1, :lon]
            o_ref[t, 8, r : r + 1, at] = out[32 + 4 * r + t : 33 + 4 * r + t, :lon]


PIECES = ((0, 0, 0, 1), (0, 0, 1, 1), (0, 1, None, 2), (1, None, None, 4), (2, None, None, 4), (3, None, None, 4))


def greet(lat, lev, levs):
    for i in range(1, levs):
        pl.semaphore_signal(
            pltpu.get_barrier_semaphore(), inc=1, device_id=(lat, lax.rem(lev + i, levs)), device_id_type=MESH
        )


def greeted(levs):
    pl.semaphore_wait(pltpu.get_barrier_semaphore(), levs - 1)


def send(src, dst, ssem, rsem, lat, to):
    return pltpu.make_async_remote_copy(
        src_ref=src, dst_ref=dst, send_sem=ssem, recv_sem=rsem, device_id=(lat, to), device_id_type=MESH
    )


def forth_kernel(
    rest, levs, tr_ref, south_ref, north_ref, both_ref, c_ref, slot_ref,
    r_ref, all_ref, g_ref, col_ref, p_ref, a_ref, s1, r1, s2, r2, s3, r3, lsem,
):
    lat, lev = lax.axis_index("lat"), lax.axis_index("lev")
    block = tr_ref.shape[1]
    greet(lat, lev, levs)

    def slot_copy(i):
        to = lax.rem(lev + i, levs)
        return send(slot_ref, all_ref.at[lev], s3.at[i], r3.at[i], lat, to)

    own_slots = pltpu.make_async_copy(slot_ref, all_ref.at[lev], lsem.at[2])
    own_slots.start()

    def level_copy(k, i):
        to = lax.rem(lev + i, levs)
        return send(g_ref.at[to, k], col_ref.at[lev, k], s1.at[k, i], r1.at[k, i], lat, to)

    def level_ready(k):
        pl.when(k == 0)(lambda: greeted(levs))
        for i in range(1, levs):
            level_copy(k, i).start()

    horizontal(tr_ref, south_ref, north_ref, both_ref, g_ref, level_ready)
    for i in range(1, levs):
        slot_copy(i).start()
    own = pltpu.make_async_copy(g_ref.at[lev], col_ref.at[lev], lsem.at[0])
    own.start()
    own.wait()

    @pl.loop(0, block)
    def _(k):
        for i in range(1, levs):
            level_copy(k, i).wait()

    def tiles(r):
        return slice(2 * r, 2 * r + (3 if r == 3 else 2))

    def row_copy(r, i):
        to = lax.rem(lev + i, levs)
        return send(p_ref.at[tiles(r), to, :, 0:3], r_ref.at[tiles(r), :, lev, 0:3], s2.at[r, i], r2.at[r, i], lat, to)

    def row_ready(r):
        for i in range(1, levs):
            row_copy(r, i).start()

    select(rest, col_ref, c_ref, slot_ref, p_ref, a_ref, row_ready)
    own = pltpu.make_async_copy(p_ref.at[:, lev, :, 0:3], r_ref.at[:, :, lev, 0:3], lsem.at[1])
    own.start()
    own.wait()
    for r in range(4):
        for i in range(1, levs):
            row_copy(r, i).wait()
    own_slots.wait()
    for i in range(1, levs):
        slot_copy(i).wait()


def back_kernel(
    rest, levs, order, r_ref, n0, n1, n2, n3, f0, f1, f2, f3, slot_ref,
    o_ref, y_ref, v_ref, w_ref, z_ref, m_ref, move_ref, s1, r1, s2, r2, lsem, msem,
):
    lat, lev = lax.axis_index("lat"), lax.axis_index("lev")
    greet(lat, lev, levs)

    fetches = []
    for n, ref in enumerate((n0, f0, n1, f1, n2, f2, n3, f3)):
        fetches.append(pltpu.make_async_copy(ref, m_ref.at[n], msem.at[n]))
        fetches[n].start()

    def begin(n):
        d, turn, core, _ = PIECES[n]
        at = lax.rem(lat // 4 - d + 4, 4) * 4
        if turn is not None:
            at = at + lax.rem(lat // 2 + turn, 2) * 2
        return at if core is None else at + lax.rem(lat + core, 2)

    def part(n):
        return pl.ds(begin(n), PIECES[n][3])

    def piece_copy(n, i):
        to = lax.rem(lev + i, levs)
        return send(y_ref.at[:, part(n), to, 0:3], v_ref.at[:, lev, part(n), 0:3], s1.at[n, i], r1.at[n, i], lat, to)

    def tile_copy(j, i):
        to = lax.rem(lev + i, levs)
        at = part(len(PIECES) - 1)
        return send(y_ref.at[j, at, to, 0:3], v_ref.at[j, lev, at, 0:3], s2.at[j, i], r2.at[j, i], lat, to)

    def own_copy(n):
        return pltpu.make_async_copy(y_ref.at[:, part(n), lev, 0:3], v_ref.at[:, lev, part(n), 0:3], lsem.at[n])

    to_lane = lax.broadcasted_iota(jnp.int32, (256, 1024), 1)
    from_lane = lax.broadcasted_iota(jnp.int32, (256, 1024), 0) & 127
    wanted = ((to_lane >> 2) & 3) * 32 + (to_lane >> 7) * 4 + (to_lane & 3)
    move_ref[...] = (from_lane == wanted).astype(F32).astype(BF16)

    def place_last(n):
        size = PIECES[n][3]
        many = 4 * size
        hi, lo = split(z_ref[:, part(n)].reshape(8 * many, 128))
        moved = dot(jnp.concatenate([hi, lo], axis=1), move_ref[...])
        group = (lax.broadcasted_iota(jnp.int32, (many, 1024), 1) >> 4) & 7
        x = moved[:many]
        for g in range(1, 8):
            x = jnp.where(group == g, moved[many * g : many * (g + 1)], x)
        for l in range(8):
            y_ref[8, part(n), l] = x[:, 128 * l : 128 * l + 128].reshape(size, 4, 128)

    def mix(n, at):
        tiles = [r_ref[j, n].reshape(4 * levs, 128) for j in range(9)]
        rows = []
        for r in range(4):
            x = jnp.concatenate(tiles[2 * r : 2 * r + 3], axis=1)
            if r > 0:
                x = pltpu.roll(x, 384 - 32 * r, 1)
            rows.append(x[:, :order])
        hi, lo = split(jnp.concatenate(rows, axis=0))
        y = dot(hi, w_ref[0, at], NT) + dot(lo, w_ref[0, at], NT) + dot(hi, w_ref[1, at], NT)
        many = 4 * levs
        quarter = lax.broadcasted_iota(jnp.int32, (many, 128), 1) >> 5
        for half in range(2):
            turns = []
            for r in range(4):
                tile = y[r * many : (r + 1) * many, 128 * half : 128 * half + 128]
                turns.append([tile] + [pltpu.roll(tile, 32 * m, 1) for m in range(1, 4)])
            for m in range(4):
                x = turns[3][(3 - m) % 4]
                for r in range(3):
                    x = jnp.where(quarter == r, turns[r][(r - m) % 4], x)
                y_ref[pl.ds(0, 8), n, 4 * half + m] = x.reshape(8, 4, 128)
        z = jnp.concatenate([y[r * many : (r + 1) * many, 256:] for r in range(4)], axis=1)
        z_ref[:, n] = z.reshape(8, 4, 128)

    arrivals = [8] + list(range(8))
    fetched = set()
    for n, (d, turn, core, size) in enumerate(PIECES):
        for ref in (2 * d, 2 * d + 1) if core is None else (2 * d + core,):
            if ref not in fetched:
                fetched.add(ref)
                fetches[ref].wait()
        for at in range(size):
            hi, lo = split(unpacked(m_ref[2 * d + (at % 2 if core is None else core), at // 2 + (turn or 0)]))
            w_ref[0, at] = hi
            w_ref[1, at] = lo
        first = lax.rem(lat // 4 - d + 4, 4) * 4

        @pl.loop(0, size)
        def _(at):
            steps = at // 2 if turn is None else turn
            mix(first + lax.rem(lat // 2 + steps, 2) * 2 + lax.rem(lat + at + (core or 0), 2), at)

        place_last(n)
        own_copy(n).start()
        if n == 0:
            greeted(levs)
        if n < len(PIECES) - 1:
            for i in range(1, levs):
                piece_copy(n, i).start()
        else:
            for j in arrivals:
                for i in range(1, levs):
                    tile_copy(j, i).start()

    for n in range(len(PIECES)):
        own_copy(n).wait()
    for n in range(len(PIECES) - 1):
        for i in range(1, levs):
            piece_copy(n, i).wait()
    last = None
    for j in arrivals:
        for i in range(1, levs):
            tile_copy(j, i).wait()
        tile = turned_tile(v_ref, j)
        if j == 8:
            last = tile
        else:
            unselect(128 + rest, j, tile, last, slot_ref, o_ref)


def call(kernel, shape, count, scratch=(), limit=48, extra=None, large=(), **params):
    return pl.pallas_call(
        kernel,
        out_shape=jax.ShapeDtypeStruct(shape, F32) if extra is None else (jax.ShapeDtypeStruct(shape, F32), extra),
        in_specs=[pl.BlockSpec(memory_space=pl.ANY) if n in large else VMEM for n in range(count)],
        out_specs=VMEM if extra is None else (VMEM, VMEM),
        scratch_shapes=list(scratch),
        compiler_params=pltpu.CompilerParams(vmem_limit_bytes=limit << 20, **params),
    )


def body(tracers, zonal, meridional, vertical, route, inverse):
    trac, levs_here, rows, width = tracers.shape
    lats, groups = lax.axis_size("lat"), lax.axis_size("lev")
    levels, _, lon = vertical.shape
    rest = lon - 128
    order = inverse.shape[2]
    own = inverse[0, 0]
    across = lax.ppermute(own, "lat", [(i, i ^ 2) for i in range(lats)])
    turned = jnp.transpose(tracers, (2, 1, 0, 3))
    up = [(i, i + 1) for i in range(lats - 1)]
    down = [(i + 1, i) for i in range(lats - 1)]
    south = lax.ppermute(turned[rows - 3 :], "lat", up)
    edge = jnp.pad(meridional[:, 0], ((0, -levs_here % 4), (0, 0))).reshape(-1, 4, width)
    north = lax.ppermute(
        jnp.concatenate([turned[:3].reshape(3 * levs_here, trac, width), edge], axis=0), "lat", down
    )
    pair = call(functools.partial(reorder_kernel, groups), (2, order * order // 128, 128), 1, limit=12)(jnp.stack([own, across]))
    targets = route[:, :, 0]
    before = jnp.arange(lon)[:, None] < jnp.arange(lon)[None, :]
    same = jnp.logical_and(targets[:, :, None] == targets[:, None, :], before[None])
    place = (targets % groups) * lats + targets // groups
    slots = place * 4 + jnp.sum(same.astype(jnp.int32), axis=1)
    slots = jnp.pad(slots, ((0, 0), (0, 256 - lon)), constant_values=-1)
    v = vertical.reshape(levels, 2, 2, lon)
    courant = jnp.concatenate(
        [v[:, 0, :, :128], v[:, 1, :, :128], v[:, 0, :, 128:], v[:, 1, :, 128:], jnp.zeros((levels, 2, 128 - 2 * rest), F32)],
        axis=-1,
    )
    south, north, pair, courant = lax.optimization_barrier((south, north, pair, courant))
    shifted = [lax.ppermute(pair, "lat", [(i, (i + 4 * d) % lats) for i in range(lats)]) for d in range(1, 4)]
    other = [(i, i ^ 1) for i in range(lats)]
    dma = pltpu.SemaphoreType.DMA
    levels_of = pltpu.VMEM((groups, levs_here, 8, 384), F32)
    received, all_slots = call(
        functools.partial(forth_kernel, rest, groups),
        (9, lats, groups, 4, 128),
        6,
        [
            levels_of,
            levels_of,
            pltpu.VMEM((9, groups, lats, 4, 128), F32),
            pltpu.VMEM((4, 384, 512), BF16),
            dma((levs_here, groups)),
            dma((levs_here, groups)),
            dma((4, groups)),
            dma((4, groups)),
            dma((groups,)),
            dma((groups,)),
            dma((3,)),
        ],
        extra=jax.ShapeDtypeStruct((groups, 4, 256), jnp.int32),
        limit=24,
        collective_id=0,
        has_side_effects=True,
    )(turned, south, north, jnp.stack([zonal, meridional]), courant, slots)
    received, pair, shifted = lax.optimization_barrier((received, pair, shifted))
    far = [lax.ppermute(x, "lat", other) for x in [pair] + shifted]
    whole = call(
        functools.partial(back_kernel, rest, groups, order),
        (trac, levs_here, rows, width),
        10,
        [
            pltpu.VMEM((9, lats, groups, 4, 128), F32),
            pltpu.VMEM((9, groups, lats, 4, 128), F32),
            pltpu.VMEM((2, 4, order, order), BF16),
            pltpu.VMEM((groups, lats, 4, 128), F32),
            pltpu.VMEM((8,) + pair.shape, F32),
            pltpu.VMEM((256, 1024), BF16),
            dma((len(PIECES) - 1, groups)),
            dma((len(PIECES) - 1, groups)),
            dma((9, groups)),
            dma((9, groups)),
            dma((len(PIECES),)),
            dma((8,)),
        ],
        large=range(1, 9),
        limit=28,
        collective_id=1,
        has_side_effects=True,
    )(received, pair, *shifted, *far, all_slots)
    return whole - tracers


def solution(mesh):
    in_specs = (
        P(None, "lev", "lat", None),
        P("lev", "lat", None),
        P("lev", "lat", None),
        P(None, "lat", "lev"),
        P("lat", "lev", None),
        P("lat", "lev", None, None),
    )
    out_specs = P(None, "lev", "lat", None)
    return jax.shard_map(body, mesh=mesh, in_specs=in_specs, out_specs=out_specs, check_vma=False)
```
